128 devices in a mesh: ctx: 8 (over z_lo, x), exp: 16 (over y, z_hi, core).
Axes of the slice: x: 4, y: 4, z: 4 (z_hi: 2, z_lo: 2; z = z_hi * 2 + z_lo), core: 2. Of those that a mesh axis runs over, the one named last changes fastest.
Arguments:
- tokens: bfloat16 [16384, 4096], P(('ctx', 'exp')), may hold values from -6 to 6
- block_order: int32 [128], replicated, may hold values from 0 to 127, each once
- attn_gain: bfloat16 [4096], replicated, may hold values from 0.25 to 1.75
- query_gain: bfloat16 [128], replicated, may hold values from 0.25 to 1.75
- key_gain: bfloat16 [128], replicated, may hold values from 0.25 to 1.75
- w_qkv: bfloat16 [4096, 768], P(None, 'exp'), may hold values from -0.09375 to 0.09375
- w_out: bfloat16 [512, 4096], P('exp'), may hold values from -0.25 to 0.25
- moe_gain: bfloat16 [4096], replicated, may hold values from 0.25 to 1.75
- router: bfloat16 [4096, 128], replicated, may hold values from -0.09375 to 0.09375
- routes: int32 [16384, 8], P(('ctx', 'exp')), may hold values from 0 to 127, all different within a row; in each aligned block of 128 rows (0 to 127, 128 to 255, ...) at most 9 rows name the same one
- w_gate_up: bfloat16 [128, 4096, 1536], P(('ctx', 'exp')), may hold values from -0.09375 to 0.09375
- w_down: bfloat16 [128, 768, 4096], P(('ctx', 'exp')), may hold values from -0.21875 to 0.21875
Outputs:
- layer_out: bfloat16 [16384, 4096], P(('ctx', 'exp'))
The draws below stay inside these ranges and needn't reach their ends.
Inputs may be any that keep to these rules, and one draw needn't show every extreme that they name: Every block number appears once; index k of ctx+exp (ctx slowest) holds positions block_order[k] * 128 to block_order[k] * 128 + 127. `routes`: each token names 8 different experts. Among the rows of one device no expert is named more than 9 times, and in every draw some device names some expert exactly 9 times.
All inputs are finite; a program needn't handle non-finite values.
Results may differ from the reference program's by a relative error of at most 0.01.
Values may be sent and summed in bfloat16 or wider, within the bound.
No kernel may reach another device: no remote copies, remote signals or barrier semaphores. Data moves between devices by JAX's collectives and lax.ppermute only.
A program may use at most 128 MiB of HBM per device.

```python
import math
import jax
import jax.numpy as jnp
import numpy as np
from jax import lax

D = 4096
HQ = 4
HD = 128
EH = 768
TOP = 8
TOK_DEV = 128
BLOCKS = 128
EXPERTS = 128
SEQ_LEN = 16384
CAP = 9


def block_levels(rng, dims, split, smallest, high):
    def one(dim, blocks):
        steps = jax.random.uniform(jax.random.fold_in(jax.random.fold_in(rng, 6), dim), (blocks,), jnp.float32, smallest / len(split), high / len(split))
        return jnp.repeat(jnp.exp(steps), dims[dim] // blocks).reshape((-1,) + (1,) * (len(dims) - dim - 1))

    factor_of = one(*split[0])
    for cut in split[1:]:
        factor_of = factor_of * one(*cut)
    return factor_of


def routed_block(key, own, number, rows, number_of, top, most, lean):
    sequence = jax.random.permutation(key, number_of)
    packed, common = load_shares(number_of, rows * top, most, lean, True), load_shares(number_of, rows * top, most, lean, False)
    places = jnp.arange(number_of)

    def named(lengths, turn):
        used = int((lengths > 0).sum())
        fixed = max(1, used // 4)
        moved = fixed + (places - fixed + turn * (used - fixed)) % max(1, number_of - fixed)
        return jnp.zeros((number_of,), jnp.int32).at[sequence[jnp.where(places < fixed, places, moved)]].set(jnp.asarray(lengths, jnp.int32))

    lengths = jnp.where(number % 4 == 0, named(packed, number // 4), named(common, number - number // 4 - 1))
    mixed = jax.random.permutation(jax.random.fold_in(own, 3), number_of)
    source_of, receiver = mixed[0:number_of // 2 * 2:2], mixed[1:number_of // 2 * 2:2]
    room = jnp.minimum(lengths[source_of] - 1, most - lengths[receiver]) // 2
    room = jnp.where((source_of == sequence[0]) | (receiver == sequence[0]) | (lengths[receiver] == 0), 0, jnp.maximum(room, 0))
    moved = jax.random.randint(jax.random.fold_in(own, 4), (number_of // 2,), 0, 1 << 20) % (room + 1)
    lengths = lengths.at[source_of].add(-moved).at[receiver].add(moved)
    labels = jnp.searchsorted(jnp.cumsum(lengths), jnp.arange(rows * top), side="right").astype(jnp.int32)
    grid = labels.reshape(top, rows).T
    grid = grid[jax.random.permutation(jax.random.fold_in(own, 1), rows)]
    turn = jax.random.randint(jax.random.fold_in(own, 2), (rows, 1), 0, top)
    return jnp.take_along_axis(grid, (jnp.arange(top)[None, :] + turn) % top, axis=1)


def load_shares(count, total, most, lean, full):
    weights = [(1 << 20) // math.isqrt(standing ** lean) + 1 for standing in range(1, count + 1)]
    largest = most if full else min(most, max(-(-total // count), total * weights[0] // sum(weights)))
    least = 1 if total - largest >= count - 1 else 0
    given, rest = [largest] + [least] * (count - 1), total - largest - least * (count - 1)
    while rest > 0:
        free = [i for i in range(1, count) if given[i] < largest] or [i for i in range(1, count) if given[i] < most]
        pool, left = sum([weights[i] for i in free]), rest
        for i in free:
            extra = min(most - given[i], max(1, left * weights[i] // pool), rest)
            given[i] = given[i] + extra
            rest = rest - extra
    return np.array(given)


def normal_values(rng, dims, scale, bound, cuts=(), kind=jnp.bfloat16):
    factor_of = block_levels(rng, dims, cuts, -0.22, 0.18) if cuts else 1.0
    drawn = jax.random.normal(rng, dims, jnp.float32) * scale * factor_of
    return jnp.minimum(jnp.maximum(drawn, -bound), bound).astype(kind)


def setup_inputs(seed: int = 0) -> dict:
    arg_keys = jax.random.split(jax.random.key(seed), 13)
    tokens = normal_values(arg_keys[0], (SEQ_LEN, D), 1.0, 6.0, ((0, 128),))
    block_order = jax.random.permutation(arg_keys[1], BLOCKS).astype(jnp.int32)
    attn_gain = jnp.clip(1.0 + 0.15 * jax.random.normal(arg_keys[2], (D,), jnp.float32), 0.25, 1.75).astype(jnp.bfloat16)
    query_gain = jnp.clip(1.0 + 0.15 * jax.random.normal(arg_keys[3], (HD,), jnp.float32), 0.25, 1.75).astype(jnp.bfloat16)
    key_gain = jnp.clip(1.0 + 0.15 * jax.random.normal(arg_keys[4], (HD,), jnp.float32), 0.25, 1.75).astype(jnp.bfloat16)
    w_qkv = normal_values(arg_keys[5], (D, (HQ + 2) * HD), D ** -0.5, 0.09375, ((1, 16),))
    w_out = normal_values(arg_keys[6], (HQ * HD, D), (HQ * HD) ** -0.5, 0.25, ((0, 16),))
    moe_gain = jnp.clip(1.0 + 0.15 * jax.random.normal(arg_keys[7], (D,), jnp.float32), 0.25, 1.75).astype(jnp.bfloat16)
    router = normal_values(arg_keys[8], (D, EXPERTS), D ** -0.5, 0.09375)
    routes_keys = jax.random.split(jax.random.fold_in(arg_keys[9], 1), SEQ_LEN // TOK_DEV)
    routes_turns = jax.random.permutation(jax.random.fold_in(arg_keys[9], 3), SEQ_LEN // TOK_DEV)
    routes = jax.vmap(lambda own, number: routed_block(jax.random.fold_in(arg_keys[9], 2), own, number, TOK_DEV, EXPERTS, TOP, CAP, 2))(routes_keys, routes_turns).reshape((SEQ_LEN, TOP))
    w_gate_up = normal_values(arg_keys[10], (EXPERTS, D, 2 * EH), D ** -0.5, 0.09375, ((0, 128),))
    w_down = normal_values(arg_keys[11], (EXPERTS, EH, D), EH ** -0.5, 0.21875, ((0, 128),))
    return dict(tokens=tokens, block_order=block_order, attn_gain=attn_gain, query_gain=query_gain, key_gain=key_gain, w_qkv=w_qkv, w_out=w_out, moe_gain=moe_gain, router=router, routes=routes, w_gate_up=w_gate_up, w_down=w_down)


rope_base = 1000000.0

def rms_scale(values, gain):
    widened = values.astype(jnp.float32)
    return widened * lax.rsqrt(lax.optimization_barrier(jnp.mean(widened * widened, axis=-1, keepdims=True)) + 1e-06) * gain.astype(jnp.float32)

def rotate(values, positions):
    half = values.shape[-1] // 2
    freqs = jnp.exp(-math.log(rope_base) * jnp.arange(half, dtype=jnp.float32) * 2.0 / values.shape[-1])
    angles = positions[..., None] * freqs
    first = values[..., :half]
    second = values[..., half:]
    return jnp.concatenate([first * jnp.cos(angles) - second * jnp.sin(angles), second * jnp.cos(angles) + first * jnp.sin(angles)], axis=-1)

def reference(tokens, block_order, attn_gain, query_gain, key_gain, w_qkv, w_out, moe_gain, router, routes, w_gate_up, w_down):
    seq_rows = jnp.arange(SEQ_LEN, dtype=jnp.int32)
    score_scale = 1.0 / math.sqrt(HD)
    positions = block_order[seq_rows // TOK_DEV] * TOK_DEV + seq_rows % TOK_DEV
    normed = rms_scale(tokens, attn_gain).astype(jnp.bfloat16)
    mixed = jnp.dot(normed, w_qkv, preferred_element_type=jnp.float32)
    queries = rotate(rms_scale(mixed[:, :HQ * HD].reshape(SEQ_LEN, HQ, HD), query_gain), positions[:, None].astype(jnp.float32)).astype(jnp.bfloat16)
    keys = rotate(rms_scale(mixed[:, HQ * HD:(HQ + 1) * HD], key_gain), positions.astype(jnp.float32)).astype(jnp.bfloat16)
    values = mixed[:, (HQ + 1) * HD:].astype(jnp.bfloat16)

    def query_block(index):
        block_queries = lax.dynamic_slice_in_dim(queries, index * TOK_DEV, TOK_DEV, 0)
        block_pos = lax.dynamic_slice_in_dim(positions, index * TOK_DEV, TOK_DEV, 0)
        scores = jnp.einsum('qhd,kd->hqk', block_queries.astype(jnp.float32), keys.astype(jnp.float32)) * score_scale
        visible = positions[None, None, :] <= block_pos[None, :, None]
        largest = lax.optimization_barrier(jnp.max(jnp.where(visible, scores, -1e+30), axis=2))
        mass = jnp.where(visible, jnp.exp(scores - largest[:, :, None]), 0.0)
        total = lax.optimization_barrier(jnp.sum(mass, axis=2))
        summed = jnp.einsum('hqk,kd->qhd', mass.astype(jnp.bfloat16).astype(jnp.float32), values.astype(jnp.float32))
        return (summed / jnp.transpose(total)[:, :, None]).astype(jnp.bfloat16)
    attended = lax.map(query_block, jnp.arange(BLOCKS, dtype=jnp.int32)).reshape(SEQ_LEN, HQ * HD)
    resid = tokens.astype(jnp.float32) + jnp.dot(attended, w_out, preferred_element_type=jnp.float32)
    moe_in = rms_scale(resid, moe_gain).astype(jnp.bfloat16)
    logits = jnp.dot(moe_in, router, preferred_element_type=jnp.float32)
    chosen = jnp.take_along_axis(logits, routes, axis=1)
    route_weights = jax.nn.softmax(chosen, axis=1)
    count_all = SEQ_LEN * TOP
    flat_ids = routes.reshape(-1)
    flat_weights = route_weights.reshape(-1)
    limit = BLOCKS * CAP

    def add_expert(expert_id, running):
        found = jnp.nonzero(flat_ids == expert_id, size=limit, fill_value=count_all)[0].astype(jnp.int32)
        valid = found < count_all
        safe = jnp.where(valid, found, 0)
        token_index = safe // TOP
        chosen_rows = moe_in[token_index]
        gate_up = jnp.dot(chosen_rows, w_gate_up[expert_id], preferred_element_type=jnp.float32)
        activated = (jax.nn.silu(gate_up[:, :EH]) * gate_up[:, EH:]).astype(jnp.bfloat16)
        produced = lax.optimization_barrier(jnp.dot(activated, w_down[expert_id], preferred_element_type=jnp.float32).astype(jnp.bfloat16)).astype(jnp.float32)
        scaled = produced * jnp.where(valid, flat_weights[safe], 0.0)[:, None]
        return running.at[token_index].add(scaled)
    moe_out = lax.fori_loop(0, EXPERTS, add_expert, jnp.zeros((SEQ_LEN, D), jnp.float32))
    return (resid + moe_out).astype(jnp.bfloat16)
```

```python
import functools
import math

import jax
import jax.numpy as jnp
from jax import lax
from jax.experimental import pallas as pl
from jax.experimental.pallas import tpu as pltpu
from jax.sharding import PartitionSpec as P

rope_base = 1000000.0
CHUNKS = 2
GROUP = 8


def rms_scale(values, gain):
    widened = values.astype(jnp.float32)
    return (
        widened
        * lax.rsqrt(jnp.mean(widened * widened, axis=-1, keepdims=True) + 1e-06)
        * gain.astype(jnp.float32)
    )


def rotate(values, positions):
    half = values.shape[-1] // 2
    freqs = jnp.exp(
        -math.log(rope_base) * jnp.arange(half, dtype=jnp.float32) * 2.0 / values.shape[-1]
    )
    angles = positions[..., None] * freqs
    first = values[..., :half]
    second = values[..., half:]
    return jnp.concatenate(
        [
            first * jnp.cos(angles) - second * jnp.sin(angles),
            second * jnp.cos(angles) + first * jnp.sin(angles),
        ],
        axis=-1,
    )


def params(megabytes, axes=1):
    return pltpu.CompilerParams(
        vmem_limit_bytes=megabytes * 1024 * 1024, dimension_semantics=("arbitrary",) * axes
    )


def f32dot(a, b):
    return jnp.dot(a, b, preferred_element_type=jnp.float32)


def attend_kernel(heads, size, width, qblock_ref, q_ref, kv_ref, kpos_ref, out_ref, vext):
    index = pl.program_id(0)
    rows = q_ref.shape[1]

    @pl.when(index == 0)
    def _():
        vext[:, :size] = kv_ref[:, size:]
        vext[:, size:] = jnp.ones((kv_ref.shape[0], size), vext.dtype)

    q = jnp.concatenate([q_ref[0, :, h * size : (h + 1) * size] for h in range(heads)], axis=0)
    row_pos = qblock_ref[index] * rows + lax.rem(
        lax.broadcasted_iota(jnp.int32, (heads * rows, 1), 0), rows
    )
    total = jnp.zeros((heads * rows, 2 * size), jnp.float32)
    for step in range(kv_ref.shape[0] // width):
        part = pl.ds(step * width, width)
        scores = lax.dot_general(
            q, kv_ref[part, :size], (((1,), (1,)), ((), ())), preferred_element_type=jnp.float32
        )
        mass = jnp.exp(scores * (1.0 / math.sqrt(size)))
        mass = jnp.where(kpos_ref[:, part] <= row_pos, mass, 0.0).astype(jnp.bfloat16)
        total = total + f32dot(mass, vext[part, :])
    lane = lax.broadcasted_iota(jnp.int32, (rows, size), 1)
    sums = jnp.zeros((rows, size), jnp.float32)
    for h in range(heads):
        block = total[h * rows : (h + 1) * rows]
        out_ref[0, :, h * size : (h + 1) * size] = block[:, :size].astype(jnp.bfloat16)
        high = block[:, size:].astype(jnp.bfloat16).astype(jnp.float32)
        sums = jnp.where(lane == 2 * h, high, sums)
        sums = jnp.where(lane == 2 * h + 1, block[:, size:] - high, sums)
    out_ref[0, :, heads * size :] = sums.astype(jnp.bfloat16)


def attend(queries, key_values, q_blocks, key_pos, heads, size):
    groups, rows, columns = queries.shape
    length = key_values.shape[0]
    whole = lambda i, s: (0, 0)
    return pl.pallas_call(
        functools.partial(attend_kernel, heads, size, 512),
        grid_spec=pltpu.PrefetchScalarGridSpec(
            num_scalar_prefetch=1,
            grid=(groups,),
            in_specs=[
                pl.BlockSpec((1, rows, columns), lambda i, s: (i, 0, 0)),
                pl.BlockSpec((length, 2 * size), whole),
                pl.BlockSpec((1, length), whole),
            ],
            out_specs=pl.BlockSpec((1, rows, columns + size), lambda i, s: (i, 0, 0)),
            scratch_shapes=[pltpu.VMEM((length, 2 * size), jnp.bfloat16)],
        ),
        out_shape=jax.ShapeDtypeStruct((groups, rows, columns + size), jnp.bfloat16),
        compiler_params=params(40),
        name="attend",
    )(q_blocks, queries, key_values, key_pos)


def fold(rows, place):
    piece = rows.shape[1] // GROUP
    stacked = jnp.concatenate([rows[:, s * piece : (s + 1) * piece] for s in range(GROUP)], axis=0)
    return f32dot(place, stacked)


def unfold(stacked, count):
    return jnp.concatenate([stacked[s * count : (s + 1) * count] for s in range(GROUP)], axis=1)


def dispatch_kernel(blocks, x_ref, pick_ref, last_ref, place_ref, out_ref, stacked):
    features = x_ref.shape[1]
    piece = features // GROUP
    count = last_ref.shape[0]

    @pl.when(pl.program_id(0) == 0)
    def _():
        last = f32dot(last_ref[...], x_ref[...]).astype(jnp.bfloat16)
        for s in range(GROUP):
            stacked[s * count : (s + 1) * count, :] = last[:, s * piece : (s + 1) * piece]

    out_ref[:, :features] = f32dot(pick_ref[...], x_ref[...]).astype(jnp.bfloat16)
    out_ref[:, features:] = f32dot(place_ref[...], stacked[...]).astype(jnp.bfloat16)


def dispatch(moe_in, pick, last, place, chunk, features):
    rows, tokens = pick.shape
    count = last.shape[0]
    blocks = 4
    return pl.pallas_call(
        functools.partial(dispatch_kernel, blocks),
        grid=(blocks,),
        in_specs=[
            pl.BlockSpec((tokens, features), lambda i: (0, chunk)),
            pl.BlockSpec((rows // blocks, tokens), lambda i: (i, 0)),
            pl.BlockSpec((count, tokens), lambda i: (0, 0)),
            pl.BlockSpec((rows // blocks, rows), lambda i: (i, 0)),
        ],
        out_specs=pl.BlockSpec((rows // blocks, features + features // GROUP), lambda i: (i, 0)),
        out_shape=jax.ShapeDtypeStruct((rows, features + features // GROUP), jnp.bfloat16),
        scratch_shapes=[pltpu.VMEM((rows, features // GROUP), jnp.bfloat16)],
        compiler_params=params(32),
        cost_estimate=pl.CostEstimate(
            flops=4 * rows * tokens * features, bytes_accessed=4 * rows * features, transcendentals=0
        ),
        name="dispatch",
    )(moe_in, pick, last, place)


def take_last(x_ref, place_ref, features, last):
    count = last.shape[0]
    stacked = f32dot(place_ref[...], x_ref[:, features:]).astype(jnp.bfloat16)
    last[...] = unfold(stacked, count)


def up_first_kernel(features, x_ref, place_ref, w_ref, out_ref, last):
    rows = x_ref.shape[0]

    @pl.when(pl.program_id(0) == 0)
    def _():
        take_last(x_ref, place_ref, features, last)

    out_ref[:rows, :] = f32dot(x_ref[:, :features], w_ref[0])
    out_ref[rows:, :] = f32dot(last[...], w_ref[0])


def up_first(received, place, weights, features, count):
    rows, wide = received.shape
    columns = weights.shape[2]
    tile = 256
    return pl.pallas_call(
        functools.partial(up_first_kernel, features),
        grid=(columns // tile,),
        in_specs=[
            pl.BlockSpec((rows, wide), lambda n: (0, 0)),
            pl.BlockSpec((rows, rows), lambda n: (0, 0)),
            pl.BlockSpec((1, features, tile), lambda n: (0, 0, n)),
        ],
        out_specs=pl.BlockSpec((rows + count, tile), lambda n: (0, n)),
        out_shape=jax.ShapeDtypeStruct((rows + count, columns), jnp.float32),
        scratch_shapes=[pltpu.VMEM((count, features), jnp.bfloat16)],
        compiler_params=params(48),
        cost_estimate=pl.CostEstimate(
            flops=2 * rows * features * columns, bytes_accessed=20000000, transcendentals=0
        ),
        name="up_first",
    )(received, place, weights)


def up_last_kernel(features, x_ref, place_ref, wg_ref, wu_ref, g_ref, u_ref, out_ref, last):
    rows = x_ref.shape[0]

    @pl.when(pl.program_id(0) == 0)
    def _():
        take_last(x_ref, place_ref, features, last)

    def finish(part, x):
        gate = g_ref[part, :] + f32dot(x, wg_ref[0])
        up = u_ref[part, :] + f32dot(x, wu_ref[0])
        out_ref[part, :] = (gate / (1.0 + jnp.exp(-gate)) * up).astype(jnp.bfloat16)

    finish(pl.ds(0, rows), x_ref[:, :features])
    finish(pl.ds(rows, last.shape[0]), last[...])


def up_last(received, place, weights, earlier, features, chunk, count):
    rows, wide = received.shape
    hidden = weights.shape[2] // 2
    tile = 256
    steps = hidden // tile
    return pl.pallas_call(
        functools.partial(up_last_kernel, features),
        grid=(steps,),
        in_specs=[
            pl.BlockSpec((rows, wide), lambda n: (0, 0)),
            pl.BlockSpec((rows, rows), lambda n: (0, 0)),
            pl.BlockSpec((1, features, tile), lambda n: (0, chunk, n)),
            pl.BlockSpec((1, features, tile), lambda n: (0, chunk, n + steps)),
            pl.BlockSpec((rows + count, tile), lambda n: (0, n)),
            pl.BlockSpec((rows + count, tile), lambda n: (0, n + steps)),
        ],
        out_specs=pl.BlockSpec((rows + count, tile), lambda n: (0, n)),
        out_shape=jax.ShapeDtypeStruct((rows + count, hidden), jnp.bfloat16),
        scratch_shapes=[pltpu.VMEM((count, features), jnp.bfloat16)],
        compiler_params=params(52),
        cost_estimate=pl.CostEstimate(
            flops=4 * rows * features * hidden, bytes_accessed=20000000, transcendentals=0
        ),
        name="up_last",
    )(received, place, weights, weights, earlier, earlier)


def down_kernel(x_ref, last_ref, place_ref, w_ref, out_ref, stacked):
    features = w_ref.shape[2]
    piece = features // GROUP
    count = last_ref.shape[0]

    @pl.when(pl.program_id(0) == 0)
    def _():
        last = f32dot(last_ref[...], w_ref[0]).astype(jnp.bfloat16)
        for s in range(GROUP):
            stacked[s * count : (s + 1) * count, :] = last[:, s * piece : (s + 1) * piece]

    out_ref[:, :features] = f32dot(x_ref[...], w_ref[0]).astype(jnp.bfloat16)
    out_ref[:, features:] = f32dot(place_ref[...], stacked[...]).astype(jnp.bfloat16)


def down(activated, place, weights, features, chunk, count):
    rows = activated.shape[0] - count
    hidden = activated.shape[1]
    blocks = 4
    return pl.pallas_call(
        down_kernel,
        grid=(blocks,),
        in_specs=[
            pl.BlockSpec((rows // blocks, hidden), lambda i: (i, 0)),
            pl.BlockSpec((count, hidden), lambda i: (rows // count, 0)),
            pl.BlockSpec((rows // blocks, rows), lambda i: (i, 0)),
            pl.BlockSpec((1, hidden, features), lambda i: (0, 0, chunk)),
        ],
        out_specs=pl.BlockSpec((rows // blocks, features + features // GROUP), lambda i: (i, 0)),
        out_shape=jax.ShapeDtypeStruct((rows, features + features // GROUP), jnp.bfloat16),
        scratch_shapes=[pltpu.VMEM((rows, features // GROUP), jnp.bfloat16)],
        compiler_params=params(40),
        cost_estimate=pl.CostEstimate(
            flops=2 * rows * hidden * features, bytes_accessed=10000000, transcendentals=0
        ),
        name="down",
    )(activated, activated, place, weights)


def combine_kernel(features, x_ref, place_ref, w_ref, wlast_ref, resid_ref, out_ref, total, stacked):
    index = pl.program_id(0)
    tokens = resid_ref.shape[0]
    count = wlast_ref.shape[1]
    added = f32dot(w_ref[...], x_ref[:, :features])
    moved = f32dot(place_ref[...], x_ref[:, features:])

    @pl.when(index == 0)
    def _():
        total[...] = added
        stacked[...] = moved

    @pl.when(index > 0)
    def _():
        total[...] += added
        stacked[...] += moved

    @pl.when(index == pl.num_programs(0) - 1)
    def _():
        last = unfold(stacked[...].astype(jnp.bfloat16), count)
        both = total[...] + f32dot(wlast_ref[...], last)
        out_ref[...] = (resid_ref[...] + both[:tokens] + both[tokens:]).astype(jnp.bfloat16)


def combine(returned, place, weights, last_weights, resid, features, chunk):
    rows, wide = returned.shape
    tokens = resid.shape[0]
    count = last_weights.shape[1]
    blocks = 4
    return pl.pallas_call(
        functools.partial(combine_kernel, features),
        grid=(blocks,),
        in_specs=[
            pl.BlockSpec((rows // blocks, wide), lambda i: (i, 0)),
            pl.BlockSpec((rows, rows // blocks), lambda i: (0, i)),
            pl.BlockSpec((2 * tokens, rows // blocks), lambda i: (0, i)),
            pl.BlockSpec((2 * tokens, count), lambda i: (0, 0)),
            pl.BlockSpec((tokens, features), lambda i: (0, chunk)),
        ],
        out_specs=pl.BlockSpec((tokens, features), lambda i: (0, 0)),
        out_shape=jax.ShapeDtypeStruct((tokens, features), jnp.bfloat16),
        scratch_shapes=[
            pltpu.VMEM((2 * tokens, features), jnp.float32),
            pltpu.VMEM((rows, wide - features), jnp.float32),
        ],
        compiler_params=params(32),
        cost_estimate=pl.CostEstimate(
            flops=4 * rows * tokens * features, bytes_accessed=2 * rows * wide, transcendentals=0
        ),
        name="combine",
    )(returned, place, weights, last_weights, resid)


def split_high_low(values):
    high = values.astype(jnp.bfloat16)
    return jnp.concatenate(
        [high, (values - high.astype(jnp.float32)).astype(jnp.bfloat16)], axis=0
    )


def on_device(
    tokens,
    block_order,
    attn_gain,
    query_gain,
    key_gain,
    w_qkv,
    w_out,
    moe_gain,
    router,
    routes,
    w_gate_up,
    w_down,
):
    rows, model_width = tokens.shape
    size = query_gain.shape[0]
    ctx_size, exp_size = lax.axis_size("ctx"), lax.axis_size("exp")
    ctx_at, exp_at = lax.axis_index("ctx"), lax.axis_index("exp")
    local_rows = jnp.arange(rows, dtype=jnp.int32)
    order = block_order.reshape(ctx_size, exp_size)
    q_blocks = lax.dynamic_index_in_dim(order, exp_at, 1, keepdims=False)
    k_blocks = lax.dynamic_index_in_dim(order, ctx_at, 0, keepdims=False)
    key_pos = (k_blocks[:, None] * rows + local_rows[None, :]).reshape(1, -1)
    own_pos = lax.dynamic_index_in_dim(q_blocks, ctx_at, 0, keepdims=False) * rows + local_rows

    normed = rms_scale(tokens, attn_gain).astype(jnp.bfloat16)
    mixed = f32dot(normed, lax.all_gather(w_qkv, "exp", axis=1, tiled=True))
    heads = mixed.shape[1] // size - 2
    queries = mixed[:, : heads * size].reshape(rows, heads, size)
    queries = (
        rotate(rms_scale(queries, query_gain), own_pos[:, None].astype(jnp.float32))
        .astype(jnp.bfloat16)
        .reshape(rows, heads * size)
    )
    keys = rotate(
        rms_scale(mixed[:, heads * size : (heads + 1) * size], key_gain),
        own_pos.astype(jnp.float32),
    ).astype(jnp.bfloat16)
    values = mixed[:, (heads + 1) * size :].astype(jnp.bfloat16)
    key_values = jnp.concatenate([keys, values], axis=1)

    def spread(x, axis):
        copies = jnp.broadcast_to(x[None], (lax.axis_size(axis),) + x.shape)
        return lax.all_to_all(copies, axis, split_axis=0, concat_axis=0, tiled=True)

    all_keys = spread(key_values, "exp").reshape(exp_size * rows, 2 * size)
    all_queries = spread(queries, "ctx")
    parts = attend(all_queries, all_keys, q_blocks, key_pos, heads, size)
    parts = lax.all_to_all(parts, "ctx", split_axis=0, concat_axis=0, tiled=True)
    summed = jnp.sum(parts.astype(jnp.float32), axis=0)
    totals = jnp.sum(
        summed[:, heads * size : heads * (size + 2)].reshape(rows, heads, 2), axis=2
    )
    attended = (
        (summed[:, : heads * size].reshape(rows, heads, size) / totals[:, :, None])
        .astype(jnp.bfloat16)
        .reshape(rows, heads * size)
    )
    projected = f32dot(attended, lax.all_gather(w_out, "exp", axis=0, tiled=True))
    resid = tokens.astype(jnp.float32) + projected
    moe_in = rms_scale(resid, moe_gain).astype(jnp.bfloat16)

    count = router.shape[1]
    experts = jnp.arange(count, dtype=jnp.int32)
    named = jnp.any(routes.T[:, None, :] == experts[None, :, None], axis=0)
    before = (local_rows[:, None] < local_rows[None, :]).astype(jnp.bfloat16)
    rank = f32dot(named.astype(jnp.bfloat16), before).astype(jnp.int32)
    slots = jnp.arange(GROUP, dtype=jnp.int32)
    in_slot = (named[:, None, :] & (rank[:, None, :] == slots[None, :, None])).reshape(
        count * GROUP, rows
    )
    in_last = named & (rank == GROUP)
    pick = in_slot.astype(jnp.bfloat16)
    pick_last = in_last.astype(jnp.bfloat16)
    folded = jnp.arange(count * GROUP, dtype=jnp.int32)
    place = (
        (folded[:, None] % GROUP) * count + folded[:, None] // GROUP == folded[None, :]
    ).astype(jnp.bfloat16)
    place_back = (
        (folded[None, :] % GROUP) * count + folded[None, :] // GROUP == folded[:, None]
    ).astype(jnp.bfloat16)

    logits = lax.dot_general(
        router, moe_in, (((0,), (1,)), ((), ())), preferred_element_type=jnp.float32
    )
    largest = jnp.max(jnp.where(named, logits, -jnp.inf), axis=0, keepdims=True)
    shares = jnp.where(named, jnp.exp(logits - largest), 0.0)
    shares = shares / jnp.sum(shares, axis=0, keepdims=True)
    slot_weights = jnp.where(in_slot, jnp.repeat(shares, GROUP, axis=0), 0.0)
    weights = split_high_low(slot_weights.T)
    last_weights = split_high_low(jnp.where(in_last, shares, 0.0).T)

    features = model_width // CHUNKS
    wide = features + features // GROUP

    def exchange(x):
        x = lax.all_to_all(
            x.reshape(count, GROUP, wide), ("ctx", "exp"), split_axis=0, concat_axis=0, tiled=True
        )
        return x.reshape(count * GROUP, wide)

    received = [
        exchange(dispatch(moe_in, pick, pick_last, place, c, features)) for c in range(CHUNKS)
    ]
    partial = up_first(received[0], place_back, w_gate_up, features, count)
    activated = up_last(received[1], place_back, w_gate_up, partial, features, 1, count)
    outputs = []
    for c in range(CHUNKS):
        returned = exchange(down(activated, place, w_down, features, c, count))
        outputs.append(combine(returned, place_back, weights, last_weights, resid, features, c))
    return jnp.concatenate(outputs, axis=1)


def solution(mesh):
    return jax.shard_map(
        on_device,
        mesh=mesh,
        in_specs=(
            P(("ctx", "exp"), None),
            P(),
            P(),
            P(),
            P(),
            P(None, "exp"),
            P("exp", None),
            P(),
            P(),
            P(("ctx", "exp"), None),
            P(("ctx", "exp"), None, None),
            P(("ctx", "exp"), None, None),
        ),
        out_specs=P(("ctx", "exp"), None),
        check_vma=False,
    )
```

```python
import functools
import math

import jax
import jax.numpy as jnp
from jax import lax
from jax.experimental import pallas as pl
from jax.experimental.pallas import tpu as pltpu
from jax.sharding import PartitionSpec as P

rope_base = 1000000.0
GROUP = 8
VMEM_MB = 58


def rms_scale(values, gain):
    widened = values.astype(jnp.float32)
    return (
        widened
        * lax.rsqrt(jnp.mean(widened * widened, axis=-1, keepdims=True) + 1e-06)
        * gain.astype(jnp.float32)
    )


def rotate(values, positions):
    half = values.shape[-1] // 2
    freqs = jnp.exp(
        -math.log(rope_base) * jnp.arange(half, dtype=jnp.float32) * 2.0 / values.shape[-1]
    )
    angles = positions[..., None] * freqs
    first = values[..., :half]
    second = values[..., half:]
    return jnp.concatenate(
        [
            first * jnp.cos(angles) - second * jnp.sin(angles),
            second * jnp.cos(angles) + first * jnp.sin(angles),
        ],
        axis=-1,
    )


def params(axes=1):
    return pltpu.CompilerParams(
        vmem_limit_bytes=VMEM_MB * 1024 * 1024, dimension_semantics=("arbitrary",) * axes
    )


def f32dot(a, b):
    return jnp.dot(a, b, preferred_element_type=jnp.float32)


def project_kernel(order_ref, x_ref, pieces_ref, out_ref, whole):
    columns = pieces_ref.shape[1]

    @pl.when(pl.program_id(0) == 0)
    def _():
        for e in range(pieces_ref.shape[0]):
            whole[e * columns : (e + 1) * columns, :] = pieces_ref[order_ref[e]]

    out_ref[...] = lax.dot_general(
        x_ref[...], whole[...], (((1,), (1,)), ((), ())), preferred_element_type=jnp.float32
    ).astype(jnp.bfloat16)


def project(x, pieces, order):
    rows, depth = x.shape
    shards, columns = pieces.shape[:2]
    blocks = 4
    return pl.pallas_call(
        project_kernel,
        grid_spec=pltpu.PrefetchScalarGridSpec(
            num_scalar_prefetch=1,
            grid=(blocks,),
            in_specs=[
                pl.BlockSpec((rows // blocks, depth), lambda i, s: (i, 0)),
                pl.BlockSpec(pieces.shape, lambda i, s: (0, 0, 0)),
            ],
            out_specs=pl.BlockSpec((rows // blocks, shards * columns), lambda i, s: (i, 0)),
            scratch_shapes=[pltpu.VMEM((shards * columns, depth), jnp.bfloat16)],
        ),
        out_shape=jax.ShapeDtypeStruct((rows, shards * columns), jnp.bfloat16),
        compiler_params=params(),
        name="project",
    )(order, x, pieces)


def attend_kernel(heads, size, width, place_ref, qblock_ref, q_ref, kv_ref, kpos_ref, out_ref, vext):
    index = pl.program_id(0)
    rows = q_ref.shape[1]

    @pl.when(index == 0)
    def _():
        vext[:, :size] = kv_ref[:, size:]
        vext[:, size:] = jnp.ones((kv_ref.shape[0], size), vext.dtype)

    q = jnp.concatenate([q_ref[0, :, h * size : (h + 1) * size] for h in range(heads)], axis=0)
    row_pos = qblock_ref[index] * rows + lax.rem(
        lax.broadcasted_iota(jnp.int32, (heads * rows, 1), 0), rows
    )
    total = jnp.zeros((heads * rows, 2 * size), jnp.float32)
    for step in range(kv_ref.shape[0] // width):
        part = pl.ds(step * width, width)
        scores = lax.dot_general(
            q, kv_ref[part, :size], (((1,), (1,)), ((), ())), preferred_element_type=jnp.float32
        )
        mass = jnp.exp(scores * (1.0 / math.sqrt(size)))
        mass = jnp.where(kpos_ref[:, part] <= row_pos, mass, 0.0).astype(jnp.bfloat16)
        total = total + f32dot(mass, vext[part, :])
    lane = lax.broadcasted_iota(jnp.int32, (rows, size), 1)
    sums = jnp.zeros((rows, size), jnp.float32)
    for h in range(heads):
        block = total[h * rows : (h + 1) * rows]
        out_ref[0, :, h * size : (h + 1) * size] = block[:, :size].astype(jnp.bfloat16)
        high = block[:, size:].astype(jnp.bfloat16).astype(jnp.float32)
        sums = jnp.where(lane == 2 * h, high, sums)
        sums = jnp.where(lane == 2 * h + 1, block[:, size:] - high, sums)
    out_ref[0, :, heads * size :] = sums.astype(jnp.bfloat16)


def attend(queries, key_values, q_place, q_blocks, key_pos, heads, size):
    groups, rows, columns = queries.shape
    length = key_values.shape[0]
    whole = lambda i, p, s: (0, 0)
    return pl.pallas_call(
        functools.partial(attend_kernel, heads, size, 512),
        grid_spec=pltpu.PrefetchScalarGridSpec(
            num_scalar_prefetch=2,
            grid=(groups,),
            in_specs=[
                pl.BlockSpec((1, rows, columns), lambda i, p, s: (i, 0, 0)),
                pl.BlockSpec((length, 2 * size), whole),
                pl.BlockSpec((1, length), whole),
            ],
            out_specs=pl.BlockSpec((1, rows, columns + size), lambda i, p, s: (p[i], 0, 0)),
            scratch_shapes=[pltpu.VMEM((length, 2 * size), jnp.bfloat16)],
        ),
        out_shape=jax.ShapeDtypeStruct((groups, rows, columns + size), jnp.bfloat16),
        compiler_params=params(),
        name="attend",
    )(q_place, q_blocks, queries, key_values, key_pos)


def finish_kernel(heads, size, parts_ref, w_ref, x_ref, gain_ref, resid_ref, out_ref):
    summed = parts_ref[0].astype(jnp.float32)
    for c in range(1, parts_ref.shape[0]):
        summed = summed + parts_ref[c].astype(jnp.float32)
    base = heads * size
    attended = []
    for h in range(heads):
        at = base + 2 * h
        total = summed[:, at : at + 1] + summed[:, at + 1 : at + 2]
        attended.append((summed[:, h * size : (h + 1) * size] / total).astype(jnp.bfloat16))
    resid = x_ref[...].astype(jnp.float32) + f32dot(jnp.concatenate(attended, axis=1), w_ref[...])
    resid_ref[...] = resid
    scale = lax.rsqrt(jnp.mean(resid * resid, axis=1, keepdims=True) + 1e-06)
    out_ref[...] = (resid * scale * gain_ref[...].astype(jnp.float32)).astype(jnp.bfloat16)


def finish(parts, w_out, tokens, gain, heads, size):
    return pl.pallas_call(
        functools.partial(finish_kernel, heads, size),
        out_shape=[
            jax.ShapeDtypeStruct(tokens.shape, jnp.float32),
            jax.ShapeDtypeStruct(tokens.shape, jnp.bfloat16),
        ],
        compiler_params=pltpu.CompilerParams(vmem_limit_bytes=VMEM_MB * 1024 * 1024),
        name="finish",
    )(parts, w_out, tokens, gain.reshape(1, -1))


def repeat_rows(values):
    rows = values.shape[0]
    row = lax.broadcasted_iota(jnp.int32, (rows * GROUP, rows), 0)
    column = lax.broadcasted_iota(jnp.int32, (rows * GROUP, rows), 1)
    copies = (lax.div(row, GROUP) == column).astype(jnp.bfloat16)
    return f32dot(copies, values)


def slots_kernel(routes_ref, pick_ref, last_ref, named_ref):
    fanout, tokens = routes_ref.shape
    count = named_ref.shape[0]
    expert = lax.broadcasted_iota(jnp.int32, (count, tokens), 0)
    named = jnp.zeros((count, tokens), jnp.float32)
    for j in range(fanout):
        named = named + jnp.where(routes_ref[j : j + 1, :] == expert, 1.0, 0.0)
    earlier = lax.broadcasted_iota(jnp.int32, (tokens, tokens), 0)
    later = lax.broadcasted_iota(jnp.int32, (tokens, tokens), 1)
    before = (earlier < later).astype(jnp.bfloat16)
    rank = f32dot(named.astype(jnp.bfloat16), before)
    code = named * (rank + 1.0)
    named_ref[...] = named
    last_ref[...] = (code == GROUP + 1.0).astype(jnp.bfloat16)
    spread = repeat_rows(code.astype(jnp.bfloat16))
    slot = lax.rem(lax.broadcasted_iota(jnp.int32, spread.shape, 0), GROUP) + 1
    pick_ref[...] = (spread == slot.astype(jnp.float32)).astype(jnp.bfloat16)


def slots(routes_t, count):
    fanout, tokens = routes_t.shape
    return pl.pallas_call(
        slots_kernel,
        out_shape=[
            jax.ShapeDtypeStruct((count * GROUP, tokens), jnp.bfloat16),
            jax.ShapeDtypeStruct((count, tokens), jnp.bfloat16),
            jax.ShapeDtypeStruct((count, tokens), jnp.float32),
        ],
        compiler_params=pltpu.CompilerParams(vmem_limit_bytes=VMEM_MB * 1024 * 1024),
        name="slots",
    )(routes_t)


def weigh_kernel(x_ref, router_ref, named_ref, pick_ref, last_ref, out_ref, out_last_ref):
    tokens = x_ref.shape[0]
    logits = lax.dot_general(
        router_ref[...], x_ref[...], (((0,), (1,)), ((), ())), preferred_element_type=jnp.float32
    )
    named = named_ref[...] > 0.5
    largest = jnp.max(jnp.where(named, logits, -jnp.inf), axis=0, keepdims=True)
    shares = jnp.where(named, jnp.exp(jnp.minimum(logits - largest, 0.0)), 0.0)
    shares = shares / jnp.sum(shares, axis=0, keepdims=True)
    high = shares.astype(jnp.bfloat16)
    low = (shares - high.astype(jnp.float32)).astype(jnp.bfloat16)
    for at, part in ((0, high), (tokens, low)):
        out_ref[:, at : at + tokens] = repeat_rows(part).astype(jnp.bfloat16) * pick_ref[...]
        out_last_ref[:, at : at + tokens] = part * last_ref[...]


def weigh(moe_in, router, named, pick, last):
    tokens = moe_in.shape[0]
    return pl.pallas_call(
        weigh_kernel,
        out_shape=[
            jax.ShapeDtypeStruct((pick.shape[0], 2 * tokens), jnp.bfloat16),
            jax.ShapeDtypeStruct((last.shape[0], 2 * tokens), jnp.bfloat16),
        ],
        compiler_params=pltpu.CompilerParams(vmem_limit_bytes=VMEM_MB * 1024 * 1024),
        name="weigh",
    )(moe_in, router, named, pick, last)


def unfold(stacked, count):
    return jnp.concatenate([stacked[s * count : (s + 1) * count] for s in range(GROUP)], axis=1)


def dispatch_kernel(blocks, x_ref, pick_ref, last_ref, place_ref, out_ref, stacked):
    features = x_ref.shape[1]
    piece = features // GROUP
    count = last_ref.shape[0]

    @pl.when(pl.program_id(0) == 0)
    def _():
        last = f32dot(last_ref[...], x_ref[...]).astype(jnp.bfloat16)
        for s in range(GROUP):
            stacked[s * count : (s + 1) * count, :] = last[:, s * piece : (s + 1) * piece]

    out_ref[:, :features] = f32dot(pick_ref[...], x_ref[...]).astype(jnp.bfloat16)
    out_ref[:, features:] = f32dot(place_ref[...], stacked[...]).astype(jnp.bfloat16)


def dispatch(moe_in, pick, last, place, chunk, features):
    rows, tokens = pick.shape
    count = last.shape[0]
    blocks = 4
    return pl.pallas_call(
        functools.partial(dispatch_kernel, blocks),
        grid=(blocks,),
        in_specs=[
            pl.BlockSpec((tokens, features), lambda i: (0, chunk)),
            pl.BlockSpec((rows // blocks, tokens), lambda i: (i, 0)),
            pl.BlockSpec((count, tokens), lambda i: (0, 0)),
            pl.BlockSpec((rows // blocks, rows), lambda i: (i, 0)),
        ],
        out_specs=pl.BlockSpec((rows // blocks, features + features // GROUP), lambda i: (i, 0)),
        out_shape=jax.ShapeDtypeStruct((rows, features + features // GROUP), jnp.bfloat16),
        scratch_shapes=[pltpu.VMEM((rows, features // GROUP), jnp.bfloat16)],
        compiler_params=params(),
        cost_estimate=pl.CostEstimate(
            flops=4 * rows * tokens * features, bytes_accessed=4 * rows * features, transcendentals=0
        ),
        name="dispatch",
    )(moe_in, pick, last, place)


def take_last(x_ref, place_ref, features, last):
    count = last.shape[0]
    stacked = f32dot(place_ref[...], x_ref[:, features:]).astype(jnp.bfloat16)
    last[...] = unfold(stacked, count)


def up_first_kernel(features, x_ref, place_ref, w_ref, out_ref, last):
    rows = x_ref.shape[0]

    @pl.when(pl.program_id(0) == 0)
    def _():
        take_last(x_ref, place_ref, features, last)

    out_ref[:rows, :] = f32dot(x_ref[:, :features], w_ref[0])
    out_ref[rows:, :] = f32dot(last[...], w_ref[0])


def up_first(received, place, weights, features, count):
    rows, wide = received.shape
    columns = weights.shape[2]
    tile = 256
    return pl.pallas_call(
        functools.partial(up_first_kernel, features),
        grid=(columns // tile,),
        in_specs=[
            pl.BlockSpec((rows, wide), lambda n: (0, 0), pipeline_mode=pl.Buffered(1)),
            pl.BlockSpec((rows, rows), lambda n: (0, 0), pipeline_mode=pl.Buffered(1)),
            pl.BlockSpec((1, features, tile), lambda n: (0, 0, n)),
        ],
        out_specs=pl.BlockSpec((rows + count, tile), lambda n: (0, n)),
        out_shape=jax.ShapeDtypeStruct((rows + count, columns), jnp.float32),
        scratch_shapes=[pltpu.VMEM((count, features), jnp.bfloat16)],
        compiler_params=params(),
        cost_estimate=pl.CostEstimate(
            flops=2 * rows * features * columns, bytes_accessed=20000000, transcendentals=0
        ),
        name="up_first",
    )(received, place, weights)


def up_last_kernel(features, x_ref, place_ref, wg_ref, wu_ref, g_ref, u_ref, out_ref, last):
    rows = x_ref.shape[0]

    @pl.when(pl.program_id(0) == 0)
    def _():
        take_last(x_ref, place_ref, features, last)

    def finish(part, x):
        gate = g_ref[part, :] + f32dot(x, wg_ref[0])
        up = u_ref[part, :] + f32dot(x, wu_ref[0])
        out_ref[part, :] = (gate / (1.0 + jnp.exp(-gate)) * up).astype(jnp.bfloat16)

    finish(pl.ds(0, rows), x_ref[:, :features])
    finish(pl.ds(rows, last.shape[0]), last[...])


def up_last(received, place, weights, earlier, features, chunk, count):
    rows, wide = received.shape
    hidden = weights.shape[2] // 2
    tile = 256
    steps = hidden // tile
    return pl.pallas_call(
        functools.partial(up_last_kernel, features),
        grid=(steps,),
        in_specs=[
            pl.BlockSpec((rows, wide), lambda n: (0, 0), pipeline_mode=pl.Buffered(1)),
            pl.BlockSpec((rows, rows), lambda n: (0, 0), pipeline_mode=pl.Buffered(1)),
            pl.BlockSpec((1, features, tile), lambda n: (0, chunk, n)),
            pl.BlockSpec((1, features, tile), lambda n: (0, chunk, n + steps)),
            pl.BlockSpec((rows + count, tile), lambda n: (0, n)),
            pl.BlockSpec((rows + count, tile), lambda n: (0, n + steps)),
        ],
        out_specs=pl.BlockSpec((rows + count, tile), lambda n: (0, n)),
        out_shape=jax.ShapeDtypeStruct((rows + count, hidden), jnp.bfloat16),
        scratch_shapes=[pltpu.VMEM((count, features), jnp.bfloat16)],
        compiler_params=params(),
        cost_estimate=pl.CostEstimate(
            flops=4 * rows * features * hidden, bytes_accessed=20000000, transcendentals=0
        ),
        name="up_last",
    )(received, place, weights, weights, earlier, earlier)


def down_kernel(x_ref, last_ref, place_ref, w_ref, out_ref, stacked):
    features = w_ref.shape[2]
    piece = features // GROUP
    count = last_ref.shape[0]

    @pl.when(pl.program_id(0) == 0)
    def _():
        last = f32dot(last_ref[...], w_ref[0]).astype(jnp.bfloat16)
        for s in range(GROUP):
            stacked[s * count : (s + 1) * count, :] = last[:, s * piece : (s + 1) * piece]

    out_ref[:, :features] = f32dot(x_ref[...], w_ref[0]).astype(jnp.bfloat16)
    out_ref[:, features:] = f32dot(place_ref[...], stacked[...]).astype(jnp.bfloat16)


def down(activated, place, weights, features, chunk, count):
    rows = activated.shape[0] - count
    hidden = activated.shape[1]
    blocks = 4
    return pl.pallas_call(
        down_kernel,
        grid=(blocks,),
        in_specs=[
            pl.BlockSpec((rows // blocks, hidden), lambda i: (i, 0)),
            pl.BlockSpec((count, hidden), lambda i: (rows // count, 0)),
            pl.BlockSpec((rows // blocks, rows), lambda i: (i, 0)),
            pl.BlockSpec((1, hidden, features), lambda i: (0, 0, chunk)),
        ],
        out_specs=pl.BlockSpec((rows // blocks, features + features // GROUP), lambda i: (i, 0)),
        out_shape=jax.ShapeDtypeStruct((rows, features + features // GROUP), jnp.bfloat16),
        scratch_shapes=[pltpu.VMEM((rows, features // GROUP), jnp.bfloat16)],
        compiler_params=params(),
        cost_estimate=pl.CostEstimate(
            flops=2 * rows * hidden * features, bytes_accessed=10000000, transcendentals=0
        ),
        name="down",
    )(activated, activated, place, weights)


def combine_kernel(features, x_ref, place_ref, w_ref, wlast_ref, resid_ref, *rest):
    early_ref, out_ref, total, stacked = rest if len(rest) == 4 else (None, *rest)
    index = pl.program_id(0)
    tokens = resid_ref.shape[0]
    count = wlast_ref.shape[0]

    def weighted(weights, x):
        return lax.dot_general(
            weights, x, (((0,), (0,)), ((), ())), preferred_element_type=jnp.float32
        )

    added = weighted(w_ref[...], x_ref[:, :features])
    moved = f32dot(place_ref[...], x_ref[:, features:])

    @pl.when(index == 0)
    def _():
        total[...] = added
        stacked[...] = moved

    @pl.when(index > 0)
    def _():
        total[...] += added
        stacked[...] += moved

    @pl.when(index == pl.num_programs(0) - 1)
    def _():
        last = unfold(stacked[...].astype(jnp.bfloat16), count)
        both = total[...] + weighted(wlast_ref[...], last)
        out_ref[:, :features] = (resid_ref[...] + both[:tokens] + both[tokens:]).astype(
            jnp.bfloat16
        )
        if early_ref is not None:
            out_ref[:, features:] = early_ref[...]


def combine(returned, place, weights, last_weights, resid, early, features, chunk):
    rows, wide = returned.shape
    tokens = resid.shape[0]
    count = last_weights.shape[0]
    blocks = 4
    in_specs = [
        pl.BlockSpec((rows // blocks, wide), lambda i: (i, 0)),
        pl.BlockSpec((rows, rows // blocks), lambda i: (0, i)),
        pl.BlockSpec((rows // blocks, 2 * tokens), lambda i: (i, 0)),
        pl.BlockSpec((count, 2 * tokens), lambda i: (0, 0)),
        pl.BlockSpec((tokens, features), lambda i: (0, chunk)),
    ]
    operands = [returned, place, weights, last_weights, resid]
    out_wide = features
    if early is not None:
        in_specs.append(pl.BlockSpec(early.shape, lambda i: (0, 0)))
        operands.append(early)
        out_wide = features + early.shape[1]
    return pl.pallas_call(
        functools.partial(combine_kernel, features),
        grid=(blocks,),
        in_specs=in_specs,
        out_specs=pl.BlockSpec((tokens, out_wide), lambda i: (0, 0)),
        out_shape=jax.ShapeDtypeStruct((tokens, out_wide), jnp.bfloat16),
        scratch_shapes=[
            pltpu.VMEM((2 * tokens, features), jnp.float32),
            pltpu.VMEM((rows, wide - features), jnp.float32),
        ],
        compiler_params=params(),
        cost_estimate=pl.CostEstimate(
            flops=4 * rows * tokens * features, bytes_accessed=2 * rows * wide, transcendentals=0
        ),
        name="combine",
    )(*operands)


def on_device(
    tokens,
    block_order,
    attn_gain,
    query_gain,
    key_gain,
    w_qkv,
    w_out,
    moe_gain,
    router,
    routes,
    w_gate_up,
    w_down,
):
    rows, model_width = tokens.shape
    size = query_gain.shape[0]
    ctx_size, exp_size = lax.axis_size("ctx"), lax.axis_size("exp")
    ctx_at, exp_at = lax.axis_index("ctx"), lax.axis_index("exp")
    ring = 4
    inner = exp_size // ring
    x_at, z_lo = ctx_at % ring, ctx_at // ring
    y_at, z_hi, core = exp_at // inner, exp_at // 2 % 2, exp_at % 2

    def from_exp(x, source):
        return lax.ppermute(x, "exp", [(source(i), i) for i in range(exp_size)])

    def from_ctx(x, source):
        return lax.ppermute(x, "ctx", [(source(i), i) for i in range(ctx_size)])

    def gather_exp(x):
        pair = jnp.stack([x, from_exp(x, lambda i: i ^ 2)])
        line = jnp.stack(
            [pair]
            + [from_exp(pair, lambda i, k=k: (i - k * inner) % exp_size) for k in range(1, ring)]
        )
        other = from_exp(line, lambda i: i ^ 1)
        return jnp.stack([line, other]).reshape((exp_size,) + x.shape)

    def gather_ctx(x):
        pair = jnp.stack([x, from_ctx(x, lambda i: i ^ ring)])
        line = jnp.stack(
            [pair]
            + [
                from_ctx(pair, lambda i, k=k: i // ring * ring + (i - k) % ring)
                for k in range(1, ring)
            ]
        )
        return line.reshape((ctx_size,) + x.shape)

    relative = jnp.arange(exp_size, dtype=jnp.int32)
    exp_blocks = (
        (y_at - relative // 2 % ring) % ring * inner
        + (z_hi + relative % 2) % 2 * 2
        + (core + relative // (2 * ring)) % 2
    )
    piece_of = (
        (core + relative) % 2 * (2 * ring)
        + (y_at - relative // inner) % ring * 2
        + (z_hi + relative // 2) % 2
    )
    near = jnp.arange(ctx_size, dtype=jnp.int32)
    ctx_blocks = (z_lo + near) % 2 * ring + (x_at - near // 2) % ring

    def block_numbers(devices):
        every = jnp.arange(block_order.shape[0], dtype=jnp.int32)
        return jnp.sum(
            jnp.where(devices[:, None] == every[None, :], block_order[None, :], 0), axis=1
        )

    k_blocks = block_numbers(ctx_at * exp_size + exp_blocks)
    q_blocks = block_numbers(ctx_blocks * exp_size + exp_at)
    local_rows = jnp.arange(rows, dtype=jnp.int32)
    key_pos = (k_blocks[:, None] * rows + local_rows[None, :]).reshape(1, -1)
    own_pos = q_blocks[0] * rows + local_rows

    count = router.shape[1]
    pick, pick_last, named = slots(routes.T, count)
    folded = jnp.arange(count * GROUP, dtype=jnp.int32)
    place = (
        (folded[:, None] % GROUP) * count + folded[:, None] // GROUP == folded[None, :]
    ).astype(jnp.bfloat16)
    place_back = (
        (folded[None, :] % GROUP) * count + folded[None, :] // GROUP == folded[:, None]
    ).astype(jnp.bfloat16)

    depth = model_width // ctx_size
    widened = tokens.astype(jnp.float32)
    row_scale = lax.rsqrt(jnp.mean(widened * widened, axis=1, keepdims=True) + 1e-06)
    gained = (widened * attn_gain.astype(jnp.float32)).astype(jnp.bfloat16)
    gained = jnp.transpose(gained.reshape(rows, ctx_size, depth), (1, 0, 2))
    w_share = lax.dynamic_slice_in_dim(w_qkv.T, ctx_at * depth, depth, 1)
    pieces = gather_exp(w_share)
    w_out, pieces = lax.optimization_barrier((w_out, pieces))
    w_out_all = lax.all_gather(w_out, "exp", axis=0, tiled=True)

    def swap_ctx(x):
        return lax.all_to_all(x, "ctx", split_axis=0, concat_axis=0, tiled=True)

    shares = swap_ctx(gained).reshape(ctx_size * rows, depth)
    shares, pick, pick_last, named, place, place_back, key_pos, q_blocks = lax.optimization_barrier(
        (shares, pick, pick_last, named, place, place_back, key_pos, q_blocks)
    )
    mixed = swap_ctx(project(shares, pieces, piece_of).reshape(ctx_size, rows, -1))
    mixed = jnp.sum(mixed.astype(jnp.float32), axis=0) * row_scale
    heads = mixed.shape[1] // size - 2
    queries = mixed[:, : heads * size].reshape(rows, heads, size)
    queries = (
        rotate(rms_scale(queries, query_gain), own_pos[:, None].astype(jnp.float32))
        .astype(jnp.bfloat16)
        .reshape(rows, heads * size)
    )
    keys = rotate(
        rms_scale(mixed[:, heads * size : (heads + 1) * size], key_gain),
        own_pos.astype(jnp.float32),
    ).astype(jnp.bfloat16)
    values = mixed[:, (heads + 1) * size :].astype(jnp.bfloat16)
    key_values = jnp.concatenate([keys, values], axis=1)

    all_keys = gather_exp(key_values).reshape(exp_size * rows, 2 * size)
    all_queries = gather_ctx(queries)
    parts = attend(all_queries, all_keys, ctx_blocks, q_blocks, key_pos, heads, size)
    resid, moe_in = finish(swap_ctx(parts), w_out_all, tokens, moe_gain, heads, size)

    def exchange(x):
        wide = x.shape[1]
        x = lax.all_to_all(
            x.reshape(count, GROUP, wide), ("ctx", "exp"), split_axis=0, concat_axis=0, tiled=True
        )
        return x.reshape(count * GROUP, wide)

    main = model_width // 4 * 3
    rest = model_width - main
    first = exchange(dispatch(moe_in, pick, pick_last, place, 0, main))
    second = exchange(dispatch(moe_in, pick, pick_last, place, main // rest, rest))
    first, moe_in = lax.optimization_barrier((first, moe_in))
    weights, last_weights = weigh(moe_in, router, named, pick, pick_last)
    partial = up_first(first, place_back, w_gate_up, main, count)
    activated = up_last(second, place_back, w_gate_up, partial, rest, main // rest, count)
    back_rest = exchange(down(activated, place, w_down, rest, main // rest, count))
    back_main = exchange(down(activated, place, w_down, main, 0, count))
    early = combine(
        back_rest, place_back, weights, last_weights, resid, None, rest, main // rest
    )
    return combine(back_main, place_back, weights, last_weights, resid, early, main, 0)


def solution(mesh):
    return jax.shard_map(
        on_device,
        mesh=mesh,
        in_specs=(
            P(("ctx", "exp"), None),
            P(),
            P(),
            P(),
            P(),
            P(None, "exp"),
            P("exp", None),
            P(),
            P(),
            P(("ctx", "exp"), None),
            P(("ctx", "exp"), None, None),
            P(("ctx", "exp"), None, None),
        ),
        out_specs=P(("ctx", "exp"), None),
        check_vma=False,
    )
```

```python
import functools
import math

import jax
import jax.numpy as jnp
from jax import lax
from jax.experimental import pallas as pl
from jax.experimental.pallas import tpu as pltpu
from jax.sharding import PartitionSpec as P

rope_base = 1000000.0
GROUP = 8
VMEM_MB = 58
HIDDEN = -30000.0


def rms_scale(values, gain):
    widened = values.astype(jnp.float32)
    return (
        widened
        * lax.rsqrt(jnp.mean(widened * widened, axis=-1, keepdims=True) + 1e-06)
        * gain.astype(jnp.float32)
    )


def rotate(values, positions):
    half = values.shape[-1] // 2
    freqs = jnp.exp(
        -math.log(rope_base) * jnp.arange(half, dtype=jnp.float32) * 2.0 / values.shape[-1]
    )
    angles = positions[..., None] * freqs
    first = values[..., :half]
    second = values[..., half:]
    return jnp.concatenate(
        [
            first * jnp.cos(angles) - second * jnp.sin(angles),
            second * jnp.cos(angles) + first * jnp.sin(angles),
        ],
        axis=-1,
    )


def params(axes=1):
    return pltpu.CompilerParams(
        vmem_limit_bytes=VMEM_MB * 1024 * 1024, dimension_semantics=("arbitrary",) * axes
    )


def f32dot(a, b):
    return jnp.dot(a, b, preferred_element_type=jnp.float32)


def whole_block(shape):
    zeros = (0,) * len(shape)
    return pl.BlockSpec(shape, lambda *_: zeros, pipeline_mode=pl.Buffered(1))


def project_kernel(order_ref, x_ref, near_ref, far_ref, out_ref, whole):
    half, columns = near_ref.shape[:2]

    @pl.when(pl.program_id(0) == 0)
    def _():
        for e in range(2 * half):
            at = order_ref[e]
            near = near_ref[lax.rem(at, half)].astype(jnp.float32)
            far = far_ref[lax.rem(at, half)].astype(jnp.float32)
            whole[e * columns : (e + 1) * columns, :] = jnp.where(at < half, near, far).astype(
                jnp.bfloat16
            )

    out_ref[...] = lax.dot_general(
        x_ref[...], whole[...], (((1,), (1,)), ((), ())), preferred_element_type=jnp.float32
    ).astype(jnp.bfloat16)


def project(x, near, far, order):
    rows, depth = x.shape
    half, columns = near.shape[:2]
    blocks = 4
    return pl.pallas_call(
        project_kernel,
        grid_spec=pltpu.PrefetchScalarGridSpec(
            num_scalar_prefetch=1,
            grid=(blocks,),
            in_specs=[
                pl.BlockSpec((rows // blocks, depth), lambda i, s: (i, 0)),
                whole_block(near.shape),
                whole_block(far.shape),
            ],
            out_specs=pl.BlockSpec((rows // blocks, 2 * half * columns), lambda i, s: (i, 0)),
            scratch_shapes=[pltpu.VMEM((2 * half * columns, depth), jnp.bfloat16)],
        ),
        out_shape=jax.ShapeDtypeStruct((rows, 2 * half * columns), jnp.bfloat16),
        compiler_params=params(),
        name="project",
    )(order, x, near, far)


def attend_kernel(
    heads, size, width, place_ref, *refs
):
    q_refs, (near_ref, far_ref, hide_ref, out_ref, keys, values) = refs[:-6], refs[-6:]
    index = pl.program_id(0)
    pair, rows = q_refs[0].shape[:2]
    half = near_ref.shape[0]
    length = 2 * half

    @pl.when(index == 0)
    def _():
        for at, ref in ((0, near_ref), (half, far_ref)):
            keys[at : at + half, :size] = ref[:, :size]
            values[at : at + half, :size] = ref[:, size:]
        keys[:, size:] = hide_ref[...]
        values[:, size:] = jnp.ones((length, size), jnp.bfloat16)

    def body(q_ref, step, own):
        mark = lax.broadcasted_iota(jnp.int32, (rows, size), 1) == step
        mark = jnp.where(mark, 1.0, 0.0).astype(jnp.bfloat16)
        q = jnp.concatenate(
            [
                jnp.concatenate([q_ref[:, h * size : (h + 1) * size], mark], axis=1)
                for h in range(heads)
            ],
            axis=0,
        )
        total = jnp.zeros((heads * rows, 2 * size), jnp.float32)
        for start in range(0, length, width):
            part = pl.ds(start, width)
            scores = lax.dot_general(
                q, keys[part, :], (((1,), (1,)), ((), ())), preferred_element_type=jnp.float32
            )
            if own and start == 0:
                row = lax.rem(lax.broadcasted_iota(jnp.int32, scores.shape, 0), rows)
                key = lax.broadcasted_iota(jnp.int32, scores.shape, 1)
                scores = jnp.where((key > row) & (key < rows), HIDDEN, scores)
            mass = jnp.exp2(scores).astype(jnp.bfloat16)
            total = total + f32dot(mass, values[part, :])
        lane = lax.broadcasted_iota(jnp.int32, (rows, size), 1)
        sums = jnp.zeros((rows, size), jnp.float32)
        for h in range(heads):
            block = total[h * rows : (h + 1) * rows]
            out_ref[0, :, h * size : (h + 1) * size] = block[:, :size].astype(jnp.bfloat16)
            high = block[:, size:].astype(jnp.bfloat16).astype(jnp.float32)
            sums = jnp.where(lane == 2 * h, high, sums)
            sums = jnp.where(lane == 2 * h + 1, block[:, size:] - high, sums)
        out_ref[0, :, heads * size :] = sums.astype(jnp.bfloat16)

    for step in range(len(q_refs) * pair):
        pl.when(index == step)(
            functools.partial(body, q_refs[step // pair].at[step % pair], step, step == 0)
        )


def attend(queries, near, far, hide, q_place, heads, size):
    pair, rows, columns = queries[0].shape
    groups = len(queries) * pair
    length = 2 * near.shape[0]
    return pl.pallas_call(
        functools.partial(attend_kernel, heads, size, 512),
        grid_spec=pltpu.PrefetchScalarGridSpec(
            num_scalar_prefetch=1,
            grid=(groups,),
            in_specs=[whole_block(x.shape) for x in (*queries, near, far, hide)],
            out_specs=pl.BlockSpec((1, rows, columns + size), lambda i, p: (p[i], 0, 0)),
            scratch_shapes=[pltpu.VMEM((length, 2 * size), jnp.bfloat16)] * 2,
        ),
        out_shape=jax.ShapeDtypeStruct((groups, rows, columns + size), jnp.bfloat16),
        compiler_params=params(),
        name="attend",
    )(q_place, *queries, near, far, hide)


def repeat_rows(values):
    rows = values.shape[0]
    row = lax.broadcasted_iota(jnp.int32, (rows * GROUP, rows), 0)
    column = lax.broadcasted_iota(jnp.int32, (rows * GROUP, rows), 1)
    copies = (lax.div(row, GROUP) == column).astype(jnp.bfloat16)
    return f32dot(copies, values)


def slots_kernel(routes_ref, pick_ref, last_ref, named_ref):
    fanout, tokens = routes_ref.shape
    count = named_ref.shape[0]
    expert = lax.broadcasted_iota(jnp.int32, (count, tokens), 0)
    named = jnp.zeros((count, tokens), jnp.float32)
    for j in range(fanout):
        named = named + jnp.where(routes_ref[j : j + 1, :] == expert, 1.0, 0.0)
    earlier = lax.broadcasted_iota(jnp.int32, (tokens, tokens), 0)
    later = lax.broadcasted_iota(jnp.int32, (tokens, tokens), 1)
    before = (earlier < later).astype(jnp.bfloat16)
    rank = f32dot(named.astype(jnp.bfloat16), before)
    code = named * (rank + 1.0)
    named_ref[...] = named
    last_ref[...] = (code == GROUP + 1.0).astype(jnp.bfloat16)
    spread = repeat_rows(code.astype(jnp.bfloat16))
    slot = lax.rem(lax.broadcasted_iota(jnp.int32, spread.shape, 0), GROUP) + 1
    pick_ref[...] = (spread == slot.astype(jnp.float32)).astype(jnp.bfloat16)


def slots(routes_t, count):
    fanout, tokens = routes_t.shape
    return pl.pallas_call(
        slots_kernel,
        out_shape=[
            jax.ShapeDtypeStruct((count * GROUP, tokens), jnp.bfloat16),
            jax.ShapeDtypeStruct((count, tokens), jnp.bfloat16),
            jax.ShapeDtypeStruct((count, tokens), jnp.float32),
        ],
        compiler_params=pltpu.CompilerParams(vmem_limit_bytes=VMEM_MB * 1024 * 1024),
        name="slots",
    )(routes_t)


def weigh_kernel(x_ref, router_ref, named_ref, pick_ref, last_ref, out_ref, out_last_ref):
    tokens = x_ref.shape[0]
    logits = lax.dot_general(
        router_ref[...], x_ref[...], (((0,), (1,)), ((), ())), preferred_element_type=jnp.float32
    )
    named = named_ref[...] > 0.5
    largest = jnp.max(jnp.where(named, logits, -jnp.inf), axis=0, keepdims=True)
    shares = jnp.where(named, jnp.exp(jnp.minimum(logits - largest, 0.0)), 0.0)
    shares = shares / jnp.sum(shares, axis=0, keepdims=True)
    high = shares.astype(jnp.bfloat16)
    low = (shares - high.astype(jnp.float32)).astype(jnp.bfloat16)
    for at, part in ((0, high), (tokens, low)):
        out_ref[:, at : at + tokens] = repeat_rows(part).astype(jnp.bfloat16) * pick_ref[...]
        out_last_ref[:, at : at + tokens] = part * last_ref[...]


def weigh(moe_in, router, named, pick, last):
    tokens = moe_in.shape[0]
    return pl.pallas_call(
        weigh_kernel,
        out_shape=[
            jax.ShapeDtypeStruct((pick.shape[0], 2 * tokens), jnp.bfloat16),
            jax.ShapeDtypeStruct((last.shape[0], 2 * tokens), jnp.bfloat16),
        ],
        compiler_params=pltpu.CompilerParams(vmem_limit_bytes=VMEM_MB * 1024 * 1024),
        name="weigh",
    )(moe_in, router, named, pick, last)


def fold(rows):
    count, features = rows.shape
    return rows.reshape(count, GROUP, features // GROUP).reshape(count * GROUP, features // GROUP)


def unfold(rows):
    count, piece = rows.shape
    return rows.reshape(count // GROUP, GROUP, piece).reshape(count // GROUP, GROUP * piece)


def fill(out_ref, x, pick, last):
    features = x.shape[1]
    out_ref[:, :features] = f32dot(pick, x).astype(jnp.bfloat16)
    out_ref[:, features:] = fold(f32dot(last, x).astype(jnp.bfloat16))


def finish_kernel(
    heads,
    size,
    features,
    parts_ref,
    w_ref,
    x_ref,
    gain_ref,
    pick_ref,
    last_ref,
    resid_ref,
    norm_ref,
    out_ref,
):
    @pl.when(pl.program_id(0) == 0)
    def _():
        summed = parts_ref[0].astype(jnp.float32)
        for c in range(1, parts_ref.shape[0]):
            summed = summed + parts_ref[c].astype(jnp.float32)
        base = heads * size
        attended = []
        for h in range(heads):
            at = base + 2 * h
            total = summed[:, at : at + 1] + summed[:, at + 1 : at + 2]
            attended.append((summed[:, h * size : (h + 1) * size] / total).astype(jnp.bfloat16))
        projected = f32dot(jnp.concatenate(attended, axis=1), w_ref[...])
        resid = x_ref[...].astype(jnp.float32) + projected
        resid_ref[...] = resid
        scale = lax.rsqrt(jnp.mean(resid * resid, axis=1, keepdims=True) + 1e-06)
        norm_ref[...] = (resid * scale * gain_ref[...].astype(jnp.float32)).astype(jnp.bfloat16)

    fill(out_ref, norm_ref[:, :features], pick_ref[...], last_ref[...])


def finish(parts, w_out, tokens, gain, pick, last, heads, size, features):
    rows, count = pick.shape[0], last.shape[0]
    wide = features + features // GROUP
    blocks = 4
    return pl.pallas_call(
        functools.partial(finish_kernel, heads, size, features),
        grid=(blocks,),
        in_specs=[
            whole_block(parts.shape),
            whole_block(w_out.shape),
            whole_block(tokens.shape),
            whole_block((1, gain.shape[0])),
            pl.BlockSpec((rows // blocks, pick.shape[1]), lambda i: (i, 0)),
            pl.BlockSpec((count // blocks, pick.shape[1]), lambda i: (i, 0)),
        ],
        out_specs=[
            pl.BlockSpec(tokens.shape, lambda i: (0, 0)),
            pl.BlockSpec(tokens.shape, lambda i: (0, 0)),
            pl.BlockSpec((rows // blocks, wide), lambda i: (i, 0)),
        ],
        out_shape=[
            jax.ShapeDtypeStruct(tokens.shape, jnp.float32),
            jax.ShapeDtypeStruct(tokens.shape, jnp.bfloat16),
            jax.ShapeDtypeStruct((rows, wide), jnp.bfloat16),
        ],
        compiler_params=params(),
        name="finish",
    )(parts, w_out, tokens, gain.reshape(1, -1), pick, last)


def dispatch_kernel(x_ref, pick_ref, last_ref, out_ref):
    fill(out_ref, x_ref[...], pick_ref[...], last_ref[...])


def dispatch(normed, pick, last, chunk, features):
    rows, tokens = pick.shape
    count = last.shape[0]
    wide = features + features // GROUP
    blocks = 4
    return pl.pallas_call(
        dispatch_kernel,
        grid=(blocks,),
        in_specs=[
            pl.BlockSpec((tokens, features), lambda i: (0, chunk)),
            pl.BlockSpec((rows // blocks, tokens), lambda i: (i, 0)),
            pl.BlockSpec((count // blocks, tokens), lambda i: (i, 0)),
        ],
        out_specs=pl.BlockSpec((rows // blocks, wide), lambda i: (i, 0)),
        out_shape=jax.ShapeDtypeStruct((rows, wide), jnp.bfloat16),
        compiler_params=params(),
        cost_estimate=pl.CostEstimate(
            flops=4 * rows * tokens * features, bytes_accessed=4 * rows * features, transcendentals=0
        ),
        name="dispatch",
    )(normed, pick, last)


def all_rows(x_ref, features):
    return jnp.concatenate([x_ref[:, :features], unfold(x_ref[:, features:])], axis=0)


def up_kernel(features, x_ref, w_ref, out_ref):
    out_ref[...] = f32dot(all_rows(x_ref, features), w_ref[0])


def up_first(received, weights, features):
    rows, wide = received.shape
    columns = weights.shape[2]
    blocks = 4
    taken = rows // blocks * (GROUP + 1) // GROUP
    return pl.pallas_call(
        functools.partial(up_kernel, features),
        grid=(blocks,),
        in_specs=[
            pl.BlockSpec((rows // blocks, wide), lambda i: (i, 0)),
            pl.BlockSpec(
                (1, features, columns), lambda i: (0, 0, 0), pipeline_mode=pl.Buffered(1)
            ),
        ],
        out_specs=pl.BlockSpec((taken, columns), lambda i: (i, 0)),
        out_shape=jax.ShapeDtypeStruct((taken * blocks, columns), jnp.float32),
        compiler_params=params(),
        cost_estimate=pl.CostEstimate(
            flops=2 * rows * features * columns, bytes_accessed=20000000, transcendentals=0
        ),
        name="up_first",
    )(received, weights)


def expert_kernel(
    features, x_ref, wu_ref, partial_ref, wd_hbm, out_ref, wd, arrived
):
    index = pl.program_id(0)
    copy = pltpu.make_async_copy(wd_hbm.at[0], wd, arrived)

    @pl.when(index == 0)
    def _():
        copy.start()

    gate_up = partial_ref[...] + f32dot(all_rows(x_ref, features), wu_ref[0])
    hidden = gate_up.shape[1] // 2
    gate = gate_up[:, :hidden]
    active = (gate / (1.0 + jnp.exp(-gate)) * gate_up[:, hidden:]).astype(jnp.bfloat16)

    @pl.when(index == 0)
    def _():
        copy.wait()

    rows = x_ref.shape[0]
    out = f32dot(active, wd[...])
    out_ref[:, : wd.shape[1]] = out[:rows].astype(jnp.bfloat16)
    out_ref[:, wd.shape[1] :] = fold(out[rows:].astype(jnp.bfloat16))


def expert(received, w_up, partial, w_down, features, chunk):
    rows, wide = received.shape
    columns = w_up.shape[2]
    hidden, width = w_down.shape[1:]
    blocks = 4
    taken = rows // blocks * (GROUP + 1) // GROUP
    out_wide = width + width // GROUP
    return pl.pallas_call(
        functools.partial(expert_kernel, features),
        grid=(blocks,),
        in_specs=[
            pl.BlockSpec((rows // blocks, wide), lambda i: (i, 0)),
            pl.BlockSpec(
                (1, features, columns), lambda i: (0, chunk, 0), pipeline_mode=pl.Buffered(1)
            ),
            pl.BlockSpec((taken, columns), lambda i: (i, 0)),
            pl.BlockSpec(memory_space=pl.ANY),
        ],
        out_specs=pl.BlockSpec((rows // blocks, out_wide), lambda i: (i, 0)),
        out_shape=jax.ShapeDtypeStruct((rows, out_wide), jnp.bfloat16),
        scratch_shapes=[pltpu.VMEM((hidden, width), jnp.bfloat16), pltpu.SemaphoreType.DMA(())],
        compiler_params=params(),
        cost_estimate=pl.CostEstimate(
            flops=2 * rows * (features * columns + hidden * width),
            bytes_accessed=30000000,
            transcendentals=0,
        ),
        name="expert",
    )(received, w_up, partial, w_down)


def combine_kernel(x_ref, w_ref, wlast_ref, resid_ref, out_ref, total, last):
    index = pl.program_id(0)
    tokens, features = resid_ref.shape
    lasts = x_ref.shape[0] // GROUP

    def weighted(weights, x):
        both = lax.dot_general(
            weights, x, (((0,), (0,)), ((), ())), preferred_element_type=jnp.float32
        )
        return both[:tokens] + both[tokens:]

    added = weighted(w_ref[...], x_ref[:, :features])
    last[pl.ds(pl.multiple_of(index * lasts, lasts), lasts), :] = unfold(x_ref[:, features:])

    @pl.when(index == 0)
    def _():
        total[...] = resid_ref[...] + added

    @pl.when(index > 0)
    def _():
        total[...] += added

    @pl.when(index == pl.num_programs(0) - 1)
    def _():
        out_ref[...] = (total[...] + weighted(wlast_ref[...], last[...])).astype(jnp.bfloat16)


def combine(returned, weights, last_weights, resid):
    rows, wide = returned.shape
    tokens, features = resid.shape
    count = last_weights.shape[0]
    blocks = 4
    return pl.pallas_call(
        combine_kernel,
        grid=(blocks,),
        in_specs=[
            pl.BlockSpec((rows // blocks, wide), lambda i: (i, 0)),
            pl.BlockSpec((rows // blocks, 2 * tokens), lambda i: (i, 0)),
            whole_block((count, 2 * tokens)),
            whole_block((tokens, features)),
        ],
        out_specs=pl.BlockSpec((tokens, features), lambda i: (0, 0)),
        out_shape=jax.ShapeDtypeStruct((tokens, features), jnp.bfloat16),
        scratch_shapes=[
            pltpu.VMEM((tokens, features), jnp.float32),
            pltpu.VMEM((count, features), jnp.bfloat16),
        ],
        compiler_params=params(),
        name="combine",
    )(returned, weights, last_weights, resid)


def on_device(
    tokens,
    block_order,
    attn_gain,
    query_gain,
    key_gain,
    w_qkv,
    w_out,
    moe_gain,
    router,
    routes,
    w_gate_up,
    w_down,
):
    rows, model_width = tokens.shape
    size = query_gain.shape[0]
    ctx_size, exp_size = lax.axis_size("ctx"), lax.axis_size("exp")
    ctx_at, exp_at = lax.axis_index("ctx"), lax.axis_index("exp")
    ring = 4
    inner = exp_size // ring
    x_at, z_lo = ctx_at % ring, ctx_at // ring
    y_at, z_hi, core = exp_at // inner, exp_at // 2 % 2, exp_at % 2

    def from_exp(x, source):
        return lax.ppermute(x, "exp", [(source(i), i) for i in range(exp_size)])

    def from_ctx(x, source):
        return lax.ppermute(x, "ctx", [(source(i), i) for i in range(ctx_size)])

    def exp_pair(x):
        return jnp.stack([x, from_exp(x, lambda i: i ^ 2)])

    def exp_line(pair):
        return jnp.concatenate(
            [pair]
            + [from_exp(pair, lambda i, k=k: (i - k * inner) % exp_size) for k in range(1, ring)]
        )

    def other_core(line):
        return from_exp(line, lambda i: i ^ 1)

    def ctx_pair(x):
        return jnp.stack([x, from_ctx(x, lambda i: i ^ ring)])

    def ctx_line(pair):
        return [pair] + [
            from_ctx(pair, lambda i, k=k: i // ring * ring + (i - k) % ring)
            for k in range(1, ring)
        ]

    relative = jnp.arange(exp_size, dtype=jnp.int32)
    exp_blocks = (
        (y_at - relative // 2 % ring) % ring * inner
        + (z_hi + relative % 2) % 2 * 2
        + (core + relative // (2 * ring)) % 2
    )
    piece_of = (
        (core + relative) % 2 * (2 * ring)
        + (y_at - relative // inner) % ring * 2
        + (z_hi + relative // 2) % 2
    )
    near = jnp.arange(ctx_size, dtype=jnp.int32)
    ctx_blocks = (z_lo + near) % 2 * ring + (x_at - near // 2) % ring

    def block_numbers(devices):
        every = jnp.arange(block_order.shape[0], dtype=jnp.int32)
        return jnp.sum(
            jnp.where(devices[:, None] == every[None, :], block_order[None, :], 0), axis=1
        )

    k_blocks = block_numbers(ctx_at * exp_size + exp_blocks)
    q_blocks = block_numbers(ctx_blocks * exp_size + exp_at)
    own_pos = q_blocks[0] * rows + jnp.arange(rows, dtype=jnp.int32)
    hide = jnp.repeat(
        jnp.where(k_blocks[:, None] > q_blocks[None, :], HIDDEN, 0.0), rows, axis=0
    )
    hide = jnp.pad(hide, ((0, 0), (0, size - ctx_size))).astype(jnp.bfloat16)

    depth = model_width // ctx_size
    widened = tokens.astype(jnp.float32)
    row_scale = lax.rsqrt(jnp.mean(widened * widened, axis=1, keepdims=True) + 1e-06)
    gained = (widened * attn_gain.astype(jnp.float32)).astype(jnp.bfloat16)
    gained = jnp.transpose(gained.reshape(rows, ctx_size, depth), (1, 0, 2))
    w_share = lax.dynamic_slice_in_dim(w_qkv.T, ctx_at * depth, depth, 1)
    gained, w_share = lax.optimization_barrier((gained, w_share))
    near = exp_line(exp_pair(w_share))
    far = other_core(near)
    w_out, near = lax.optimization_barrier((w_out, near))
    w_out_all = lax.all_gather(w_out, "exp", axis=0, tiled=True)

    def swap_ctx(x):
        return lax.all_to_all(x, "ctx", split_axis=0, concat_axis=0, tiled=True)

    shares = swap_ctx(gained).reshape(ctx_size * rows, depth)
    shares = project(shares, near, far, piece_of).reshape(ctx_size, rows, -1)
    shares, routes = lax.optimization_barrier((shares, routes))
    count = router.shape[1]
    pick, pick_last, named = slots(routes.T, count)
    mixed = swap_ctx(shares)
    mixed, pick, pick_last, named, hide = lax.optimization_barrier(
        (mixed, pick, pick_last, named, hide)
    )
    mixed = jnp.sum(mixed.astype(jnp.float32), axis=0) * row_scale
    heads = mixed.shape[1] // size - 2
    queries = mixed[:, : heads * size].reshape(rows, heads, size)
    queries = (
        (
            rotate(rms_scale(queries, query_gain), own_pos[:, None].astype(jnp.float32))
            * (math.log2(math.e) / math.sqrt(size))
        )
        .astype(jnp.bfloat16)
        .reshape(rows, heads * size)
    )
    keys = rotate(
        rms_scale(mixed[:, heads * size : (heads + 1) * size], key_gain),
        own_pos.astype(jnp.float32),
    ).astype(jnp.bfloat16)
    values = mixed[:, (heads + 1) * size :].astype(jnp.bfloat16)
    key_values = jnp.concatenate([keys, values], axis=1)

    queries, key_values = lax.optimization_barrier((queries, key_values))
    queries, key_values = lax.optimization_barrier((ctx_pair(queries), exp_pair(key_values)))
    key_values, queries = exp_line(key_values), ctx_line(queries)
    near = key_values.reshape(-1, 2 * size)
    far = other_core(near)
    parts = attend(queries, near, far, hide, ctx_blocks, heads, size)
    main = model_width // 4 * 3
    rest = model_width - main
    resid, moe_in, outgoing = finish(
        swap_ctx(parts), w_out_all, tokens, moe_gain, pick, pick_last, heads, size, main
    )

    def exchange(x):
        wide = x.shape[1]
        x = lax.all_to_all(
            x.reshape(count, GROUP, wide), ("ctx", "exp"), split_axis=0, concat_axis=0, tiled=True
        )
        return x.reshape(count * GROUP, wide)

    first = exchange(outgoing)
    second = exchange(dispatch(moe_in, pick, pick_last, main // rest, rest))
    first, moe_in = lax.optimization_barrier((first, moe_in))
    weights, last_weights = weigh(moe_in, router, named, pick, pick_last)
    partial = up_first(first, w_gate_up, main)
    returned = exchange(expert(second, w_gate_up, partial, w_down, rest, main // rest))
    return combine(returned, weights, last_weights, resid)


def solution(mesh):
    return jax.shard_map(
        on_device,
        mesh=mesh,
        in_specs=(
            P(("ctx", "exp"), None),
            P(),
            P(),
            P(),
            P(),
            P(None, "exp"),
            P("exp", None),
            P(),
            P(),
            P(("ctx", "exp"), None),
            P(("ctx", "exp"), None, None),
            P(("ctx", "exp"), None, None),
        ),
        out_specs=P(("ctx", "exp"), None),
        check_vma=False,
    )
```

```python
import functools
import math

import jax
import jax.numpy as jnp
from jax import lax
from jax.experimental import pallas as pl
from jax.experimental.pallas import tpu as pltpu
from jax.sharding import PartitionSpec as P

rope_base = 1000000.0
GROUP = 8
VMEM_MB = 58
HIDDEN = -30000.0


def rms_scale(values, gain):
    widened = values.astype(jnp.float32)
    return (
        widened
        * lax.rsqrt(jnp.mean(widened * widened, axis=-1, keepdims=True) + 1e-06)
        * gain.astype(jnp.float32)
    )


def rotate(values, positions):
    half = values.shape[-1] // 2
    freqs = jnp.exp(
        -math.log(rope_base) * jnp.arange(half, dtype=jnp.float32) * 2.0 / values.shape[-1]
    )
    angles = positions[..., None] * freqs
    first = values[..., :half]
    second = values[..., half:]
    return jnp.concatenate(
        [
            first * jnp.cos(angles) - second * jnp.sin(angles),
            second * jnp.cos(angles) + first * jnp.sin(angles),
        ],
        axis=-1,
    )


def params(axes=1):
    return pltpu.CompilerParams(
        vmem_limit_bytes=VMEM_MB * 1024 * 1024, dimension_semantics=("arbitrary",) * axes
    )


def f32dot(a, b):
    return jnp.dot(a, b, preferred_element_type=jnp.float32)


def whole_block(shape):
    zeros = (0,) * len(shape)
    return pl.BlockSpec(shape, lambda *_: zeros, pipeline_mode=pl.Buffered(1))


def project_kernel(order_ref, *refs):
    ring = (len(refs) - 3) // 2
    x_refs, (near_ref, far_ref), out_refs, whole = (
        refs[:ring],
        refs[ring : ring + 2],
        refs[ring + 2 : -1],
        refs[-1],
    )
    half, columns = near_ref.shape[:2]
    rows = x_refs[0].shape[0]
    for e in range(2 * half):
        at = order_ref[e]
        near = near_ref[lax.rem(at, half)].astype(jnp.float32)
        far = far_ref[lax.rem(at, half)].astype(jnp.float32)
        whole[e * columns : (e + 1) * columns, :] = jnp.where(at < half, near, far).astype(
            jnp.bfloat16
        )
    x = jnp.concatenate([ref[...] for ref in x_refs], axis=0)
    out = lax.dot_general(
        x, whole[...], (((1,), (1,)), ((), ())), preferred_element_type=jnp.float32
    ).astype(jnp.bfloat16)
    for at, ref in enumerate(out_refs):
        ref[...] = out[at * rows : (at + 1) * rows]


def project(shares, near, far, order):
    rows, depth = shares[0].shape
    half, columns = near.shape[:2]
    out = jax.ShapeDtypeStruct((rows, 2 * half * columns), jnp.bfloat16)
    return pl.pallas_call(
        project_kernel,
        grid_spec=pltpu.PrefetchScalarGridSpec(
            num_scalar_prefetch=1,
            grid=(1,),
            in_specs=[whole_block(x.shape) for x in (*shares, near, far)],
            out_specs=[whole_block(out.shape)] * len(shares),
            scratch_shapes=[pltpu.VMEM((2 * half * columns, depth), jnp.bfloat16)],
        ),
        out_shape=[out] * len(shares),
        compiler_params=params(),
        name="project",
    )(order, *shares, near, far)


def attend_kernel(heads, size, width, ring, *refs):
    q_refs, (near_ref, far_ref, hide_ref), out_refs, (held, keys, values) = (
        refs[:ring],
        refs[ring : ring + 3],
        refs[ring + 3 : -3],
        refs[-3:],
    )
    index = pl.program_id(0)
    rows = q_refs[0].shape[0]
    half = near_ref.shape[0]
    length = 2 * half

    @pl.when(index == 0)
    def _():
        for at, ref in enumerate(q_refs):
            held[at] = ref[...]
        for at, ref in ((0, near_ref), (half, far_ref)):
            keys[at : at + half, :size] = ref[:, :size]
            values[at : at + half, :size] = ref[:, size:]
        keys[:, size:] = hide_ref[...]
        values[:, size:] = jnp.ones((length, size), jnp.bfloat16)

    mark = lax.broadcasted_iota(jnp.int32, (rows, size), 1) == index
    mark = jnp.where(mark, 1.0, 0.0).astype(jnp.bfloat16)
    row = lax.broadcasted_iota(jnp.int32, (rows, width), 0)
    key = lax.broadcasted_iota(jnp.int32, (rows, width), 1)
    later = (key > row) & (key < rows) & (index == 0)
    lane = lax.broadcasted_iota(jnp.int32, (rows, size), 1)
    sums = jnp.zeros((rows, size), jnp.float32)
    results = []
    for h in range(heads):
        q = jnp.concatenate([held[index, :, h * size : (h + 1) * size], mark], axis=1)
        total = jnp.zeros((rows, 2 * size), jnp.float32)
        for start in range(0, length, width):
            part = pl.ds(start, width)
            scores = lax.dot_general(
                q, keys[part, :], (((1,), (1,)), ((), ())), preferred_element_type=jnp.float32
            )
            if start == 0:
                scores = jnp.where(later, HIDDEN, scores)
            total = total + f32dot(jnp.exp2(scores).astype(jnp.bfloat16), values[part, :])
        results.append(total[:, :size].astype(jnp.bfloat16))
        high = total[:, size:].astype(jnp.bfloat16).astype(jnp.float32)
        sums = jnp.where(lane == 2 * h, high, sums)
        sums = jnp.where(lane == 2 * h + 1, total[:, size:] - high, sums)
    packed = jnp.concatenate([*results, sums.astype(jnp.bfloat16)], axis=1)
    for at, ref in enumerate(out_refs):

        @pl.when(index == at)
        def _(ref=ref):
            ref[...] = packed


def attend(queries, near, far, hide, heads, size):
    rows, columns = queries[0].shape
    ring = len(queries)
    length = 2 * near.shape[0]
    out = jax.ShapeDtypeStruct((rows, columns + size), jnp.bfloat16)
    return pl.pallas_call(
        functools.partial(attend_kernel, heads, size, 512, ring),
        grid=(ring,),
        in_specs=[whole_block(x.shape) for x in (*queries, near, far, hide)],
        out_specs=[whole_block(out.shape)] * ring,
        scratch_shapes=[
            pltpu.VMEM((ring, rows, columns), jnp.bfloat16),
            pltpu.VMEM((length, 2 * size), jnp.bfloat16),
            pltpu.VMEM((length, 2 * size), jnp.bfloat16),
        ],
        out_shape=[out] * ring,
        compiler_params=params(),
        name="attend",
    )(*queries, near, far, hide)


def repeat_rows(values):
    rows = values.shape[0]
    row = lax.broadcasted_iota(jnp.int32, (rows * GROUP, rows), 0)
    column = lax.broadcasted_iota(jnp.int32, (rows * GROUP, rows), 1)
    copies = (lax.div(row, GROUP) == column).astype(jnp.bfloat16)
    return f32dot(copies, values)


def slots_kernel(routes_ref, pick_ref, last_ref, named_ref):
    fanout, tokens = routes_ref.shape
    count = named_ref.shape[0]
    expert = lax.broadcasted_iota(jnp.int32, (count, tokens), 0)
    named = jnp.zeros((count, tokens), jnp.float32)
    for j in range(fanout):
        named = named + jnp.where(routes_ref[j : j + 1, :] == expert, 1.0, 0.0)
    earlier = lax.broadcasted_iota(jnp.int32, (tokens, tokens), 0)
    later = lax.broadcasted_iota(jnp.int32, (tokens, tokens), 1)
    before = (earlier < later).astype(jnp.bfloat16)
    rank = f32dot(named.astype(jnp.bfloat16), before)
    code = named * (rank + 1.0)
    named_ref[...] = named
    last_ref[...] = (code == GROUP + 1.0).astype(jnp.bfloat16)
    spread = repeat_rows(code.astype(jnp.bfloat16))
    slot = lax.rem(lax.broadcasted_iota(jnp.int32, spread.shape, 0), GROUP) + 1
    pick_ref[...] = (spread == slot.astype(jnp.float32)).astype(jnp.bfloat16)


def slots(routes_t, count):
    fanout, tokens = routes_t.shape
    return pl.pallas_call(
        slots_kernel,
        out_shape=[
            jax.ShapeDtypeStruct((count * GROUP, tokens), jnp.bfloat16),
            jax.ShapeDtypeStruct((count, tokens), jnp.bfloat16),
            jax.ShapeDtypeStruct((count, tokens), jnp.float32),
        ],
        compiler_params=pltpu.CompilerParams(vmem_limit_bytes=VMEM_MB * 1024 * 1024),
        name="slots",
    )(routes_t)


def weigh_kernel(x_ref, router_ref, named_ref, pick_ref, last_ref, out_ref, out_last_ref):
    tokens = x_ref.shape[0]
    logits = lax.dot_general(
        router_ref[...], x_ref[...], (((0,), (1,)), ((), ())), preferred_element_type=jnp.float32
    )
    named = named_ref[...] > 0.5
    largest = jnp.max(jnp.where(named, logits, -jnp.inf), axis=0, keepdims=True)
    shares = jnp.where(named, jnp.exp(jnp.minimum(logits - largest, 0.0)), 0.0)
    shares = shares / jnp.sum(shares, axis=0, keepdims=True)
    high = shares.astype(jnp.bfloat16)
    low = (shares - high.astype(jnp.float32)).astype(jnp.bfloat16)
    for at, part in ((0, high), (tokens, low)):
        out_ref[:, at : at + tokens] = repeat_rows(part).astype(jnp.bfloat16) * pick_ref[...]
        out_last_ref[:, at : at + tokens] = part * last_ref[...]


def weigh(moe_in, router, named, pick, last):
    tokens = moe_in.shape[0]
    return pl.pallas_call(
        weigh_kernel,
        out_shape=[
            jax.ShapeDtypeStruct((pick.shape[0], 2 * tokens), jnp.bfloat16),
            jax.ShapeDtypeStruct((last.shape[0], 2 * tokens), jnp.bfloat16),
        ],
        compiler_params=pltpu.CompilerParams(vmem_limit_bytes=VMEM_MB * 1024 * 1024),
        name="weigh",
    )(moe_in, router, named, pick, last)


def fold(rows):
    count, features = rows.shape
    return rows.reshape(count, GROUP, features // GROUP).reshape(count * GROUP, features // GROUP)


def unfold(rows):
    count, piece = rows.shape
    return rows.reshape(count // GROUP, GROUP, piece).reshape(count // GROUP, GROUP * piece)


def fill(out_ref, x, pick, last):
    features = x.shape[1]
    out_ref[:, :features] = f32dot(pick, x).astype(jnp.bfloat16)
    out_ref[:, features:] = fold(f32dot(last, x).astype(jnp.bfloat16))


def finish_kernel(
    heads,
    size,
    features,
    *refs,
):
    parts_refs, refs = refs[:-8], refs[-8:]
    w_ref, x_ref, gain_ref, pick_ref, last_ref, resid_ref, norm_ref, out_ref = refs

    @pl.when(pl.program_id(0) == 0)
    def _():
        summed = parts_refs[0][...].astype(jnp.float32)
        for ref in parts_refs[1:]:
            summed = summed + ref[...].astype(jnp.float32)
        base = heads * size
        attended = []
        for h in range(heads):
            at = base + 2 * h
            total = summed[:, at : at + 1] + summed[:, at + 1 : at + 2]
            attended.append((summed[:, h * size : (h + 1) * size] / total).astype(jnp.bfloat16))
        projected = f32dot(jnp.concatenate(attended, axis=1), w_ref[...])
        resid = x_ref[...].astype(jnp.float32) + projected
        resid_ref[...] = resid
        scale = lax.rsqrt(jnp.mean(resid * resid, axis=1, keepdims=True) + 1e-06)
        norm_ref[...] = (resid * scale * gain_ref[...].astype(jnp.float32)).astype(jnp.bfloat16)

    fill(out_ref, norm_ref[:, :features], pick_ref[...], last_ref[...])


def finish(parts, w_out, tokens, gain, pick, last, heads, size, features):
    rows, count = pick.shape[0], last.shape[0]
    wide = features + features // GROUP
    blocks = 4
    return pl.pallas_call(
        functools.partial(finish_kernel, heads, size, features),
        grid=(blocks,),
        in_specs=[
            *(whole_block(x.shape) for x in parts),
            whole_block(w_out.shape),
            whole_block(tokens.shape),
            whole_block((1, gain.shape[0])),
            pl.BlockSpec((rows // blocks, pick.shape[1]), lambda i: (i, 0)),
            pl.BlockSpec((count // blocks, pick.shape[1]), lambda i: (i, 0)),
        ],
        out_specs=[
            pl.BlockSpec(tokens.shape, lambda i: (0, 0)),
            pl.BlockSpec(tokens.shape, lambda i: (0, 0)),
            pl.BlockSpec((rows // blocks, wide), lambda i: (i, 0)),
        ],
        out_shape=[
            jax.ShapeDtypeStruct(tokens.shape, jnp.float32),
            jax.ShapeDtypeStruct(tokens.shape, jnp.bfloat16),
            jax.ShapeDtypeStruct((rows, wide), jnp.bfloat16),
        ],
        compiler_params=params(),
        name="finish",
    )(*parts, w_out, tokens, gain.reshape(1, -1), pick, last)


def dispatch_kernel(x_ref, pick_ref, last_ref, out_ref):
    fill(out_ref, x_ref[...], pick_ref[...], last_ref[...])


def dispatch(normed, pick, last, chunk, features):
    rows, tokens = pick.shape
    count = last.shape[0]
    wide = features + features // GROUP
    blocks = 4
    return pl.pallas_call(
        dispatch_kernel,
        grid=(blocks,),
        in_specs=[
            pl.BlockSpec((tokens, features), lambda i: (0, chunk)),
            pl.BlockSpec((rows // blocks, tokens), lambda i: (i, 0)),
            pl.BlockSpec((count // blocks, tokens), lambda i: (i, 0)),
        ],
        out_specs=pl.BlockSpec((rows // blocks, wide), lambda i: (i, 0)),
        out_shape=jax.ShapeDtypeStruct((rows, wide), jnp.bfloat16),
        compiler_params=params(),
        cost_estimate=pl.CostEstimate(
            flops=4 * rows * tokens * features, bytes_accessed=4 * rows * features, transcendentals=0
        ),
        name="dispatch",
    )(normed, pick, last)


def all_rows(x_ref, features):
    return jnp.concatenate([x_ref[:, :features], unfold(x_ref[:, features:])], axis=0)


def up_kernel(features, x_ref, w_ref, out_ref):
    out_ref[...] = f32dot(all_rows(x_ref, features), w_ref[0])


def up_first(received, weights, features):
    rows, wide = received.shape
    columns = weights.shape[2]
    blocks = 4
    taken = rows // blocks * (GROUP + 1) // GROUP
    return pl.pallas_call(
        functools.partial(up_kernel, features),
        grid=(blocks,),
        in_specs=[
            pl.BlockSpec((rows // blocks, wide), lambda i: (i, 0)),
            pl.BlockSpec(
                (1, features, columns), lambda i: (0, 0, 0), pipeline_mode=pl.Buffered(1)
            ),
        ],
        out_specs=pl.BlockSpec((taken, columns), lambda i: (i, 0)),
        out_shape=jax.ShapeDtypeStruct((taken * blocks, columns), jnp.float32),
        compiler_params=params(),
        cost_estimate=pl.CostEstimate(
            flops=2 * rows * features * columns, bytes_accessed=20000000, transcendentals=0
        ),
        name="up_first",
    )(received, weights)


def expert_kernel(
    features, x_ref, wu_ref, partial_ref, wd_hbm, out_ref, wd, arrived
):
    index = pl.program_id(0)
    copy = pltpu.make_async_copy(wd_hbm.at[0], wd, arrived)

    @pl.when(index == 0)
    def _():
        copy.start()

    gate_up = partial_ref[...] + f32dot(all_rows(x_ref, features), wu_ref[0])
    hidden = gate_up.shape[1] // 2
    gate = gate_up[:, :hidden]
    active = (gate / (1.0 + jnp.exp(-gate)) * gate_up[:, hidden:]).astype(jnp.bfloat16)

    @pl.when(index == 0)
    def _():
        copy.wait()

    rows = x_ref.shape[0]
    out = f32dot(active, wd[...])
    out_ref[:, : wd.shape[1]] = out[:rows].astype(jnp.bfloat16)
    out_ref[:, wd.shape[1] :] = fold(out[rows:].astype(jnp.bfloat16))


def expert(received, w_up, partial, w_down, features, chunk):
    rows, wide = received.shape
    columns = w_up.shape[2]
    hidden, width = w_down.shape[1:]
    blocks = 4
    taken = rows // blocks * (GROUP + 1) // GROUP
    out_wide = width + width // GROUP
    return pl.pallas_call(
        functools.partial(expert_kernel, features),
        grid=(blocks,),
        in_specs=[
            pl.BlockSpec((rows // blocks, wide), lambda i: (i, 0)),
            pl.BlockSpec(
                (1, features, columns), lambda i: (0, chunk, 0), pipeline_mode=pl.Buffered(1)
            ),
            pl.BlockSpec((taken, columns), lambda i: (i, 0)),
            pl.BlockSpec(memory_space=pl.ANY),
        ],
        out_specs=pl.BlockSpec((rows // blocks, out_wide), lambda i: (i, 0)),
        out_shape=jax.ShapeDtypeStruct((rows, out_wide), jnp.bfloat16),
        scratch_shapes=[pltpu.VMEM((hidden, width), jnp.bfloat16), pltpu.SemaphoreType.DMA(())],
        compiler_params=params(),
        cost_estimate=pl.CostEstimate(
            flops=2 * rows * (features * columns + hidden * width),
            bytes_accessed=30000000,
            transcendentals=0,
        ),
        name="expert",
    )(received, w_up, partial, w_down)


def combine_kernel(x_ref, w_ref, wlast_ref, resid_ref, out_ref, total, last):
    index = pl.program_id(0)
    tokens, features = resid_ref.shape
    lasts = x_ref.shape[0] // GROUP

    def weighted(weights, x):
        both = lax.dot_general(
            weights, x, (((0,), (0,)), ((), ())), preferred_element_type=jnp.float32
        )
        return both[:tokens] + both[tokens:]

    added = weighted(w_ref[...], x_ref[:, :features])
    last[pl.ds(pl.multiple_of(index * lasts, lasts), lasts), :] = unfold(x_ref[:, features:])

    @pl.when(index == 0)
    def _():
        total[...] = resid_ref[...] + added

    @pl.when(index > 0)
    def _():
        total[...] += added

    @pl.when(index == pl.num_programs(0) - 1)
    def _():
        out_ref[...] = (total[...] + weighted(wlast_ref[...], last[...])).astype(jnp.bfloat16)


def combine(returned, weights, last_weights, resid):
    rows, wide = returned.shape
    tokens, features = resid.shape
    count = last_weights.shape[0]
    blocks = 4
    return pl.pallas_call(
        combine_kernel,
        grid=(blocks,),
        in_specs=[
            pl.BlockSpec((rows // blocks, wide), lambda i: (i, 0)),
            pl.BlockSpec((rows // blocks, 2 * tokens), lambda i: (i, 0)),
            whole_block((count, 2 * tokens)),
            whole_block((tokens, features)),
        ],
        out_specs=pl.BlockSpec((tokens, features), lambda i: (0, 0)),
        out_shape=jax.ShapeDtypeStruct((tokens, features), jnp.bfloat16),
        scratch_shapes=[
            pltpu.VMEM((tokens, features), jnp.float32),
            pltpu.VMEM((count, features), jnp.bfloat16),
        ],
        compiler_params=params(),
        name="combine",
    )(returned, weights, last_weights, resid)


def on_device(
    tokens,
    block_order,
    attn_gain,
    query_gain,
    key_gain,
    w_qkv,
    w_out,
    moe_gain,
    router,
    routes,
    w_gate_up,
    w_down,
):
    rows, model_width = tokens.shape
    size = query_gain.shape[0]
    ctx_size, exp_size = lax.axis_size("ctx"), lax.axis_size("exp")
    ctx_at, exp_at = lax.axis_index("ctx"), lax.axis_index("exp")
    ring = 4
    inner = exp_size // ring
    x_at, z_lo = ctx_at % ring, ctx_at // ring
    y_at, z_hi, core = exp_at // inner, exp_at // 2 % 2, exp_at % 2

    def device(z_lo, x, y, z_hi, core):
        return (z_lo * ring + x) * exp_size + y * inner + z_hi * 2 + core

    def bring(value, z_lo=0, x=0, y=0, z_hi=0, core=0):
        pairs = []
        for at in range(ctx_size * exp_size):
            c, e = at // exp_size, at % exp_size
            source = device(
                c // ring ^ z_lo,
                (c - x) % ring,
                (e // inner - y) % ring,
                e // 2 % 2 ^ z_hi,
                e % 2 ^ core,
            )
            pairs.append((source, at))
        return lax.ppermute(value, ("ctx", "exp"), pairs)

    def along_y(value):
        return jnp.concatenate([value] + [bring(value, y=k) for k in range(1, ring)])

    def along_x(values, step):
        return [values[0]] + [bring(values[k], x=step * k) for k in range(1, ring)]

    relative = jnp.arange(exp_size, dtype=jnp.int32)
    piece_of = (
        (core + relative) % 2 * (2 * ring)
        + (y_at - relative // inner) % ring * 2
        + (z_hi + relative // 2) % 2
    )
    relative = jnp.arange(2 * exp_size, dtype=jnp.int32)
    key_devices = device(
        (z_lo + relative) % 2,
        x_at,
        (y_at - relative // 4) % ring,
        (z_hi + relative // 2) % 2,
        (core + relative // (4 * ring)) % 2,
    )
    steps = jnp.arange(ring, dtype=jnp.int32)
    query_devices = device(z_lo, (x_at - steps) % ring, y_at, z_hi, core)

    def block_numbers(devices):
        every = jnp.arange(block_order.shape[0], dtype=jnp.int32)
        return jnp.sum(
            jnp.where(devices[:, None] == every[None, :], block_order[None, :], 0), axis=1
        )

    k_blocks = block_numbers(key_devices)
    q_blocks = block_numbers(query_devices)
    own_pos = q_blocks[0] * rows + jnp.arange(rows, dtype=jnp.int32)
    hide = jnp.repeat(
        jnp.where(k_blocks[:, None] > q_blocks[None, :], HIDDEN, 0.0), rows, axis=0
    )
    hide = jnp.pad(hide, ((0, 0), (0, size - ring))).astype(jnp.bfloat16)

    depth = model_width // ring
    widened = tokens.astype(jnp.float32)
    row_scale = lax.rsqrt(jnp.mean(widened * widened, axis=1, keepdims=True) + 1e-06)
    gained = (widened * attn_gain.astype(jnp.float32)).astype(jnp.bfloat16)
    w_share = lax.dynamic_slice_in_dim(w_qkv.T, x_at * depth, depth, 1)
    near = along_y(jnp.stack([w_share, bring(w_share, z_hi=1)]))
    far = bring(near, core=1)
    w_out, near = lax.optimization_barrier((w_out, near))
    w_out_all = lax.all_gather(w_out, "exp", axis=0, tiled=True)
    shares = along_x(
        [
            lax.dynamic_slice_in_dim(gained, (x_at + k) % ring * depth, depth, 1)
            for k in range(ring)
        ],
        1,
    )
    shares = project(shares, near, far, piece_of)
    shares, routes = lax.optimization_barrier((shares, routes))
    count = router.shape[1]
    pick, pick_last, named = slots(routes.T, count)
    mixed = sum(x.astype(jnp.float32) for x in along_x(shares, -1)) * row_scale
    mixed, pick, pick_last, named, hide = lax.optimization_barrier(
        (mixed, pick, pick_last, named, hide)
    )
    heads = mixed.shape[1] // size - 2
    queries = mixed[:, : heads * size].reshape(rows, heads, size)
    queries = (
        (
            rotate(rms_scale(queries, query_gain), own_pos[:, None].astype(jnp.float32))
            * (math.log2(math.e) / math.sqrt(size))
        )
        .astype(jnp.bfloat16)
        .reshape(rows, heads * size)
    )
    keys = rotate(
        rms_scale(mixed[:, heads * size : (heads + 1) * size], key_gain),
        own_pos.astype(jnp.float32),
    ).astype(jnp.bfloat16)
    values = mixed[:, (heads + 1) * size :].astype(jnp.bfloat16)
    key_values = jnp.concatenate([keys, values], axis=1)

    near = along_y(
        jnp.stack(
            [
                key_values,
                bring(key_values, z_lo=1),
                bring(key_values, z_hi=1),
                bring(key_values, z_lo=1, z_hi=1),
            ]
        )
    ).reshape(-1, 2 * size)
    far = bring(near, core=1)
    parts = along_x(attend(along_x([queries] * ring, 1), near, far, hide, heads, size), -1)
    main = model_width // 4 * 3
    rest = model_width - main
    resid, moe_in, outgoing = finish(
        parts, w_out_all, tokens, moe_gain, pick, pick_last, heads, size, main
    )

    def exchange(x):
        wide = x.shape[1]
        x = lax.all_to_all(
            x.reshape(count, GROUP, wide), ("ctx", "exp"), split_axis=0, concat_axis=0, tiled=True
        )
        return x.reshape(count * GROUP, wide)

    first = exchange(outgoing)
    second = exchange(dispatch(moe_in, pick, pick_last, main // rest, rest))
    first, moe_in = lax.optimization_barrier((first, moe_in))
    weights, last_weights = weigh(moe_in, router, named, pick, pick_last)
    partial = up_first(first, w_gate_up, main)
    returned = exchange(expert(second, w_gate_up, partial, w_down, rest, main // rest))
    return combine(returned, weights, last_weights, resid)


def solution(mesh):
    return jax.shard_map(
        on_device,
        mesh=mesh,
        in_specs=(
            P(("ctx", "exp"), None),
            P(),
            P(),
            P(),
            P(),
            P(None, "exp"),
            P("exp", None),
            P(),
            P(),
            P(("ctx", "exp"), None),
            P(("ctx", "exp"), None, None),
            P(("ctx", "exp"), None, None),
        ),
        out_specs=P(("ctx", "exp"), None),
        check_vma=False,
    )
```

```python
import functools
import math

import jax
import jax.numpy as jnp
from jax import lax
from jax.experimental import pallas as pl
from jax.experimental.pallas import tpu as pltpu
from jax.sharding import PartitionSpec as P

rope_base = 1000000.0
GROUP = 8
VMEM_MB = 58
HIDDEN = -30000.0


def rms_scale(values, gain):
    widened = values.astype(jnp.float32)
    return (
        widened
        * lax.rsqrt(jnp.mean(widened * widened, axis=-1, keepdims=True) + 1e-06)
        * gain.astype(jnp.float32)
    )


def rotate(values, positions):
    half = values.shape[-1] // 2
    freqs = jnp.exp(
        -math.log(rope_base) * jnp.arange(half, dtype=jnp.float32) * 2.0 / values.shape[-1]
    )
    angles = positions[..., None] * freqs
    first = values[..., :half]
    second = values[..., half:]
    return jnp.concatenate(
        [
            first * jnp.cos(angles) - second * jnp.sin(angles),
            second * jnp.cos(angles) + first * jnp.sin(angles),
        ],
        axis=-1,
    )


def params(axes=1):
    return pltpu.CompilerParams(
        vmem_limit_bytes=VMEM_MB * 1024 * 1024, dimension_semantics=("arbitrary",) * axes
    )


def f32dot(a, b):
    return jnp.dot(a, b, preferred_element_type=jnp.float32)


def whole_block(shape):
    zeros = (0,) * len(shape)
    return pl.BlockSpec(shape, lambda *_: zeros, pipeline_mode=pl.Buffered(1))


def project_kernel(order_ref, *refs):
    ring = (len(refs) - 3) // 2
    x_refs, (near_ref, far_ref), out_refs, whole = (
        refs[:ring],
        refs[ring : ring + 2],
        refs[ring + 2 : -1],
        refs[-1],
    )
    half, columns = near_ref.shape[:2]
    rows = x_refs[0].shape[0]
    for e in range(2 * half):
        at = order_ref[e]
        near = near_ref[lax.rem(at, half)].astype(jnp.float32)
        far = far_ref[lax.rem(at, half)].astype(jnp.float32)
        whole[e * columns : (e + 1) * columns, :] = jnp.where(at < half, near, far).astype(
            jnp.bfloat16
        )
    x = jnp.concatenate([ref[...] for ref in x_refs], axis=0)
    out = lax.dot_general(
        x, whole[...], (((1,), (1,)), ((), ())), preferred_element_type=jnp.float32
    ).astype(jnp.bfloat16)
    for at, ref in enumerate(out_refs):
        ref[...] = out[at * rows : (at + 1) * rows]


def project(shares, near, far, order):
    rows, depth = shares[0].shape
    half, columns = near.shape[:2]
    out = jax.ShapeDtypeStruct((rows, 2 * half * columns), jnp.bfloat16)
    return pl.pallas_call(
        project_kernel,
        grid_spec=pltpu.PrefetchScalarGridSpec(
            num_scalar_prefetch=1,
            grid=(1,),
            in_specs=[whole_block(x.shape) for x in (*shares, near, far)],
            out_specs=[whole_block(out.shape)] * len(shares),
            scratch_shapes=[pltpu.VMEM((2 * half * columns, depth), jnp.bfloat16)],
        ),
        out_shape=[out] * len(shares),
        compiler_params=params(),
        name="project",
    )(order, *shares, near, far)


def attend_kernel(heads, size, width, ring, *refs):
    q_refs, (near_ref, far_ref, hide_ref), out_refs, (held, keys, values) = (
        refs[:ring],
        refs[ring : ring + 3],
        refs[ring + 3 : -3],
        refs[-3:],
    )
    index = pl.program_id(0)
    rows = q_refs[0].shape[0]
    half = near_ref.shape[0]
    length = 2 * half

    @pl.when(index == 0)
    def _():
        for at, ref in enumerate(q_refs):
            held[at] = ref[...]
        for at, ref in ((0, near_ref), (half, far_ref)):
            keys[:size, at : at + half] = ref[:, :size].T
            values[at : at + half, :size] = ref[:, size:]
        keys[size:, :] = hide_ref[...]
        values[:, size:] = jnp.ones((length, size), jnp.bfloat16)

    mark = lax.broadcasted_iota(jnp.int32, (rows, size), 1) == index
    mark = jnp.where(mark, 1.0, 0.0).astype(jnp.bfloat16)
    row = lax.broadcasted_iota(jnp.int32, (rows, width), 0)
    key = lax.broadcasted_iota(jnp.int32, (rows, width), 1)
    later = (key > row) & (key < rows) & (index == 0)
    lane = lax.broadcasted_iota(jnp.int32, (rows, size), 1)
    sums = jnp.zeros((rows, size), jnp.float32)
    results = []
    for h in range(heads):
        q = jnp.concatenate([held[index, :, h * size : (h + 1) * size], mark], axis=1)
        total = jnp.zeros((rows, 2 * size), jnp.float32)
        for start in range(0, length, width):
            part = pl.ds(start, width)
            scores = f32dot(q, keys[:, part])
            if start == 0:
                scores = jnp.where(later, HIDDEN, scores)
            total = total + f32dot(jnp.exp2(scores).astype(jnp.bfloat16), values[part, :])
        results.append(total[:, :size].astype(jnp.bfloat16))
        high = total[:, size:].astype(jnp.bfloat16).astype(jnp.float32)
        sums = jnp.where(lane == 2 * h, high, sums)
        sums = jnp.where(lane == 2 * h + 1, total[:, size:] - high, sums)
    packed = jnp.concatenate([*results, sums.astype(jnp.bfloat16)], axis=1)
    for at, ref in enumerate(out_refs):

        @pl.when(index == at)
        def _(ref=ref):
            ref[...] = packed


def attend(queries, near, far, hide, heads, size):
    rows, columns = queries[0].shape
    ring = len(queries)
    length = 2 * near.shape[0]
    out = jax.ShapeDtypeStruct((rows, columns + size), jnp.bfloat16)
    return pl.pallas_call(
        functools.partial(attend_kernel, heads, size, 512, ring),
        grid=(ring,),
        in_specs=[whole_block(x.shape) for x in (*queries, near, far, hide)],
        out_specs=[whole_block(out.shape)] * ring,
        scratch_shapes=[
            pltpu.VMEM((ring, rows, columns), jnp.bfloat16),
            pltpu.VMEM((2 * size, length), jnp.bfloat16),
            pltpu.VMEM((length, 2 * size), jnp.bfloat16),
        ],
        out_shape=[out] * ring,
        compiler_params=params(),
        name="attend",
    )(*queries, near, far, hide)


def repeat_rows(values):
    rows = values.shape[0]
    row = lax.broadcasted_iota(jnp.int32, (rows * GROUP, rows), 0)
    column = lax.broadcasted_iota(jnp.int32, (rows * GROUP, rows), 1)
    copies = (lax.div(row, GROUP) == column).astype(jnp.bfloat16)
    return f32dot(copies, values)


def slots_kernel(routes_ref, pick_ref, last_ref, named_ref):
    fanout, tokens = routes_ref.shape
    count = named_ref.shape[0]
    expert = lax.broadcasted_iota(jnp.int32, (count, tokens), 0)
    named = jnp.zeros((count, tokens), jnp.float32)
    for j in range(fanout):
        named = named + jnp.where(routes_ref[j : j + 1, :] == expert, 1.0, 0.0)
    earlier = lax.broadcasted_iota(jnp.int32, (tokens, tokens), 0)
    later = lax.broadcasted_iota(jnp.int32, (tokens, tokens), 1)
    before = (earlier < later).astype(jnp.bfloat16)
    rank = f32dot(named.astype(jnp.bfloat16), before)
    code = named * (rank + 1.0)
    named_ref[...] = named
    last_ref[...] = (code == GROUP + 1.0).astype(jnp.bfloat16)
    spread = repeat_rows(code.astype(jnp.bfloat16))
    slot = lax.rem(lax.broadcasted_iota(jnp.int32, spread.shape, 0), GROUP) + 1
    pick_ref[...] = (spread == slot.astype(jnp.float32)).astype(jnp.bfloat16)


def slots(routes_t, count):
    fanout, tokens = routes_t.shape
    return pl.pallas_call(
        slots_kernel,
        out_shape=[
            jax.ShapeDtypeStruct((count * GROUP, tokens), jnp.bfloat16),
            jax.ShapeDtypeStruct((count, tokens), jnp.bfloat16),
            jax.ShapeDtypeStruct((count, tokens), jnp.float32),
        ],
        compiler_params=pltpu.CompilerParams(vmem_limit_bytes=VMEM_MB * 1024 * 1024),
        name="slots",
    )(routes_t)


def weigh_kernel(x_ref, router_ref, named_ref, pick_ref, last_ref, out_ref, out_last_ref):
    tokens = x_ref.shape[0]
    logits = lax.dot_general(
        router_ref[...], x_ref[...], (((0,), (1,)), ((), ())), preferred_element_type=jnp.float32
    )
    named = named_ref[...] > 0.5
    largest = jnp.max(jnp.where(named, logits, -jnp.inf), axis=0, keepdims=True)
    shares = jnp.where(named, jnp.exp(jnp.minimum(logits - largest, 0.0)), 0.0)
    shares = shares / jnp.sum(shares, axis=0, keepdims=True)
    high = shares.astype(jnp.bfloat16)
    low = (shares - high.astype(jnp.float32)).astype(jnp.bfloat16)
    for at, part in ((0, high), (tokens, low)):
        out_ref[:, at : at + tokens] = repeat_rows(part).astype(jnp.bfloat16) * pick_ref[...]
        out_last_ref[:, at : at + tokens] = part * last_ref[...]


def weigh(moe_in, router, named, pick, last):
    tokens = moe_in.shape[0]
    return pl.pallas_call(
        weigh_kernel,
        out_shape=[
            jax.ShapeDtypeStruct((pick.shape[0], 2 * tokens), jnp.bfloat16),
            jax.ShapeDtypeStruct((last.shape[0], 2 * tokens), jnp.bfloat16),
        ],
        compiler_params=pltpu.CompilerParams(vmem_limit_bytes=VMEM_MB * 1024 * 1024),
        name="weigh",
    )(moe_in, router, named, pick, last)


def fold(rows):
    count, features = rows.shape
    return rows.reshape(count, GROUP, features // GROUP).reshape(count * GROUP, features // GROUP)


def unfold(rows):
    count, piece = rows.shape
    return rows.reshape(count // GROUP, GROUP, piece).reshape(count // GROUP, GROUP * piece)


def fill(out_ref, x, pick, last):
    features = x.shape[1]
    out_ref[:, :features] = f32dot(pick, x).astype(jnp.bfloat16)
    out_ref[:, features:] = fold(f32dot(last, x).astype(jnp.bfloat16))


def finish_kernel(
    heads,
    size,
    features,
    *refs,
):
    parts_refs, refs = refs[:-8], refs[-8:]
    w_ref, x_ref, gain_ref, pick_ref, last_ref, resid_ref, norm_ref, out_ref = refs

    @pl.when(pl.program_id(0) == 0)
    def _():
        summed = parts_refs[0][...].astype(jnp.float32)
        for ref in parts_refs[1:]:
            summed = summed + ref[...].astype(jnp.float32)
        base = heads * size
        attended = []
        for h in range(heads):
            at = base + 2 * h
            total = summed[:, at : at + 1] + summed[:, at + 1 : at + 2]
            attended.append((summed[:, h * size : (h + 1) * size] / total).astype(jnp.bfloat16))
        projected = f32dot(jnp.concatenate(attended, axis=1), w_ref[...])
        resid = x_ref[...].astype(jnp.float32) + projected
        resid_ref[...] = resid
        scale = lax.rsqrt(jnp.mean(resid * resid, axis=1, keepdims=True) + 1e-06)
        norm_ref[...] = (resid * scale * gain_ref[...].astype(jnp.float32)).astype(jnp.bfloat16)

    fill(out_ref, norm_ref[:, :features], pick_ref[...], last_ref[...])


def finish(parts, w_out, tokens, gain, pick, last, heads, size, features):
    rows, count = pick.shape[0], last.shape[0]
    wide = features + features // GROUP
    blocks = 4
    return pl.pallas_call(
        functools.partial(finish_kernel, heads, size, features),
        grid=(blocks,),
        in_specs=[
            *(whole_block(x.shape) for x in parts),
            whole_block(w_out.shape),
            whole_block(tokens.shape),
            whole_block((1, gain.shape[0])),
            pl.BlockSpec((rows // blocks, pick.shape[1]), lambda i: (i, 0)),
            pl.BlockSpec((count // blocks, pick.shape[1]), lambda i: (i, 0)),
        ],
        out_specs=[
            pl.BlockSpec(tokens.shape, lambda i: (0, 0)),
            pl.BlockSpec(tokens.shape, lambda i: (0, 0)),
            pl.BlockSpec((rows // blocks, wide), lambda i: (i, 0)),
        ],
        out_shape=[
            jax.ShapeDtypeStruct(tokens.shape, jnp.float32),
            jax.ShapeDtypeStruct(tokens.shape, jnp.bfloat16),
            jax.ShapeDtypeStruct((rows, wide), jnp.bfloat16),
        ],
        compiler_params=params(),
        name="finish",
    )(*parts, w_out, tokens, gain.reshape(1, -1), pick, last)


def dispatch_kernel(x_ref, pick_ref, last_ref, out_ref):
    fill(out_ref, x_ref[...], pick_ref[...], last_ref[...])


def dispatch(normed, pick, last, chunk, features):
    rows, tokens = pick.shape
    count = last.shape[0]
    wide = features + features // GROUP
    blocks = 4
    return pl.pallas_call(
        dispatch_kernel,
        grid=(blocks,),
        in_specs=[
            pl.BlockSpec((tokens, features), lambda i: (0, chunk)),
            pl.BlockSpec((rows // blocks, tokens), lambda i: (i, 0)),
            pl.BlockSpec((count // blocks, tokens), lambda i: (i, 0)),
        ],
        out_specs=pl.BlockSpec((rows // blocks, wide), lambda i: (i, 0)),
        out_shape=jax.ShapeDtypeStruct((rows, wide), jnp.bfloat16),
        compiler_params=params(),
        cost_estimate=pl.CostEstimate(
            flops=4 * rows * tokens * features, bytes_accessed=4 * rows * features, transcendentals=0
        ),
        name="dispatch",
    )(normed, pick, last)


def all_rows(x_ref, features):
    return jnp.concatenate([x_ref[:, :features], unfold(x_ref[:, features:])], axis=0)


def up_kernel(features, x_ref, w_ref, out_ref):
    out_ref[...] = f32dot(all_rows(x_ref, features), w_ref[0])


def up_first(received, weights, features):
    rows, wide = received.shape
    columns = weights.shape[2]
    blocks = 4
    taken = rows // blocks * (GROUP + 1) // GROUP
    return pl.pallas_call(
        functools.partial(up_kernel, features),
        grid=(blocks,),
        in_specs=[
            pl.BlockSpec((rows // blocks, wide), lambda i: (i, 0)),
            pl.BlockSpec(
                (1, features, columns), lambda i: (0, 0, 0), pipeline_mode=pl.Buffered(1)
            ),
        ],
        out_specs=pl.BlockSpec((taken, columns), lambda i: (i, 0)),
        out_shape=jax.ShapeDtypeStruct((taken * blocks, columns), jnp.float32),
        compiler_params=params(),
        cost_estimate=pl.CostEstimate(
            flops=2 * rows * features * columns, bytes_accessed=20000000, transcendentals=0
        ),
        name="up_first",
    )(received, weights)


def expert_kernel(
    features, x_ref, wu_ref, partial_ref, wd_hbm, out_ref, wd, arrived
):
    index = pl.program_id(0)
    copy = pltpu.make_async_copy(wd_hbm.at[0], wd, arrived)

    @pl.when(index == 0)
    def _():
        copy.start()

    gate_up = partial_ref[...] + f32dot(all_rows(x_ref, features), wu_ref[0])
    hidden = gate_up.shape[1] // 2
    gate = gate_up[:, :hidden]
    active = (gate / (1.0 + jnp.exp(-gate)) * gate_up[:, hidden:]).astype(jnp.bfloat16)

    @pl.when(index == 0)
    def _():
        copy.wait()

    rows = x_ref.shape[0]
    out = f32dot(active, wd[...])
    out_ref[:, : wd.shape[1]] = out[:rows].astype(jnp.bfloat16)
    out_ref[:, wd.shape[1] :] = fold(out[rows:].astype(jnp.bfloat16))


def expert(received, w_up, partial, w_down, features, chunk):
    rows, wide = received.shape
    columns = w_up.shape[2]
    hidden, width = w_down.shape[1:]
    blocks = 4
    taken = rows // blocks * (GROUP + 1) // GROUP
    out_wide = width + width // GROUP
    return pl.pallas_call(
        functools.partial(expert_kernel, features),
        grid=(blocks,),
        in_specs=[
            pl.BlockSpec((rows // blocks, wide), lambda i: (i, 0)),
            pl.BlockSpec(
                (1, features, columns), lambda i: (0, chunk, 0), pipeline_mode=pl.Buffered(1)
            ),
            pl.BlockSpec((taken, columns), lambda i: (i, 0)),
            pl.BlockSpec(memory_space=pl.ANY),
        ],
        out_specs=pl.BlockSpec((rows // blocks, out_wide), lambda i: (i, 0)),
        out_shape=jax.ShapeDtypeStruct((rows, out_wide), jnp.bfloat16),
        scratch_shapes=[pltpu.VMEM((hidden, width), jnp.bfloat16), pltpu.SemaphoreType.DMA(())],
        compiler_params=params(),
        cost_estimate=pl.CostEstimate(
            flops=2 * rows * (features * columns + hidden * width),
            bytes_accessed=30000000,
            transcendentals=0,
        ),
        name="expert",
    )(received, w_up, partial, w_down)


def combine_kernel(x_ref, w_ref, wlast_ref, resid_ref, out_ref, total, last):
    index = pl.program_id(0)
    tokens, features = resid_ref.shape
    lasts = x_ref.shape[0] // GROUP

    def weighted(weights, x):
        both = lax.dot_general(
            weights, x, (((0,), (0,)), ((), ())), preferred_element_type=jnp.float32
        )
        return both[:tokens] + both[tokens:]

    added = weighted(w_ref[...], x_ref[:, :features])
    last[pl.ds(pl.multiple_of(index * lasts, lasts), lasts), :] = unfold(x_ref[:, features:])

    @pl.when(index == 0)
    def _():
        total[...] = resid_ref[...] + added

    @pl.when(index > 0)
    def _():
        total[...] += added

    @pl.when(index == pl.num_programs(0) - 1)
    def _():
        out_ref[...] = (total[...] + weighted(wlast_ref[...], last[...])).astype(jnp.bfloat16)


def combine(returned, weights, last_weights, resid):
    rows, wide = returned.shape
    tokens, features = resid.shape
    count = last_weights.shape[0]
    blocks = 4
    return pl.pallas_call(
        combine_kernel,
        grid=(blocks,),
        in_specs=[
            pl.BlockSpec((rows // blocks, wide), lambda i: (i, 0)),
            pl.BlockSpec((rows // blocks, 2 * tokens), lambda i: (i, 0)),
            whole_block((count, 2 * tokens)),
            whole_block((tokens, features)),
        ],
        out_specs=pl.BlockSpec((tokens, features), lambda i: (0, 0)),
        out_shape=jax.ShapeDtypeStruct((tokens, features), jnp.bfloat16),
        scratch_shapes=[
            pltpu.VMEM((tokens, features), jnp.float32),
            pltpu.VMEM((count, features), jnp.bfloat16),
        ],
        compiler_params=params(),
        name="combine",
    )(returned, weights, last_weights, resid)


def on_device(
    tokens,
    block_order,
    attn_gain,
    query_gain,
    key_gain,
    w_qkv,
    w_out,
    moe_gain,
    router,
    routes,
    w_gate_up,
    w_down,
):
    rows, model_width = tokens.shape
    size = query_gain.shape[0]
    ctx_size, exp_size = lax.axis_size("ctx"), lax.axis_size("exp")
    ctx_at, exp_at = lax.axis_index("ctx"), lax.axis_index("exp")
    ring = 4
    inner = exp_size // ring
    x_at, z_lo = ctx_at % ring, ctx_at // ring
    y_at, z_hi, core = exp_at // inner, exp_at // 2 % 2, exp_at % 2

    def device(z_lo, x, y, z_hi, core):
        return (z_lo * ring + x) * exp_size + y * inner + z_hi * 2 + core

    def bring(value, z_lo=0, x=0, y=0, z_hi=0, core=0):
        pairs = []
        for at in range(ctx_size * exp_size):
            c, e = at // exp_size, at % exp_size
            source = device(
                c // ring ^ z_lo,
                (c - x) % ring,
                (e // inner - y) % ring,
                e // 2 % 2 ^ z_hi,
                e % 2 ^ core,
            )
            pairs.append((source, at))
        return lax.ppermute(value, ("ctx", "exp"), pairs)

    def along_y(value):
        return jnp.concatenate([value] + [bring(value, y=k) for k in range(1, ring)])

    def along_x(values, step):
        return [values[0]] + [bring(values[k], x=step * k) for k in range(1, ring)]

    relative = jnp.arange(exp_size, dtype=jnp.int32)
    piece_of = (
        (core + relative) % 2 * (2 * ring)
        + (y_at - relative // inner) % ring * 2
        + (z_hi + relative // 2) % 2
    )
    relative = jnp.arange(2 * exp_size, dtype=jnp.int32)
    key_devices = device(
        (z_lo + relative) % 2,
        x_at,
        (y_at - relative // 4) % ring,
        (z_hi + relative // 2) % 2,
        (core + relative // (4 * ring)) % 2,
    )
    steps = jnp.arange(ring, dtype=jnp.int32)
    query_devices = device(z_lo, (x_at - steps) % ring, y_at, z_hi, core)

    def block_numbers(devices):
        every = jnp.arange(block_order.shape[0], dtype=jnp.int32)
        return jnp.sum(
            jnp.where(devices[:, None] == every[None, :], block_order[None, :], 0), axis=1
        )

    k_blocks = block_numbers(key_devices)
    q_blocks = block_numbers(query_devices)
    own_pos = q_blocks[0] * rows + jnp.arange(rows, dtype=jnp.int32)
    hide = jnp.repeat(
        jnp.where(k_blocks[None, :] > q_blocks[:, None], HIDDEN, 0.0), rows, axis=1
    )
    hide = jnp.pad(hide, ((0, size - ring), (0, 0))).astype(jnp.bfloat16)

    depth = model_width // ring
    widened = tokens.astype(jnp.float32)
    row_scale = lax.rsqrt(jnp.mean(widened * widened, axis=1, keepdims=True) + 1e-06)
    gained = (widened * attn_gain.astype(jnp.float32)).astype(jnp.bfloat16)
    w_share = lax.dynamic_slice_in_dim(w_qkv.T, x_at * depth, depth, 1)
    near = along_y(jnp.stack([w_share, bring(w_share, z_hi=1)]))
    shares = along_x(
        [
            lax.dynamic_slice_in_dim(gained, (x_at + k) % ring * depth, depth, 1)
            for k in range(ring)
        ],
        1,
    )
    w_out, near, shares = lax.optimization_barrier((w_out, near, shares))
    far = bring(near, core=1)
    w_out_all = lax.all_gather(w_out, "exp", axis=0, tiled=True)
    shares = project(shares, near, far, piece_of)
    shares, routes = lax.optimization_barrier((shares, routes))
    count = router.shape[1]
    pick, pick_last, named = slots(routes.T, count)
    mixed = sum(x.astype(jnp.float32) for x in along_x(shares, -1)) * row_scale
    mixed, pick, pick_last, named, hide = lax.optimization_barrier(
        (mixed, pick, pick_last, named, hide)
    )
    heads = mixed.shape[1] // size - 2
    queries = mixed[:, : heads * size].reshape(rows, heads, size)
    queries = (
        (
            rotate(rms_scale(queries, query_gain), own_pos[:, None].astype(jnp.float32))
            * (math.log2(math.e) / math.sqrt(size))
        )
        .astype(jnp.bfloat16)
        .reshape(rows, heads * size)
    )
    keys = rotate(
        rms_scale(mixed[:, heads * size : (heads + 1) * size], key_gain),
        own_pos.astype(jnp.float32),
    ).astype(jnp.bfloat16)
    values = mixed[:, (heads + 1) * size :].astype(jnp.bfloat16)
    key_values = jnp.concatenate([keys, values], axis=1)

    near = along_y(
        jnp.stack(
            [
                key_values,
                bring(key_values, z_lo=1),
                bring(key_values, z_hi=1),
                bring(key_values, z_lo=1, z_hi=1),
            ]
        )
    ).reshape(-1, 2 * size)
    near, queries = lax.optimization_barrier((near, along_x([queries] * ring, 1)))
    far = bring(near, core=1)
    parts = along_x(attend(queries, near, far, hide, heads, size), -1)
    main = model_width // 4 * 3
    rest = model_width - main
    resid, moe_in, outgoing = finish(
        parts, w_out_all, tokens, moe_gain, pick, pick_last, heads, size, main
    )

    def exchange(x):
        wide = x.shape[1]
        x = lax.all_to_all(
            x.reshape(count, GROUP, wide), ("ctx", "exp"), split_axis=0, concat_axis=0, tiled=True
        )
        return x.reshape(count * GROUP, wide)

    first = exchange(outgoing)
    second = exchange(dispatch(moe_in, pick, pick_last, main // rest, rest))
    first, moe_in = lax.optimization_barrier((first, moe_in))
    weights, last_weights = weigh(moe_in, router, named, pick, pick_last)
    partial = up_first(first, w_gate_up, main)
    returned = exchange(expert(second, w_gate_up, partial, w_down, rest, main // rest))
    return combine(returned, weights, last_weights, resid)


def solution(mesh):
    return jax.shard_map(
        on_device,
        mesh=mesh,
        in_specs=(
            P(("ctx", "exp"), None),
            P(),
            P(),
            P(),
            P(),
            P(None, "exp"),
            P("exp", None),
            P(),
            P(),
            P(("ctx", "exp"), None),
            P(("ctx", "exp"), None, None),
            P(("ctx", "exp"), None, None),
        ),
        out_specs=P(("ctx", "exp"), None),
        check_vma=False,
    )
```

```python
import functools
import math

import jax
import jax.numpy as jnp
from jax import lax
from jax.experimental import pallas as pl
from jax.experimental.pallas import tpu as pltpu
from jax.sharding import PartitionSpec as P

rope_base = 1000000.0
GROUP = 8
VMEM_MB = 60
HIDDEN = -30000.0


def rms_scale(values, gain):
    widened = values.astype(jnp.float32)
    return (
        widened
        * lax.rsqrt(jnp.mean(widened * widened, axis=-1, keepdims=True) + 1e-06)
        * gain.astype(jnp.float32)
    )


def params(axes=1):
    return pltpu.CompilerParams(
        vmem_limit_bytes=VMEM_MB * 1024 * 1024, dimension_semantics=("arbitrary",) * axes
    )


def f32dot(a, b):
    return jnp.dot(a, b, preferred_element_type=jnp.float32)


def whole_block(shape):
    zeros = (0,) * len(shape)
    return pl.BlockSpec(shape, lambda *_: zeros, pipeline_mode=pl.Buffered(1))


def project_kernel(order_ref, *refs):
    ring = (len(refs) - 3) // 2
    x_refs, (near_ref, far_ref), out_refs, whole = (
        refs[:ring],
        refs[ring : ring + 2],
        refs[ring + 2 : -1],
        refs[-1],
    )
    half, columns = near_ref.shape[:2]
    rows = x_refs[0].shape[0]
    for e in range(2 * half):
        at = order_ref[e]
        near = near_ref[lax.rem(at, half)].astype(jnp.float32)
        far = far_ref[lax.rem(at, half)].astype(jnp.float32)
        whole[e * columns : (e + 1) * columns, :] = jnp.where(at < half, near, far).astype(
            jnp.bfloat16
        )
    x = jnp.concatenate([ref[...] for ref in x_refs], axis=0)
    out = lax.dot_general(
        x, whole[...], (((1,), (1,)), ((), ())), preferred_element_type=jnp.float32
    ).astype(jnp.bfloat16)
    for at, ref in enumerate(out_refs):
        ref[...] = out[at * rows : (at + 1) * rows]


def project(shares, near, far, order):
    rows, depth = shares[0].shape
    half, columns = near.shape[:2]
    out = jax.ShapeDtypeStruct((rows, 2 * half * columns), jnp.bfloat16)
    return pl.pallas_call(
        project_kernel,
        grid_spec=pltpu.PrefetchScalarGridSpec(
            num_scalar_prefetch=1,
            grid=(1,),
            in_specs=[whole_block(x.shape) for x in (*shares, near, far)],
            out_specs=[whole_block(out.shape)] * len(shares),
            scratch_shapes=[pltpu.VMEM((2 * half * columns, depth), jnp.bfloat16)],
        ),
        out_shape=[out] * len(shares),
        compiler_params=params(),
        name="project",
    )(order, *shares, near, far)


def shape_kernel(heads, size, *refs):
    parts, (scale_ref, qgain_ref, kgain_ref, cos_ref, sin_ref, q_ref, kv_ref) = refs[:-7], refs[-7:]
    mixed = parts[0][...].astype(jnp.float32)
    for ref in parts[1:]:
        mixed = mixed + ref[...].astype(jnp.float32)
    mixed = mixed * scale_ref[...]
    half = size // 2

    def rope(values, gain):
        scale = lax.rsqrt(jnp.mean(values * values, axis=1, keepdims=True) + 1e-06)
        values = values * scale * gain.astype(jnp.float32)
        turned = jnp.concatenate([values[:, half:], values[:, :half]], axis=1)
        return values * cos_ref[...] + turned * sin_ref[...]

    for h in range(heads):
        part = slice(h * size, (h + 1) * size)
        q = rope(mixed[:, part], qgain_ref[...]) * (math.log2(math.e) / math.sqrt(size))
        q_ref[:, part] = q.astype(jnp.bfloat16)
    at = heads * size
    kv_ref[:, :size] = rope(mixed[:, at : at + size], kgain_ref[...]).astype(jnp.bfloat16)
    kv_ref[:, size:] = mixed[:, at + size :].astype(jnp.bfloat16)


def shape(parts, scale, query_gain, key_gain, cos, sin):
    rows, columns = parts[0].shape
    size = query_gain.shape[0]
    heads = columns // size - 2
    return pl.pallas_call(
        functools.partial(shape_kernel, heads, size),
        out_shape=[
            jax.ShapeDtypeStruct((rows, heads * size), jnp.bfloat16),
            jax.ShapeDtypeStruct((rows, 2 * size), jnp.bfloat16),
        ],
        compiler_params=pltpu.CompilerParams(vmem_limit_bytes=VMEM_MB * 1024 * 1024),
        name="shape",
    )(*parts, scale, query_gain.reshape(1, -1), key_gain.reshape(1, -1), cos, sin)


def attend_kernel(heads, size, width, ring, *refs):
    q_refs, (near_ref, far_ref, hide_ref), out_refs, (held, keys, values) = (
        refs[:ring],
        refs[ring : ring + 3],
        refs[ring + 3 : -3],
        refs[-3:],
    )
    index = pl.program_id(0)
    rows = q_refs[0].shape[0]
    half = near_ref.shape[0]
    length = 2 * half

    @pl.when(index == 0)
    def _():
        for at, ref in enumerate(q_refs):
            held[at] = ref[...]
        for at, ref in ((0, near_ref), (half, far_ref)):
            keys[:size, at : at + half] = ref[:, :size].T
            values[at : at + half, :size] = ref[:, size:]
        keys[size:, :] = hide_ref[...]
        values[:, size:] = jnp.ones((length, size), jnp.bfloat16)

    mark = lax.broadcasted_iota(jnp.int32, (rows, size), 1) == index
    mark = jnp.where(mark, 1.0, 0.0).astype(jnp.bfloat16)
    row = lax.broadcasted_iota(jnp.int32, (rows, width), 0)
    key = lax.broadcasted_iota(jnp.int32, (rows, width), 1)
    later = (key > row) & (key < rows) & (index == 0)
    lane = lax.broadcasted_iota(jnp.int32, (rows, size), 1)
    sums = jnp.zeros((rows, size), jnp.float32)
    results = []
    for h in range(heads):
        q = jnp.concatenate([held[index, :, h * size : (h + 1) * size], mark], axis=1)
        total = jnp.zeros((rows, 2 * size), jnp.float32)
        for start in range(0, length, width):
            part = pl.ds(start, width)
            scores = f32dot(q, keys[:, part])
            if start == 0:
                scores = jnp.where(later, HIDDEN, scores)
            total = total + f32dot(jnp.exp2(scores).astype(jnp.bfloat16), values[part, :])
        results.append(total[:, :size].astype(jnp.bfloat16))
        high = total[:, size:].astype(jnp.bfloat16).astype(jnp.float32)
        sums = jnp.where(lane == 2 * h, high, sums)
        sums = jnp.where(lane == 2 * h + 1, total[:, size:] - high, sums)
    packed = jnp.concatenate([*results, sums.astype(jnp.bfloat16)], axis=1)
    for at, ref in enumerate(out_refs):

        @pl.when(index == at)
        def _(ref=ref):
            ref[...] = packed


def attend(queries, near, far, hide, heads, size):
    rows, columns = queries[0].shape
    ring = len(queries)
    length = 2 * near.shape[0]
    out = jax.ShapeDtypeStruct((rows, columns + size), jnp.bfloat16)
    return pl.pallas_call(
        functools.partial(attend_kernel, heads, size, 512, ring),
        grid=(ring,),
        in_specs=[whole_block(x.shape) for x in (*queries, near, far, hide)],
        out_specs=[whole_block(out.shape)] * ring,
        scratch_shapes=[
            pltpu.VMEM((ring, rows, columns), jnp.bfloat16),
            pltpu.VMEM((2 * size, length), jnp.bfloat16),
            pltpu.VMEM((length, 2 * size), jnp.bfloat16),
        ],
        out_shape=[out] * ring,
        compiler_params=params(),
        name="attend",
    )(*queries, near, far, hide)


def repeat_rows(values):
    rows = values.shape[0]
    row = lax.broadcasted_iota(jnp.int32, (rows * GROUP, rows), 0)
    column = lax.broadcasted_iota(jnp.int32, (rows * GROUP, rows), 1)
    copies = (lax.div(row, GROUP) == column).astype(jnp.bfloat16)
    return f32dot(copies, values)


def slots_kernel(routes_ref, pick_ref, last_ref, named_ref):
    fanout, tokens = routes_ref.shape
    count = named_ref.shape[0]
    expert = lax.broadcasted_iota(jnp.int32, (count, tokens), 0)
    named = jnp.zeros((count, tokens), jnp.float32)
    for j in range(fanout):
        named = named + jnp.where(routes_ref[j : j + 1, :] == expert, 1.0, 0.0)
    earlier = lax.broadcasted_iota(jnp.int32, (tokens, tokens), 0)
    later = lax.broadcasted_iota(jnp.int32, (tokens, tokens), 1)
    before = (earlier < later).astype(jnp.bfloat16)
    rank = f32dot(named.astype(jnp.bfloat16), before)
    code = named * (rank + 1.0)
    named_ref[...] = named
    last_ref[...] = (code == GROUP + 1.0).astype(jnp.bfloat16)
    spread = repeat_rows(code.astype(jnp.bfloat16))
    slot = lax.rem(lax.broadcasted_iota(jnp.int32, spread.shape, 0), GROUP) + 1
    pick_ref[...] = (spread == slot.astype(jnp.float32)).astype(jnp.bfloat16)


def slots(routes_t, count):
    fanout, tokens = routes_t.shape
    return pl.pallas_call(
        slots_kernel,
        out_shape=[
            jax.ShapeDtypeStruct((count * GROUP, tokens), jnp.bfloat16),
            jax.ShapeDtypeStruct((count, tokens), jnp.bfloat16),
            jax.ShapeDtypeStruct((count, tokens), jnp.float32),
        ],
        compiler_params=pltpu.CompilerParams(vmem_limit_bytes=VMEM_MB * 1024 * 1024),
        name="slots",
    )(routes_t)


def weigh_kernel(x_ref, router_ref, named_ref, pick_ref, last_ref, out_ref, out_last_ref):
    tokens = x_ref.shape[0]
    logits = lax.dot_general(
        router_ref[...], x_ref[...], (((0,), (1,)), ((), ())), preferred_element_type=jnp.float32
    )
    named = named_ref[...] > 0.5
    largest = jnp.max(jnp.where(named, logits, -jnp.inf), axis=0, keepdims=True)
    shares = jnp.where(named, jnp.exp(jnp.minimum(logits - largest, 0.0)), 0.0)
    shares = shares / jnp.sum(shares, axis=0, keepdims=True)
    high = shares.astype(jnp.bfloat16)
    low = (shares - high.astype(jnp.float32)).astype(jnp.bfloat16)
    for at, part in ((0, high), (tokens, low)):
        out_ref[at : at + tokens, :] = (repeat_rows(part).astype(jnp.bfloat16) * pick_ref[...]).T
        out_last_ref[at : at + tokens, :] = (part * last_ref[...]).T


def weigh(moe_in, router, named, pick, last):
    tokens = moe_in.shape[0]
    return pl.pallas_call(
        weigh_kernel,
        out_shape=[
            jax.ShapeDtypeStruct((2 * tokens, pick.shape[0]), jnp.bfloat16),
            jax.ShapeDtypeStruct((2 * tokens, last.shape[0]), jnp.bfloat16),
        ],
        compiler_params=pltpu.CompilerParams(vmem_limit_bytes=VMEM_MB * 1024 * 1024),
        name="weigh",
    )(moe_in, router, named, pick, last)


def fold(rows):
    count, features = rows.shape
    return rows.reshape(count, GROUP, features // GROUP).reshape(count * GROUP, features // GROUP)


def unfold(rows):
    count, piece = rows.shape
    return rows.reshape(count // GROUP, GROUP, piece).reshape(count // GROUP, GROUP * piece)


def fill(out_ref, x, pick, last):
    features = x.shape[1]
    out_ref[:, :features] = f32dot(pick, x).astype(jnp.bfloat16)
    out_ref[:, features:] = fold(f32dot(last, x).astype(jnp.bfloat16))


def finish_kernel(
    heads,
    size,
    features,
    *refs,
):
    parts_refs, refs = refs[:-12], refs[-12:]
    w_ref, x_ref, gain_ref, pick_ref, last_ref, resid_hbm, norm_hbm, out_ref = refs[:8]
    resid_ref, norm_ref, resid_sent, norm_sent = refs[8:]
    copies = (
        pltpu.make_async_copy(resid_ref, resid_hbm, resid_sent),
        pltpu.make_async_copy(norm_ref, norm_hbm, norm_sent),
    )

    @pl.when(pl.program_id(0) == 0)
    def _():
        summed = parts_refs[0][...].astype(jnp.float32)
        for ref in parts_refs[1:]:
            summed = summed + ref[...].astype(jnp.float32)
        base = heads * size
        attended = []
        for h in range(heads):
            at = base + 2 * h
            total = summed[:, at : at + 1] + summed[:, at + 1 : at + 2]
            attended.append((summed[:, h * size : (h + 1) * size] / total).astype(jnp.bfloat16))
        projected = f32dot(jnp.concatenate(attended, axis=1), w_ref[...])
        resid = x_ref[...].astype(jnp.float32) + projected
        resid_ref[...] = resid
        scale = lax.rsqrt(jnp.mean(resid * resid, axis=1, keepdims=True) + 1e-06)
        norm_ref[...] = (resid * scale * gain_ref[...].astype(jnp.float32)).astype(jnp.bfloat16)
        for copy in copies:
            copy.start()

    fill(out_ref, norm_ref[:, :features], pick_ref[...], last_ref[...])

    @pl.when(pl.program_id(0) == pl.num_programs(0) - 1)
    def _():
        for copy in copies:
            copy.wait()


def finish(parts, w_out, tokens, gain, pick, last, heads, size, features):
    rows, count = pick.shape[0], last.shape[0]
    wide = features + features // GROUP
    blocks = 4
    return pl.pallas_call(
        functools.partial(finish_kernel, heads, size, features),
        grid=(blocks,),
        in_specs=[
            *(whole_block(x.shape) for x in parts),
            whole_block(w_out.shape),
            whole_block(tokens.shape),
            whole_block((1, gain.shape[0])),
            pl.BlockSpec((rows // blocks, pick.shape[1]), lambda i: (i, 0)),
            pl.BlockSpec((count // blocks, pick.shape[1]), lambda i: (i, 0)),
        ],
        out_specs=[
            pl.BlockSpec(memory_space=pl.ANY),
            pl.BlockSpec(memory_space=pl.ANY),
            pl.BlockSpec((rows // blocks, wide), lambda i: (i, 0)),
        ],
        scratch_shapes=[
            pltpu.VMEM(tokens.shape, jnp.float32),
            pltpu.VMEM(tokens.shape, jnp.bfloat16),
            pltpu.SemaphoreType.DMA(()),
            pltpu.SemaphoreType.DMA(()),
        ],
        out_shape=[
            jax.ShapeDtypeStruct(tokens.shape, jnp.float32),
            jax.ShapeDtypeStruct(tokens.shape, jnp.bfloat16),
            jax.ShapeDtypeStruct((rows, wide), jnp.bfloat16),
        ],
        compiler_params=params(),
        name="finish",
    )(*parts, w_out, tokens, gain.reshape(1, -1), pick, last)


def dispatch_kernel(x_ref, pick_ref, last_ref, out_ref):
    fill(out_ref, x_ref[...], pick_ref[...], last_ref[...])


def dispatch(normed, pick, last, chunk, features):
    rows, tokens = pick.shape
    count = last.shape[0]
    wide = features + features // GROUP
    blocks = 4
    return pl.pallas_call(
        dispatch_kernel,
        grid=(blocks,),
        in_specs=[
            pl.BlockSpec((tokens, features), lambda i: (0, chunk)),
            pl.BlockSpec((rows // blocks, tokens), lambda i: (i, 0)),
            pl.BlockSpec((count // blocks, tokens), lambda i: (i, 0)),
        ],
        out_specs=pl.BlockSpec((rows // blocks, wide), lambda i: (i, 0)),
        out_shape=jax.ShapeDtypeStruct((rows, wide), jnp.bfloat16),
        compiler_params=params(),
        cost_estimate=pl.CostEstimate(
            flops=4 * rows * tokens * features, bytes_accessed=4 * rows * features, transcendentals=0
        ),
        name="dispatch",
    )(normed, pick, last)


def all_rows(x_ref, features):
    return jnp.concatenate([x_ref[:, :features], unfold(x_ref[:, features:])], axis=0)


def up_kernel(features, x_ref, w_ref, out_ref):
    out_ref[...] = f32dot(all_rows(x_ref, features), w_ref[0])


def up_first(received, weights, features):
    rows, wide = received.shape
    columns = weights.shape[2]
    blocks = 4
    taken = rows // blocks * (GROUP + 1) // GROUP
    return pl.pallas_call(
        functools.partial(up_kernel, features),
        grid=(blocks,),
        in_specs=[
            pl.BlockSpec((rows // blocks, wide), lambda i: (i, 0)),
            pl.BlockSpec(
                (1, features, columns), lambda i: (0, 0, 0), pipeline_mode=pl.Buffered(1)
            ),
        ],
        out_specs=pl.BlockSpec((taken, columns), lambda i: (i, 0)),
        out_shape=jax.ShapeDtypeStruct((taken * blocks, columns), jnp.float32),
        compiler_params=params(),
        cost_estimate=pl.CostEstimate(
            flops=2 * rows * features * columns, bytes_accessed=20000000, transcendentals=0
        ),
        name="up_first",
    )(received, weights)


def expert_kernel(
    features, x_ref, wu_ref, partial_ref, wd_hbm, out_ref, wd, arrived
):
    index = pl.program_id(0)
    copy = pltpu.make_async_copy(wd_hbm.at[0], wd, arrived)

    @pl.when(index == 0)
    def _():
        copy.start()

    gate_up = partial_ref[...] + f32dot(all_rows(x_ref, features), wu_ref[0])
    hidden = gate_up.shape[1] // 2
    gate = gate_up[:, :hidden]
    active = (gate / (1.0 + jnp.exp(-gate)) * gate_up[:, hidden:]).astype(jnp.bfloat16)

    @pl.when(index == 0)
    def _():
        copy.wait()

    rows = x_ref.shape[0]
    out = f32dot(active, wd[...])
    out_ref[:, : wd.shape[1]] = out[:rows].astype(jnp.bfloat16)
    out_ref[:, wd.shape[1] :] = fold(out[rows:].astype(jnp.bfloat16))


def expert(received, w_up, partial, w_down, features, chunk):
    rows, wide = received.shape
    columns = w_up.shape[2]
    hidden, width = w_down.shape[1:]
    blocks = 4
    taken = rows // blocks * (GROUP + 1) // GROUP
    out_wide = width + width // GROUP
    return pl.pallas_call(
        functools.partial(expert_kernel, features),
        grid=(blocks,),
        in_specs=[
            pl.BlockSpec((rows // blocks, wide), lambda i: (i, 0)),
            pl.BlockSpec(
                (1, features, columns), lambda i: (0, chunk, 0), pipeline_mode=pl.Buffered(1)
            ),
            pl.BlockSpec((taken, columns), lambda i: (i, 0)),
            pl.BlockSpec(memory_space=pl.ANY),
        ],
        out_specs=pl.BlockSpec((rows // blocks, out_wide), lambda i: (i, 0)),
        out_shape=jax.ShapeDtypeStruct((rows, out_wide), jnp.bfloat16),
        scratch_shapes=[pltpu.VMEM((hidden, width), jnp.bfloat16), pltpu.SemaphoreType.DMA(())],
        compiler_params=params(),
        cost_estimate=pl.CostEstimate(
            flops=2 * rows * (features * columns + hidden * width),
            bytes_accessed=30000000,
            transcendentals=0,
        ),
        name="expert",
    )(received, w_up, partial, w_down)


def combine_kernel(x_ref, ninth_ref, w_ref, wlast_ref, resid_ref, out_ref, last):
    tokens, width = resid_ref.shape
    index = pl.program_id(0)

    @pl.when(index == 0)
    def _():
        last[...] = unfold(ninth_ref[...])

    own = last[:, pl.ds(pl.multiple_of(index * width, width), width)]
    both = f32dot(w_ref[...], x_ref[...]) + f32dot(wlast_ref[...], own)
    out_ref[...] = (resid_ref[...] + both[:tokens] + both[tokens:]).astype(jnp.bfloat16)


def combine(returned, weights, last_weights, resid):
    rows = returned.shape[0]
    tokens, features = resid.shape
    count = last_weights.shape[1]
    blocks = 2
    width = features // blocks
    return pl.pallas_call(
        combine_kernel,
        grid=(blocks,),
        in_specs=[
            pl.BlockSpec((rows, width), lambda i: (0, i)),
            pl.BlockSpec(
                (rows, features // GROUP), lambda i: (0, GROUP), pipeline_mode=pl.Buffered(1)
            ),
            whole_block((2 * tokens, rows)),
            whole_block((2 * tokens, count)),
            pl.BlockSpec((tokens, width), lambda i: (0, i)),
        ],
        out_specs=pl.BlockSpec((tokens, width), lambda i: (0, i)),
        out_shape=jax.ShapeDtypeStruct((tokens, features), jnp.bfloat16),
        scratch_shapes=[pltpu.VMEM((count, features), jnp.bfloat16)],
        compiler_params=params(),
        name="combine",
    )(returned, returned, weights, last_weights, resid)


def on_device(
    tokens,
    block_order,
    attn_gain,
    query_gain,
    key_gain,
    w_qkv,
    w_out,
    moe_gain,
    router,
    routes,
    w_gate_up,
    w_down,
):
    rows, model_width = tokens.shape
    size = query_gain.shape[0]
    ctx_size, exp_size = lax.axis_size("ctx"), lax.axis_size("exp")
    ctx_at, exp_at = lax.axis_index("ctx"), lax.axis_index("exp")
    ring = 4
    inner = exp_size // ring
    x_at, z_lo = ctx_at % ring, ctx_at // ring
    y_at, z_hi, core = exp_at // inner, exp_at // 2 % 2, exp_at % 2

    def device(z_lo, x, y, z_hi, core):
        return (z_lo * ring + x) * exp_size + y * inner + z_hi * 2 + core

    def bring(value, z_lo=0, x=0, y=0, z_hi=0, core=0):
        pairs = []
        for at in range(ctx_size * exp_size):
            c, e = at // exp_size, at % exp_size
            source = device(
                c // ring ^ z_lo,
                (c - x) % ring,
                (e // inner - y) % ring,
                e // 2 % 2 ^ z_hi,
                e % 2 ^ core,
            )
            pairs.append((source, at))
        return lax.ppermute(value, ("ctx", "exp"), pairs)

    def along_y(value):
        return jnp.concatenate([value] + [bring(value, y=k) for k in range(1, ring)])

    def along_x(values, step):
        return [values[0]] + [bring(values[k], x=step * k) for k in range(1, ring)]

    relative = jnp.arange(exp_size, dtype=jnp.int32)
    piece_of = (
        (core + relative) % 2 * (2 * ring)
        + (y_at - relative // inner) % ring * 2
        + (z_hi + relative // 2) % 2
    )
    relative = jnp.arange(2 * exp_size, dtype=jnp.int32)
    key_devices = device(
        (z_lo + relative) % 2,
        x_at,
        (y_at - relative // 4) % ring,
        (z_hi + relative // 2) % 2,
        (core + relative // (4 * ring)) % 2,
    )
    steps = jnp.arange(ring, dtype=jnp.int32)
    query_devices = device(z_lo, (x_at - steps) % ring, y_at, z_hi, core)

    def block_numbers(devices):
        every = jnp.arange(block_order.shape[0], dtype=jnp.int32)
        return jnp.sum(
            jnp.where(devices[:, None] == every[None, :], block_order[None, :], 0), axis=1
        )

    k_blocks = block_numbers(key_devices)
    q_blocks = block_numbers(query_devices)
    own_pos = q_blocks[0] * rows + jnp.arange(rows, dtype=jnp.int32)
    hide = jnp.repeat(
        jnp.where(k_blocks[None, :] > q_blocks[:, None], HIDDEN, 0.0), rows, axis=1
    )
    hide = jnp.pad(hide, ((0, size - ring), (0, 0))).astype(jnp.bfloat16)

    depth = model_width // ring
    widened = tokens.astype(jnp.float32)
    row_scale = lax.rsqrt(jnp.mean(widened * widened, axis=1, keepdims=True) + 1e-06)
    gained = (widened * attn_gain.astype(jnp.float32)).astype(jnp.bfloat16)
    w_share = lax.dynamic_slice_in_dim(w_qkv.T, x_at * depth, depth, 1)
    other, gained = lax.optimization_barrier((bring(w_share, z_hi=1), gained))
    near = along_y(jnp.stack([w_share, other]))
    shares = along_x(
        [
            lax.dynamic_slice_in_dim(gained, (x_at + k) % ring * depth, depth, 1)
            for k in range(ring)
        ],
        1,
    )
    w_out, near, shares = lax.optimization_barrier((w_out, near, shares))
    far = bring(near, core=1)
    w_out_all = lax.all_gather(w_out, "exp", axis=0, tiled=True)
    shares = project(shares, near, far, piece_of)
    shares, routes = lax.optimization_barrier((shares, routes))
    count = router.shape[1]
    pick, pick_last, named = slots(routes.T, count)
    half = size // 2
    freqs = jnp.exp(
        -math.log(rope_base) * jnp.arange(half, dtype=jnp.float32) * 2.0 / size
    )
    angles = own_pos.astype(jnp.float32)[:, None] * freqs[None, :]
    cos, sin = jnp.cos(angles), jnp.sin(angles)
    cos = jnp.concatenate([cos, cos], axis=1)
    sin = jnp.concatenate([-sin, sin], axis=1)
    parts = along_x(shares, -1)
    parts, pick, pick_last, named, hide, cos, sin = lax.optimization_barrier(
        (parts, pick, pick_last, named, hide, cos, sin)
    )
    heads = parts[0].shape[1] // size - 2
    queries, key_values = shape(parts, row_scale, query_gain, key_gain, cos, sin)
    others = [
        bring(key_values, z_lo=1),
        bring(key_values, z_hi=1),
        bring(key_values, z_lo=1, z_hi=1),
    ]
    others, left, right = lax.optimization_barrier(
        (others, bring(queries, x=1), bring(queries, x=ring - 1))
    )
    near = along_y(jnp.stack([key_values, *others])).reshape(-1, 2 * size)
    near, across = lax.optimization_barrier((near, bring(queries, x=2)))
    queries = [queries, left, across, right]
    far = bring(near, core=1)
    parts = along_x(attend(queries, near, far, hide, heads, size), -1)
    main = model_width // 4 * 3
    rest = model_width - main
    resid, moe_in, outgoing = finish(
        parts, w_out_all, tokens, moe_gain, pick, pick_last, heads, size, main
    )

    def exchange(x):
        wide = x.shape[1]
        x = lax.all_to_all(
            x.reshape(count, GROUP, wide), ("ctx", "exp"), split_axis=0, concat_axis=0, tiled=True
        )
        return x.reshape(count * GROUP, wide)

    first = exchange(outgoing)
    second = exchange(dispatch(moe_in, pick, pick_last, main // rest, rest))
    first, moe_in = lax.optimization_barrier((first, moe_in))
    weights, last_weights = weigh(moe_in, router, named, pick, pick_last)
    partial = up_first(first, w_gate_up, main)
    returned = exchange(expert(second, w_gate_up, partial, w_down, rest, main // rest))
    return combine(returned, weights, last_weights, resid)


def solution(mesh):
    return jax.shard_map(
        on_device,
        mesh=mesh,
        in_specs=(
            P(("ctx", "exp"), None),
            P(),
            P(),
            P(),
            P(),
            P(None, "exp"),
            P("exp", None),
            P(),
            P(),
            P(("ctx", "exp"), None),
            P(("ctx", "exp"), None, None),
            P(("ctx", "exp"), None, None),
        ),
        out_specs=P(("ctx", "exp"), None),
        check_vma=False,
    )
```

```python
import functools
import math

import jax
import jax.numpy as jnp
from jax import lax
from jax.experimental import pallas as pl
from jax.experimental.pallas import tpu as pltpu
from jax.sharding import PartitionSpec as P

rope_base = 1000000.0
GROUP = 8
VMEM_MB = 60
HIDDEN = -30000.0


def rms_scale(values, gain):
    widened = values.astype(jnp.float32)
    return (
        widened
        * lax.rsqrt(jnp.mean(widened * widened, axis=-1, keepdims=True) + 1e-06)
        * gain.astype(jnp.float32)
    )


def params(megabytes=VMEM_MB):
    return pltpu.CompilerParams(
        vmem_limit_bytes=megabytes * 1024 * 1024, dimension_semantics=("arbitrary",)
    )


def f32dot(a, b):
    return jnp.dot(a, b, preferred_element_type=jnp.float32)


def whole_block(shape):
    zeros = (0,) * len(shape)
    return pl.BlockSpec(shape, lambda *_: zeros, pipeline_mode=pl.Buffered(1))


def project_kernel(order_ref, *refs):
    ring = (len(refs) - 3) // 2
    x_refs, (near_ref, far_ref), out_refs, whole = (
        refs[:ring],
        refs[ring : ring + 2],
        refs[ring + 2 : -1],
        refs[-1],
    )
    half, columns = near_ref.shape[:2]
    rows = x_refs[0].shape[0]
    for e in range(2 * half):
        at = order_ref[e]
        near = near_ref[lax.rem(at, half)].astype(jnp.float32)
        far = far_ref[lax.rem(at, half)].astype(jnp.float32)
        whole[e * columns : (e + 1) * columns, :] = jnp.where(at < half, near, far).astype(
            jnp.bfloat16
        )
    x = jnp.concatenate([ref[...] for ref in x_refs], axis=0)
    out = lax.dot_general(
        x, whole[...], (((1,), (1,)), ((), ())), preferred_element_type=jnp.float32
    ).astype(jnp.bfloat16)
    for at, ref in enumerate(out_refs):
        ref[...] = out[at * rows : (at + 1) * rows]


def project(shares, near, far, order):
    rows, depth = shares[0].shape
    half, columns = near.shape[:2]
    out = jax.ShapeDtypeStruct((rows, 2 * half * columns), jnp.bfloat16)
    return pl.pallas_call(
        project_kernel,
        grid_spec=pltpu.PrefetchScalarGridSpec(
            num_scalar_prefetch=1,
            grid=(1,),
            in_specs=[whole_block(x.shape) for x in (*shares, near, far)],
            out_specs=[whole_block(out.shape)] * len(shares),
            scratch_shapes=[pltpu.VMEM((2 * half * columns, depth), jnp.bfloat16)],
        ),
        out_shape=[out] * len(shares),
        compiler_params=params(16),
        name="project",
    )(order, *shares, near, far)


def shape_kernel(heads, size, *refs):
    parts, (scale_ref, qgain_ref, kgain_ref, cos_ref, sin_ref, q_ref, kv_ref) = refs[:-7], refs[-7:]
    mixed = parts[0][...].astype(jnp.float32)
    for ref in parts[1:]:
        mixed = mixed + ref[...].astype(jnp.float32)
    mixed = mixed * scale_ref[...]
    half = size // 2

    def rope(values, gain):
        scale = lax.rsqrt(jnp.mean(values * values, axis=1, keepdims=True) + 1e-06)
        values = values * scale * gain.astype(jnp.float32)
        turned = jnp.concatenate([values[:, half:], values[:, :half]], axis=1)
        return values * cos_ref[...] + turned * sin_ref[...]

    for h in range(heads):
        part = slice(h * size, (h + 1) * size)
        q = rope(mixed[:, part], qgain_ref[...]) * (math.log2(math.e) / math.sqrt(size))
        q_ref[:, part] = q.astype(jnp.bfloat16)
    at = heads * size
    kv_ref[:, :size] = rope(mixed[:, at : at + size], kgain_ref[...]).astype(jnp.bfloat16)
    kv_ref[:, size:] = mixed[:, at + size :].astype(jnp.bfloat16)


def shape(parts, scale, query_gain, key_gain, cos, sin):
    rows, columns = parts[0].shape
    size = query_gain.shape[0]
    heads = columns // size - 2
    return pl.pallas_call(
        functools.partial(shape_kernel, heads, size),
        out_shape=[
            jax.ShapeDtypeStruct((rows, heads * size), jnp.bfloat16),
            jax.ShapeDtypeStruct((rows, 2 * size), jnp.bfloat16),
        ],
        compiler_params=pltpu.CompilerParams(vmem_limit_bytes=8 * 1024 * 1024),
        name="shape",
    )(*parts, scale, query_gain.reshape(1, -1), key_gain.reshape(1, -1), cos, sin)


def attend_kernel(heads, size, width, ring, last, *refs):
    q_refs, (kv_ref, hide_ref), refs = refs[:ring], refs[ring : ring + 2], refs[ring + 2 :]
    index = pl.program_id(0)
    rows = q_refs[0].shape[0]
    length = kv_ref.shape[0]
    before_ref, (held, keys, values) = refs[0] if last else None, refs[-3:]
    out_refs = refs[1:-3] if last else refs[:-3]

    @pl.when(index == 0)
    def _():
        for at, ref in enumerate(q_refs):
            held[at] = ref[...]
        keys[:size, :] = kv_ref[:, :size].T
        keys[size:, :] = hide_ref[...]
        values[:, :size] = kv_ref[:, size:]
        values[:, size:] = jnp.ones((length, size), jnp.bfloat16)

    mark = lax.broadcasted_iota(jnp.int32, (rows, size), 1) == index
    mark = jnp.where(mark, 1.0, 0.0).astype(jnp.bfloat16)
    row = lax.broadcasted_iota(jnp.int32, (rows, width), 0)
    key = lax.broadcasted_iota(jnp.int32, (rows, width), 1)
    later = (key > row) & (key < rows) & (index == 0)
    totals = []
    for h in range(heads):
        q = jnp.concatenate([held[index, :, h * size : (h + 1) * size], mark], axis=1)
        if last:
            total = before_ref[0, h]
        else:
            total = jnp.zeros((rows, 2 * size), jnp.float32)
        for start in range(0, length, width):
            part = pl.ds(start, width)
            scores = f32dot(q, keys[:, part])
            if start == 0 and not last:
                scores = jnp.where(later, HIDDEN, scores)
            total = total + f32dot(jnp.exp2(scores).astype(jnp.bfloat16), values[part, :])
        totals.append(total)
    if not last:
        for h in range(heads):
            out_refs[0][0, h] = totals[h]
        return
    lane = lax.broadcasted_iota(jnp.int32, (rows, size), 1)
    sums = jnp.zeros((rows, size), jnp.float32)
    results = []
    for h, total in enumerate(totals):
        results.append(total[:, :size].astype(jnp.bfloat16))
        high = total[:, size:].astype(jnp.bfloat16).astype(jnp.float32)
        sums = jnp.where(lane == 2 * h, high, sums)
        sums = jnp.where(lane == 2 * h + 1, total[:, size:] - high, sums)
    packed = jnp.concatenate([*results, sums.astype(jnp.bfloat16)], axis=1)
    for at, ref in enumerate(out_refs):

        @pl.when(index == at)
        def _(ref=ref):
            ref[...] = packed


def attend(queries, key_values, hide, before, heads, size):
    rows, columns = queries[0].shape
    ring = len(queries)
    length = key_values.shape[0]
    last = before is not None
    totals = (heads, rows, 2 * size)
    totals_spec = pl.BlockSpec((1, *totals), lambda i: (i, 0, 0, 0))
    in_specs = [whole_block(x.shape) for x in (*queries, key_values)]
    in_specs.append(
        pl.BlockSpec((size, length), lambda i: (0, int(last)), pipeline_mode=pl.Buffered(1))
    )
    operands = [*queries, key_values, hide]
    if last:
        in_specs.append(totals_spec)
        operands.append(before)
        out = jax.ShapeDtypeStruct((rows, columns + size), jnp.bfloat16)
        out_specs, out_shape = [whole_block(out.shape)] * ring, [out] * ring
    else:
        out_specs = totals_spec
        out_shape = jax.ShapeDtypeStruct((ring, *totals), jnp.float32)
    return pl.pallas_call(
        functools.partial(attend_kernel, heads, size, 512, ring, last),
        grid=(ring,),
        in_specs=in_specs,
        out_specs=out_specs,
        scratch_shapes=[
            pltpu.VMEM((ring, rows, columns), jnp.bfloat16),
            pltpu.VMEM((2 * size, length), jnp.bfloat16),
            pltpu.VMEM((length, 2 * size), jnp.bfloat16),
        ],
        out_shape=out_shape,
        compiler_params=params(20),
        cost_estimate=pl.CostEstimate(
            flops=16 * heads * rows * ring * length * size,
            bytes_accessed=8000000,
            transcendentals=heads * rows * ring * length,
        ),
        name="attend",
    )(*operands)


def repeat_rows(values):
    rows = values.shape[0]
    row = lax.broadcasted_iota(jnp.int32, (rows * GROUP, rows), 0)
    column = lax.broadcasted_iota(jnp.int32, (rows * GROUP, rows), 1)
    copies = (lax.div(row, GROUP) == column).astype(jnp.bfloat16)
    return f32dot(copies, values)


def slots_kernel(routes_ref, pick_ref, last_ref, named_ref):
    fanout, tokens = routes_ref.shape
    count = named_ref.shape[0]
    expert = lax.broadcasted_iota(jnp.int32, (count, tokens), 0)
    named = jnp.zeros((count, tokens), jnp.float32)
    for j in range(fanout):
        named = named + jnp.where(routes_ref[j : j + 1, :] == expert, 1.0, 0.0)
    earlier = lax.broadcasted_iota(jnp.int32, (tokens, tokens), 0)
    later = lax.broadcasted_iota(jnp.int32, (tokens, tokens), 1)
    before = (earlier < later).astype(jnp.bfloat16)
    rank = f32dot(named.astype(jnp.bfloat16), before)
    code = named * (rank + 1.0)
    named_ref[...] = named
    last_ref[...] = (code == GROUP + 1.0).astype(jnp.bfloat16)
    spread = repeat_rows(code.astype(jnp.bfloat16))
    slot = lax.rem(lax.broadcasted_iota(jnp.int32, spread.shape, 0), GROUP) + 1
    pick_ref[...] = (spread == slot.astype(jnp.float32)).astype(jnp.bfloat16)


def slots(routes_t, count):
    fanout, tokens = routes_t.shape
    return pl.pallas_call(
        slots_kernel,
        out_shape=[
            jax.ShapeDtypeStruct((count * GROUP, tokens), jnp.bfloat16),
            jax.ShapeDtypeStruct((count, tokens), jnp.bfloat16),
            jax.ShapeDtypeStruct((count, tokens), jnp.float32),
        ],
        compiler_params=pltpu.CompilerParams(vmem_limit_bytes=VMEM_MB * 1024 * 1024),
        name="slots",
    )(routes_t)


def weigh_kernel(x_ref, router_ref, named_ref, pick_ref, last_ref, out_ref, out_last_ref):
    tokens = x_ref.shape[0]
    logits = lax.dot_general(
        router_ref[...], x_ref[...], (((0,), (1,)), ((), ())), preferred_element_type=jnp.float32
    )
    named = named_ref[...] > 0.5
    largest = jnp.max(jnp.where(named, logits, -jnp.inf), axis=0, keepdims=True)
    shares = jnp.where(named, jnp.exp(jnp.minimum(logits - largest, 0.0)), 0.0)
    shares = shares / jnp.sum(shares, axis=0, keepdims=True)
    high = shares.astype(jnp.bfloat16)
    low = (shares - high.astype(jnp.float32)).astype(jnp.bfloat16)
    for at, part in ((0, high), (tokens, low)):
        out_ref[at : at + tokens, :] = (repeat_rows(part).astype(jnp.bfloat16) * pick_ref[...]).T
        out_last_ref[at : at + tokens, :] = (part * last_ref[...]).T


def weigh(moe_in, router, named, pick, last):
    tokens = moe_in.shape[0]
    return pl.pallas_call(
        weigh_kernel,
        out_shape=[
            jax.ShapeDtypeStruct((2 * tokens, pick.shape[0]), jnp.bfloat16),
            jax.ShapeDtypeStruct((2 * tokens, last.shape[0]), jnp.bfloat16),
        ],
        compiler_params=pltpu.CompilerParams(vmem_limit_bytes=VMEM_MB * 1024 * 1024),
        name="weigh",
    )(moe_in, router, named, pick, last)


def fold(rows):
    count, features = rows.shape
    return rows.reshape(count, GROUP, features // GROUP).reshape(count * GROUP, features // GROUP)


def unfold(rows):
    count, piece = rows.shape
    return rows.reshape(count // GROUP, GROUP, piece).reshape(count // GROUP, GROUP * piece)


def fill(out_ref, x, pick, last):
    features = x.shape[1]
    out_ref[:, :features] = f32dot(pick, x).astype(jnp.bfloat16)
    out_ref[:, features:] = fold(f32dot(last, x).astype(jnp.bfloat16))


def finish_kernel(
    heads,
    size,
    features,
    *refs,
):
    parts_refs, refs = refs[:-12], refs[-12:]
    w_ref, x_ref, gain_ref, pick_ref, last_ref, resid_hbm, norm_hbm, out_ref = refs[:8]
    resid_ref, norm_ref, resid_sent, norm_sent = refs[8:]
    copies = (
        pltpu.make_async_copy(resid_ref, resid_hbm, resid_sent),
        pltpu.make_async_copy(norm_ref, norm_hbm, norm_sent),
    )

    @pl.when(pl.program_id(0) == 0)
    def _():
        summed = parts_refs[0][...].astype(jnp.float32)
        for ref in parts_refs[1:]:
            summed = summed + ref[...].astype(jnp.float32)
        base = heads * size
        attended = []
        for h in range(heads):
            at = base + 2 * h
            total = summed[:, at : at + 1] + summed[:, at + 1 : at + 2]
            attended.append((summed[:, h * size : (h + 1) * size] / total).astype(jnp.bfloat16))
        projected = f32dot(jnp.concatenate(attended, axis=1), w_ref[...])
        resid = x_ref[...].astype(jnp.float32) + projected
        resid_ref[...] = resid
        scale = lax.rsqrt(jnp.mean(resid * resid, axis=1, keepdims=True) + 1e-06)
        norm_ref[...] = (resid * scale * gain_ref[...].astype(jnp.float32)).astype(jnp.bfloat16)
        for copy in copies:
            copy.start()

    fill(out_ref, norm_ref[:, :features], pick_ref[...], last_ref[...])

    @pl.when(pl.program_id(0) == pl.num_programs(0) - 1)
    def _():
        for copy in copies:
            copy.wait()


def finish(parts, w_out, tokens, gain, pick, last, heads, size, features):
    rows, count = pick.shape[0], last.shape[0]
    wide = features + features // GROUP
    blocks = 4
    return pl.pallas_call(
        functools.partial(finish_kernel, heads, size, features),
        grid=(blocks,),
        in_specs=[
            *(whole_block(x.shape) for x in parts),
            whole_block(w_out.shape),
            whole_block(tokens.shape),
            whole_block((1, gain.shape[0])),
            pl.BlockSpec((rows // blocks, pick.shape[1]), lambda i: (i, 0)),
            pl.BlockSpec((count // blocks, pick.shape[1]), lambda i: (i, 0)),
        ],
        out_specs=[
            pl.BlockSpec(memory_space=pl.ANY),
            pl.BlockSpec(memory_space=pl.ANY),
            pl.BlockSpec((rows // blocks, wide), lambda i: (i, 0)),
        ],
        scratch_shapes=[
            pltpu.VMEM(tokens.shape, jnp.float32),
            pltpu.VMEM(tokens.shape, jnp.bfloat16),
            pltpu.SemaphoreType.DMA(()),
            pltpu.SemaphoreType.DMA(()),
        ],
        out_shape=[
            jax.ShapeDtypeStruct(tokens.shape, jnp.float32),
            jax.ShapeDtypeStruct(tokens.shape, jnp.bfloat16),
            jax.ShapeDtypeStruct((rows, wide), jnp.bfloat16),
        ],
        compiler_params=params(57),
        name="finish",
    )(*parts, w_out, tokens, gain.reshape(1, -1), pick, last)


def dispatch_kernel(x_ref, pick_ref, last_ref, out_ref):
    fill(out_ref, x_ref[...], pick_ref[...], last_ref[...])


def dispatch(normed, pick, last, chunk, features):
    rows, tokens = pick.shape
    count = last.shape[0]
    wide = features + features // GROUP
    blocks = 4
    return pl.pallas_call(
        dispatch_kernel,
        grid=(blocks,),
        in_specs=[
            pl.BlockSpec((tokens, features), lambda i: (0, chunk)),
            pl.BlockSpec((rows // blocks, tokens), lambda i: (i, 0)),
            pl.BlockSpec((count // blocks, tokens), lambda i: (i, 0)),
        ],
        out_specs=pl.BlockSpec((rows // blocks, wide), lambda i: (i, 0)),
        out_shape=jax.ShapeDtypeStruct((rows, wide), jnp.bfloat16),
        compiler_params=params(),
        cost_estimate=pl.CostEstimate(
            flops=4 * rows * tokens * features, bytes_accessed=4 * rows * features, transcendentals=0
        ),
        name="dispatch",
    )(normed, pick, last)


def all_rows(x_ref, features):
    return jnp.concatenate([x_ref[:, :features], unfold(x_ref[:, features:])], axis=0)


def up_kernel(features, x_ref, w_ref, out_ref):
    out_ref[...] = f32dot(all_rows(x_ref, features), w_ref[0])


def up_first(received, weights, features):
    rows, wide = received.shape
    columns = weights.shape[2]
    blocks = 4
    taken = rows // blocks * (GROUP + 1) // GROUP
    return pl.pallas_call(
        functools.partial(up_kernel, features),
        grid=(blocks,),
        in_specs=[
            pl.BlockSpec((rows // blocks, wide), lambda i: (i, 0)),
            pl.BlockSpec(
                (1, features, columns), lambda i: (0, 0, 0), pipeline_mode=pl.Buffered(1)
            ),
        ],
        out_specs=pl.BlockSpec((taken, columns), lambda i: (i, 0)),
        out_shape=jax.ShapeDtypeStruct((taken * blocks, columns), jnp.float32),
        compiler_params=params(),
        cost_estimate=pl.CostEstimate(
            flops=2 * rows * features * columns, bytes_accessed=20000000, transcendentals=0
        ),
        name="up_first",
    )(received, weights)


def expert_kernel(
    features, x_ref, wu_ref, partial_ref, wd_hbm, out_ref, wd, arrived
):
    index = pl.program_id(0)
    copy = pltpu.make_async_copy(wd_hbm.at[0], wd, arrived)

    @pl.when(index == 0)
    def _():
        copy.start()

    gate_up = partial_ref[...] + f32dot(all_rows(x_ref, features), wu_ref[0])
    hidden = gate_up.shape[1] // 2
    gate = gate_up[:, :hidden]
    active = (gate / (1.0 + jnp.exp(-gate)) * gate_up[:, hidden:]).astype(jnp.bfloat16)

    @pl.when(index == 0)
    def _():
        copy.wait()

    rows = x_ref.shape[0]
    out = f32dot(active, wd[...])
    out_ref[:, : wd.shape[1]] = out[:rows].astype(jnp.bfloat16)
    out_ref[:, wd.shape[1] :] = fold(out[rows:].astype(jnp.bfloat16))


def expert(received, w_up, partial, w_down, features, chunk):
    rows, wide = received.shape
    columns = w_up.shape[2]
    hidden, width = w_down.shape[1:]
    blocks = 4
    taken = rows // blocks * (GROUP + 1) // GROUP
    out_wide = width + width // GROUP
    return pl.pallas_call(
        functools.partial(expert_kernel, features),
        grid=(blocks,),
        in_specs=[
            pl.BlockSpec((rows // blocks, wide), lambda i: (i, 0)),
            pl.BlockSpec(
                (1, features, columns), lambda i: (0, chunk, 0), pipeline_mode=pl.Buffered(1)
            ),
            pl.BlockSpec((taken, columns), lambda i: (i, 0)),
            pl.BlockSpec(memory_space=pl.ANY),
        ],
        out_specs=pl.BlockSpec((rows // blocks, out_wide), lambda i: (i, 0)),
        out_shape=jax.ShapeDtypeStruct((rows, out_wide), jnp.bfloat16),
        scratch_shapes=[pltpu.VMEM((hidden, width), jnp.bfloat16), pltpu.SemaphoreType.DMA(())],
        compiler_params=params(55),
        cost_estimate=pl.CostEstimate(
            flops=2 * rows * (features * columns + hidden * width),
            bytes_accessed=30000000,
            transcendentals=0,
        ),
        name="expert",
    )(received, w_up, partial, w_down)


def combine_kernel(x_ref, ninth_ref, w_ref, wlast_ref, resid_ref, out_ref, last):
    tokens, width = resid_ref.shape
    index = pl.program_id(0)

    @pl.when(index == 0)
    def _():
        last[...] = unfold(ninth_ref[...])

    own = last[:, pl.ds(pl.multiple_of(index * width, width), width)]
    both = f32dot(w_ref[...], x_ref[...]) + f32dot(wlast_ref[...], own)
    out_ref[...] = (resid_ref[...] + both[:tokens] + both[tokens:]).astype(jnp.bfloat16)


def combine(returned, weights, last_weights, resid):
    rows = returned.shape[0]
    tokens, features = resid.shape
    count = last_weights.shape[1]
    blocks = 2
    width = features // blocks
    return pl.pallas_call(
        combine_kernel,
        grid=(blocks,),
        in_specs=[
            pl.BlockSpec((rows, width), lambda i: (0, i)),
            pl.BlockSpec(
                (rows, features // GROUP), lambda i: (0, GROUP), pipeline_mode=pl.Buffered(1)
            ),
            whole_block((2 * tokens, rows)),
            whole_block((2 * tokens, count)),
            pl.BlockSpec((tokens, width), lambda i: (0, i)),
        ],
        out_specs=pl.BlockSpec((tokens, width), lambda i: (0, i)),
        out_shape=jax.ShapeDtypeStruct((tokens, features), jnp.bfloat16),
        scratch_shapes=[pltpu.VMEM((count, features), jnp.bfloat16)],
        compiler_params=params(),
        name="combine",
    )(returned, returned, weights, last_weights, resid)


def on_device(
    tokens,
    block_order,
    attn_gain,
    query_gain,
    key_gain,
    w_qkv,
    w_out,
    moe_gain,
    router,
    routes,
    w_gate_up,
    w_down,
):
    rows, model_width = tokens.shape
    size = query_gain.shape[0]
    ctx_size, exp_size = lax.axis_size("ctx"), lax.axis_size("exp")
    ctx_at, exp_at = lax.axis_index("ctx"), lax.axis_index("exp")
    ring = 4
    inner = exp_size // ring
    x_at, z_lo = ctx_at % ring, ctx_at // ring
    y_at, z_hi, core = exp_at // inner, exp_at // 2 % 2, exp_at % 2

    def device(z_lo, x, y, z_hi, core):
        return (z_lo * ring + x) * exp_size + y * inner + z_hi * 2 + core

    def bring(value, z_lo=0, x=0, y=0, z_hi=0, core=0):
        pairs = []
        for at in range(ctx_size * exp_size):
            c, e = at // exp_size, at % exp_size
            source = device(
                c // ring ^ z_lo,
                (c - x) % ring,
                (e // inner - y) % ring,
                e // 2 % 2 ^ z_hi,
                e % 2 ^ core,
            )
            pairs.append((source, at))
        return lax.ppermute(value, ("ctx", "exp"), pairs)

    def along_y(value):
        return jnp.concatenate([value] + [bring(value, y=k) for k in range(1, ring)])

    def along_x(values, step):
        return [values[0]] + [bring(values[k], x=step * k) for k in range(1, ring)]

    relative = jnp.arange(exp_size, dtype=jnp.int32)
    piece_of = (
        (core + relative) % 2 * (2 * ring)
        + (y_at - relative // inner) % ring * 2
        + (z_hi + relative // 2) % 2
    )
    relative = jnp.arange(2 * exp_size, dtype=jnp.int32)
    key_devices = device(
        (z_lo + relative) % 2,
        x_at,
        (y_at - relative // 4) % ring,
        (z_hi + relative // 2) % 2,
        (core + relative // (4 * ring)) % 2,
    )
    steps = jnp.arange(ring, dtype=jnp.int32)
    query_devices = device(z_lo, (x_at - steps) % ring, y_at, z_hi, core)

    def block_numbers(devices):
        every = jnp.arange(block_order.shape[0], dtype=jnp.int32)
        return jnp.sum(
            jnp.where(devices[:, None] == every[None, :], block_order[None, :], 0), axis=1
        )

    k_blocks = block_numbers(key_devices)
    q_blocks = block_numbers(query_devices)
    own_pos = q_blocks[0] * rows + jnp.arange(rows, dtype=jnp.int32)
    hide = jnp.repeat(
        jnp.where(k_blocks[None, :] > q_blocks[:, None], HIDDEN, 0.0), rows, axis=1
    )
    hide = jnp.pad(hide, ((0, size - ring), (0, 0))).astype(jnp.bfloat16)

    depth = model_width // ring
    widened = tokens.astype(jnp.float32)
    row_scale = lax.rsqrt(jnp.mean(widened * widened, axis=1, keepdims=True) + 1e-06)
    gained = (widened * attn_gain.astype(jnp.float32)).astype(jnp.bfloat16)
    w_share = lax.dynamic_slice_in_dim(w_qkv.T, x_at * depth, depth, 1)
    other, gained = lax.optimization_barrier((bring(w_share, z_hi=1), gained))
    near = along_y(jnp.stack([w_share, other]))
    shares = along_x(
        [
            lax.dynamic_slice_in_dim(gained, (x_at + k) % ring * depth, depth, 1)
            for k in range(ring)
        ],
        1,
    )
    w_out, near, shares = lax.optimization_barrier((w_out, near, shares))
    far = bring(near, core=1)
    w_out_all = lax.all_gather(w_out, "exp", axis=0, tiled=True)
    shares = project(shares, near, far, piece_of)
    shares, routes = lax.optimization_barrier((shares, routes))
    count = router.shape[1]
    pick, pick_last, named = slots(routes.T, count)
    half = size // 2
    freqs = jnp.exp(
        -math.log(rope_base) * jnp.arange(half, dtype=jnp.float32) * 2.0 / size
    )
    angles = own_pos.astype(jnp.float32)[:, None] * freqs[None, :]
    cos, sin = jnp.cos(angles), jnp.sin(angles)
    cos = jnp.concatenate([cos, cos], axis=1)
    sin = jnp.concatenate([-sin, sin], axis=1)
    parts = along_x(shares, -1)
    parts, pick, pick_last, named, hide, cos, sin = lax.optimization_barrier(
        (parts, pick, pick_last, named, hide, cos, sin)
    )
    heads = parts[0].shape[1] // size - 2
    queries, key_values = shape(parts, row_scale, query_gain, key_gain, cos, sin)
    others = [
        bring(key_values, z_lo=1),
        bring(key_values, z_hi=1),
        bring(key_values, z_lo=1, z_hi=1),
    ]
    others, left, right = lax.optimization_barrier(
        (others, bring(queries, x=1), bring(queries, x=ring - 1))
    )
    near = along_y(jnp.stack([key_values, *others])).reshape(-1, 2 * size)
    near, across = lax.optimization_barrier((near, bring(queries, x=2)))
    queries = [queries, left, across, right]
    far = bring(near, core=1)
    totals = attend(queries, near, hide, None, heads, size)
    parts = along_x(attend(queries, far, hide, totals, heads, size), -1)
    main = model_width // 4 * 3
    rest = model_width - main
    resid, moe_in, outgoing = finish(
        parts, w_out_all, tokens, moe_gain, pick, pick_last, heads, size, main
    )

    def exchange(x):
        wide = x.shape[1]
        x = lax.all_to_all(
            x.reshape(count, GROUP, wide), ("ctx", "exp"), split_axis=0, concat_axis=0, tiled=True
        )
        return x.reshape(count * GROUP, wide)

    first = exchange(outgoing)
    second = exchange(dispatch(moe_in, pick, pick_last, main // rest, rest))
    first, moe_in = lax.optimization_barrier((first, moe_in))
    weights, last_weights = weigh(moe_in, router, named, pick, pick_last)
    partial = up_first(first, w_gate_up, main)
    returned = exchange(expert(second, w_gate_up, partial, w_down, rest, main // rest))
    return combine(returned, weights, last_weights, resid)


def solution(mesh):
    return jax.shard_map(
        on_device,
        mesh=mesh,
        in_specs=(
            P(("ctx", "exp"), None),
            P(),
            P(),
            P(),
            P(),
            P(None, "exp"),
            P("exp", None),
            P(),
            P(),
            P(("ctx", "exp"), None),
            P(("ctx", "exp"), None, None),
            P(("ctx", "exp"), None, None),
        ),
        out_specs=P(("ctx", "exp"), None),
        check_vma=False,
    )
```

```python
import functools
import math

import jax
import jax.numpy as jnp
from jax import lax
from jax.experimental import pallas as pl
from jax.experimental.pallas import tpu as pltpu
from jax.sharding import PartitionSpec as P

rope_base = 1000000.0
GROUP = 8
VMEM_MB = 60
HIDDEN = -30000.0


def rms_scale(values, gain):
    widened = values.astype(jnp.float32)
    return (
        widened
        * lax.rsqrt(jnp.mean(widened * widened, axis=-1, keepdims=True) + 1e-06)
        * gain.astype(jnp.float32)
    )


def params(megabytes=VMEM_MB):
    return pltpu.CompilerParams(
        vmem_limit_bytes=megabytes * 1024 * 1024, dimension_semantics=("arbitrary",)
    )


def f32dot(a, b):
    return jnp.dot(a, b, preferred_element_type=jnp.float32)


def whole_block(shape):
    zeros = (0,) * len(shape)
    return pl.BlockSpec(shape, lambda *_: zeros, pipeline_mode=pl.Buffered(1))


def project_kernel(order_ref, *refs):
    ring = (len(refs) - 3) // 2
    x_refs, (near_ref, far_ref), out_refs, whole = (
        refs[:ring],
        refs[ring : ring + 2],
        refs[ring + 2 : -1],
        refs[-1],
    )
    half, columns = near_ref.shape[:2]
    rows = x_refs[0].shape[0]
    for e in range(2 * half):
        at = order_ref[e]
        near = near_ref[lax.rem(at, half)].astype(jnp.float32)
        far = far_ref[lax.rem(at, half)].astype(jnp.float32)
        whole[e * columns : (e + 1) * columns, :] = jnp.where(at < half, near, far).astype(
            jnp.bfloat16
        )
    x = jnp.concatenate([ref[...] for ref in x_refs], axis=0)
    out = lax.dot_general(
        x, whole[...], (((1,), (1,)), ((), ())), preferred_element_type=jnp.float32
    ).astype(jnp.bfloat16)
    for at, ref in enumerate(out_refs):
        ref[...] = out[at * rows : (at + 1) * rows]


def project(shares, near, far, order):
    rows, depth = shares[0].shape
    half, columns = near.shape[:2]
    out = jax.ShapeDtypeStruct((rows, 2 * half * columns), jnp.bfloat16)
    return pl.pallas_call(
        project_kernel,
        grid_spec=pltpu.PrefetchScalarGridSpec(
            num_scalar_prefetch=1,
            grid=(1,),
            in_specs=[whole_block(x.shape) for x in (*shares, near, far)],
            out_specs=[whole_block(out.shape)] * len(shares),
            scratch_shapes=[pltpu.VMEM((2 * half * columns, depth), jnp.bfloat16)],
        ),
        out_shape=[out] * len(shares),
        compiler_params=params(16),
        name="project",
    )(order, *shares, near, far)


def shape_kernel(heads, size, *refs):
    parts, (scale_ref, qgain_ref, kgain_ref, cos_ref, sin_ref, q_ref, kv_ref) = refs[:-7], refs[-7:]
    mixed = parts[0][...].astype(jnp.float32)
    for ref in parts[1:]:
        mixed = mixed + ref[...].astype(jnp.float32)
    mixed = mixed * scale_ref[...]
    half = size // 2

    def rope(values, gain):
        scale = lax.rsqrt(jnp.mean(values * values, axis=1, keepdims=True) + 1e-06)
        values = values * scale * gain.astype(jnp.float32)
        turned = jnp.concatenate([values[:, half:], values[:, :half]], axis=1)
        return values * cos_ref[...] + turned * sin_ref[...]

    for h in range(heads):
        part = slice(h * size, (h + 1) * size)
        q = rope(mixed[:, part], qgain_ref[...]) * (math.log2(math.e) / math.sqrt(size))
        q_ref[:, part] = q.astype(jnp.bfloat16)
    at = heads * size
    kv_ref[:, :size] = rope(mixed[:, at : at + size], kgain_ref[...]).astype(jnp.bfloat16)
    kv_ref[:, size:] = mixed[:, at + size :].astype(jnp.bfloat16)


def shape(parts, scale, query_gain, key_gain, cos, sin):
    rows, columns = parts[0].shape
    size = query_gain.shape[0]
    heads = columns // size - 2
    return pl.pallas_call(
        functools.partial(shape_kernel, heads, size),
        out_shape=[
            jax.ShapeDtypeStruct((rows, heads * size), jnp.bfloat16),
            jax.ShapeDtypeStruct((rows, 2 * size), jnp.bfloat16),
        ],
        compiler_params=pltpu.CompilerParams(vmem_limit_bytes=8 * 1024 * 1024),
        name="shape",
    )(*parts, scale, query_gain.reshape(1, -1), key_gain.reshape(1, -1), cos, sin)


def attend_kernel(heads, size, width, ring, last, *refs):
    q_refs, (kv_ref, hide_ref), refs = refs[:ring], refs[ring : ring + 2], refs[ring + 2 :]
    index = pl.program_id(0)
    rows = q_refs[0].shape[0]
    length = kv_ref.shape[0]
    before_ref, (held, keys, values) = refs[0] if last else None, refs[-3:]
    out_refs = refs[1:-3] if last else refs[:-3]

    @pl.when(index == 0)
    def _():
        for at, ref in enumerate(q_refs):
            held[at] = ref[...]
        keys[:size, :] = kv_ref[:, :size].T
        keys[size:, :] = hide_ref[...]
        values[:, :size] = kv_ref[:, size:]
        values[:, size:] = jnp.ones((length, size), jnp.bfloat16)

    mark = lax.broadcasted_iota(jnp.int32, (rows, size), 1) == index
    mark = jnp.where(mark, 1.0, 0.0).astype(jnp.bfloat16)
    row = lax.broadcasted_iota(jnp.int32, (rows, width), 0)
    key = lax.broadcasted_iota(jnp.int32, (rows, width), 1)
    later = (key > row) & (key < rows) & (index == 0)
    totals = []
    for h in range(heads):
        q = jnp.concatenate([held[index, :, h * size : (h + 1) * size], mark], axis=1)
        if last:
            total = before_ref[0, h]
        else:
            total = jnp.zeros((rows, 2 * size), jnp.float32)
        for start in range(0, length, width):
            part = pl.ds(start, width)
            scores = f32dot(q, keys[:, part])
            if start == 0 and not last:
                scores = jnp.where(later, HIDDEN, scores)
            total = total + f32dot(jnp.exp2(scores).astype(jnp.bfloat16), values[part, :])
        totals.append(total)
    if not last:
        for h in range(heads):
            out_refs[0][0, h] = totals[h]
        return
    lane = lax.broadcasted_iota(jnp.int32, (rows, size), 1)
    sums = jnp.zeros((rows, size), jnp.float32)
    results = []
    for h, total in enumerate(totals):
        results.append(total[:, :size].astype(jnp.bfloat16))
        high = total[:, size:].astype(jnp.bfloat16).astype(jnp.float32)
        sums = jnp.where(lane == 2 * h, high, sums)
        sums = jnp.where(lane == 2 * h + 1, total[:, size:] - high, sums)
    packed = jnp.concatenate([*results, sums.astype(jnp.bfloat16)], axis=1)
    for at, ref in enumerate(out_refs):

        @pl.when(index == at)
        def _(ref=ref):
            ref[...] = packed


def attend(queries, key_values, hide, before, heads, size):
    rows, columns = queries[0].shape
    ring = len(queries)
    length = key_values.shape[0]
    last = before is not None
    totals = (heads, rows, 2 * size)
    totals_spec = pl.BlockSpec((1, *totals), lambda i: (i, 0, 0, 0))
    in_specs = [whole_block(x.shape) for x in (*queries, key_values)]
    in_specs.append(
        pl.BlockSpec((size, length), lambda i: (0, int(last)), pipeline_mode=pl.Buffered(1))
    )
    operands = [*queries, key_values, hide]
    if last:
        in_specs.append(totals_spec)
        operands.append(before)
        out = jax.ShapeDtypeStruct((rows, columns + size), jnp.bfloat16)
        out_specs, out_shape = [whole_block(out.shape)] * ring, [out] * ring
    else:
        out_specs = totals_spec
        out_shape = jax.ShapeDtypeStruct((ring, *totals), jnp.float32)
    return pl.pallas_call(
        functools.partial(attend_kernel, heads, size, 512, ring, last),
        grid=(ring,),
        in_specs=in_specs,
        out_specs=out_specs,
        scratch_shapes=[
            pltpu.VMEM((ring, rows, columns), jnp.bfloat16),
            pltpu.VMEM((2 * size, length), jnp.bfloat16),
            pltpu.VMEM((length, 2 * size), jnp.bfloat16),
        ],
        out_shape=out_shape,
        compiler_params=params(20),
        cost_estimate=pl.CostEstimate(
            flops=16 * heads * rows * ring * length * size,
            bytes_accessed=8000000,
            transcendentals=heads * rows * ring * length,
        ),
        name="attend",
    )(*operands)


def repeat_rows(values):
    rows = values.shape[0]
    row = lax.broadcasted_iota(jnp.int32, (rows * GROUP, rows), 0)
    column = lax.broadcasted_iota(jnp.int32, (rows * GROUP, rows), 1)
    copies = (lax.div(row, GROUP) == column).astype(jnp.bfloat16)
    return f32dot(copies, values)


def slots_kernel(routes_ref, pick_ref, last_ref, named_ref):
    fanout, tokens = routes_ref.shape
    count = named_ref.shape[0]
    expert = lax.broadcasted_iota(jnp.int32, (count, tokens), 0)
    named = jnp.zeros((count, tokens), jnp.float32)
    for j in range(fanout):
        named = named + jnp.where(routes_ref[j : j + 1, :] == expert, 1.0, 0.0)
    earlier = lax.broadcasted_iota(jnp.int32, (tokens, tokens), 0)
    later = lax.broadcasted_iota(jnp.int32, (tokens, tokens), 1)
    before = (earlier < later).astype(jnp.bfloat16)
    rank = f32dot(named.astype(jnp.bfloat16), before)
    code = named * (rank + 1.0)
    named_ref[...] = named
    last_ref[...] = (code == GROUP + 1.0).astype(jnp.bfloat16)
    spread = repeat_rows(code.astype(jnp.bfloat16))
    slot = lax.rem(lax.broadcasted_iota(jnp.int32, spread.shape, 0), GROUP) + 1
    pick_ref[...] = (spread == slot.astype(jnp.float32)).astype(jnp.bfloat16)


def slots(routes_t, count):
    fanout, tokens = routes_t.shape
    return pl.pallas_call(
        slots_kernel,
        out_shape=[
            jax.ShapeDtypeStruct((count * GROUP, tokens), jnp.bfloat16),
            jax.ShapeDtypeStruct((count, tokens), jnp.bfloat16),
            jax.ShapeDtypeStruct((count, tokens), jnp.float32),
        ],
        compiler_params=pltpu.CompilerParams(vmem_limit_bytes=VMEM_MB * 1024 * 1024),
        name="slots",
    )(routes_t)


def weigh_kernel(x_ref, router_ref, named_ref, pick_ref, last_ref, out_ref, out_last_ref):
    tokens = x_ref.shape[0]
    logits = lax.dot_general(
        router_ref[...], x_ref[...], (((0,), (1,)), ((), ())), preferred_element_type=jnp.float32
    )
    named = named_ref[...] > 0.5
    largest = jnp.max(jnp.where(named, logits, -jnp.inf), axis=0, keepdims=True)
    shares = jnp.where(named, jnp.exp(jnp.minimum(logits - largest, 0.0)), 0.0)
    shares = shares / jnp.sum(shares, axis=0, keepdims=True)
    high = shares.astype(jnp.bfloat16)
    low = (shares - high.astype(jnp.float32)).astype(jnp.bfloat16)
    for at, part in ((0, high), (tokens, low)):
        out_ref[at : at + tokens, :] = (repeat_rows(part).astype(jnp.bfloat16) * pick_ref[...]).T
        out_last_ref[at : at + tokens, :] = (part * last_ref[...]).T


def weigh(moe_in, router, named, pick, last):
    tokens = moe_in.shape[0]
    return pl.pallas_call(
        weigh_kernel,
        out_shape=[
            jax.ShapeDtypeStruct((2 * tokens, pick.shape[0]), jnp.bfloat16),
            jax.ShapeDtypeStruct((2 * tokens, last.shape[0]), jnp.bfloat16),
        ],
        compiler_params=pltpu.CompilerParams(vmem_limit_bytes=VMEM_MB * 1024 * 1024),
        name="weigh",
    )(moe_in, router, named, pick, last)


def fold(rows):
    count, features = rows.shape
    return rows.reshape(count, GROUP, features // GROUP).reshape(count * GROUP, features // GROUP)


def unfold(rows):
    count, piece = rows.shape
    return rows.reshape(count // GROUP, GROUP, piece).reshape(count // GROUP, GROUP * piece)


def finish_kernel(
    heads,
    size,
    features,
    *refs,
):
    parts_refs, refs = refs[:-12], refs[-12:]
    w_ref, x_ref, gain_ref, pick_ref, last_ref, resid_hbm, norm_hbm, out_ref = refs[:8]
    resid_ref, norm_ref, resid_sent, norm_sent = refs[8:]
    copies = (
        pltpu.make_async_copy(resid_ref, resid_hbm, resid_sent),
        pltpu.make_async_copy(norm_ref, norm_hbm, norm_sent),
    )

    @pl.when(pl.program_id(0) == 0)
    def _():
        summed = parts_refs[0][...].astype(jnp.float32)
        for ref in parts_refs[1:]:
            summed = summed + ref[...].astype(jnp.float32)
        base = heads * size
        attended = []
        for h in range(heads):
            at = base + 2 * h
            total = summed[:, at : at + 1] + summed[:, at + 1 : at + 2]
            attended.append((summed[:, h * size : (h + 1) * size] / total).astype(jnp.bfloat16))
        projected = f32dot(jnp.concatenate(attended, axis=1), w_ref[...])
        resid = x_ref[...].astype(jnp.float32) + projected
        resid_ref[...] = resid
        scale = lax.rsqrt(jnp.mean(resid * resid, axis=1, keepdims=True) + 1e-06)
        norm_ref[...] = (resid * scale * gain_ref[...].astype(jnp.float32)).astype(jnp.bfloat16)
        for copy in copies:
            copy.start()

    out_ref[:, :features] = f32dot(pick_ref[...], norm_ref[:, :features]).astype(jnp.bfloat16)
    out_ref[:, features:] = fold(f32dot(last_ref[...], norm_ref[...]).astype(jnp.bfloat16))

    @pl.when(pl.program_id(0) == pl.num_programs(0) - 1)
    def _():
        for copy in copies:
            copy.wait()


def finish(parts, w_out, tokens, gain, pick, last, heads, size, features):
    rows, count = pick.shape[0], last.shape[0]
    wide = features + tokens.shape[1] // GROUP
    blocks = 4
    return pl.pallas_call(
        functools.partial(finish_kernel, heads, size, features),
        grid=(blocks,),
        in_specs=[
            *(whole_block(x.shape) for x in parts),
            whole_block(w_out.shape),
            whole_block(tokens.shape),
            whole_block((1, gain.shape[0])),
            pl.BlockSpec((rows // blocks, pick.shape[1]), lambda i: (i, 0)),
            pl.BlockSpec((count // blocks, pick.shape[1]), lambda i: (i, 0)),
        ],
        out_specs=[
            pl.BlockSpec(memory_space=pl.ANY),
            pl.BlockSpec(memory_space=pl.ANY),
            pl.BlockSpec((rows // blocks, wide), lambda i: (i, 0)),
        ],
        scratch_shapes=[
            pltpu.VMEM(tokens.shape, jnp.float32),
            pltpu.VMEM(tokens.shape, jnp.bfloat16),
            pltpu.SemaphoreType.DMA(()),
            pltpu.SemaphoreType.DMA(()),
        ],
        out_shape=[
            jax.ShapeDtypeStruct(tokens.shape, jnp.float32),
            jax.ShapeDtypeStruct(tokens.shape, jnp.bfloat16),
            jax.ShapeDtypeStruct((rows, wide), jnp.bfloat16),
        ],
        compiler_params=params(57),
        name="finish",
    )(*parts, w_out, tokens, gain.reshape(1, -1), pick, last)


def dispatch_kernel(x_ref, pick_ref, out_ref):
    out_ref[...] = f32dot(pick_ref[...], x_ref[...]).astype(jnp.bfloat16)


def dispatch(normed, pick, chunk, features):
    rows, tokens = pick.shape
    blocks = 4
    return pl.pallas_call(
        dispatch_kernel,
        grid=(blocks,),
        in_specs=[
            pl.BlockSpec((tokens, features), lambda i: (0, chunk)),
            pl.BlockSpec((rows // blocks, tokens), lambda i: (i, 0)),
        ],
        out_specs=pl.BlockSpec((rows // blocks, features), lambda i: (i, 0)),
        out_shape=jax.ShapeDtypeStruct((rows, features), jnp.bfloat16),
        compiler_params=params(),
        cost_estimate=pl.CostEstimate(
            flops=4 * rows * tokens * features, bytes_accessed=4 * rows * features, transcendentals=0
        ),
        name="dispatch",
    )(normed, pick)


def gated(gate_up):
    hidden = gate_up.shape[1] // 2
    gate = gate_up[:, :hidden]
    return (gate / (1.0 + jnp.exp(-gate)) * gate_up[:, hidden:]).astype(jnp.bfloat16)


def up_kernel(features, x_ref, wu_ref, wd_ref, out_ref, ninth_ref, last):
    index = pl.program_id(0)
    lasts = x_ref.shape[0] // GROUP
    out_ref[...] = f32dot(x_ref[:, :features], wu_ref[0, :features, :])
    last[pl.ds(pl.multiple_of(index * lasts, lasts), lasts), :] = unfold(x_ref[:, features:])

    @pl.when(index == pl.num_programs(0) - 1)
    def _():
        active = gated(f32dot(last[...], wu_ref[0]))
        ninth_ref[...] = fold(f32dot(active, wd_ref[0]).astype(jnp.bfloat16))


def up_first(received, w_up, w_down, features):
    rows, wide = received.shape
    columns = w_up.shape[2]
    width = w_down.shape[2]
    blocks = 4
    return pl.pallas_call(
        functools.partial(up_kernel, features),
        grid=(blocks,),
        in_specs=[
            pl.BlockSpec((rows // blocks, wide), lambda i: (i, 0)),
            whole_block(w_up.shape),
            whole_block(w_down.shape),
        ],
        out_specs=[
            pl.BlockSpec((rows // blocks, columns), lambda i: (i, 0)),
            pl.BlockSpec((rows, width // GROUP), lambda i: (0, 0)),
        ],
        out_shape=[
            jax.ShapeDtypeStruct((rows, columns), jnp.float32),
            jax.ShapeDtypeStruct((rows, width // GROUP), jnp.bfloat16),
        ],
        scratch_shapes=[pltpu.VMEM((rows // GROUP, width), jnp.bfloat16)],
        compiler_params=params(),
        cost_estimate=pl.CostEstimate(
            flops=2 * rows * features * columns, bytes_accessed=20000000, transcendentals=0
        ),
        name="up_first",
    )(received, w_up, w_down)


def expert_kernel(x_ref, wu_ref, partial_ref, ninth_ref, wd_hbm, out_ref, wd, arrived):
    index = pl.program_id(0)
    copy = pltpu.make_async_copy(wd_hbm.at[0], wd, arrived)

    @pl.when(index == 0)
    def _():
        copy.start()

    active = gated(partial_ref[...] + f32dot(x_ref[...], wu_ref[0]))

    @pl.when(index == 0)
    def _():
        copy.wait()

    width = wd.shape[1]
    out_ref[:, :width] = f32dot(active, wd[...]).astype(jnp.bfloat16)
    out_ref[:, width:] = ninth_ref[...]


def expert(received, w_up, partial, ninth, w_down, chunk):
    rows, features = received.shape
    columns = w_up.shape[2]
    hidden, width = w_down.shape[1:]
    blocks = 4
    out_wide = width + width // GROUP
    return pl.pallas_call(
        expert_kernel,
        grid=(blocks,),
        in_specs=[
            pl.BlockSpec((rows // blocks, features), lambda i: (i, 0)),
            pl.BlockSpec(
                (1, features, columns), lambda i: (0, chunk, 0), pipeline_mode=pl.Buffered(1)
            ),
            pl.BlockSpec((rows // blocks, columns), lambda i: (i, 0)),
            pl.BlockSpec((rows // blocks, width // GROUP), lambda i: (i, 0)),
            pl.BlockSpec(memory_space=pl.ANY),
        ],
        out_specs=pl.BlockSpec((rows // blocks, out_wide), lambda i: (i, 0)),
        out_shape=jax.ShapeDtypeStruct((rows, out_wide), jnp.bfloat16),
        scratch_shapes=[pltpu.VMEM((hidden, width), jnp.bfloat16), pltpu.SemaphoreType.DMA(())],
        compiler_params=params(55),
        cost_estimate=pl.CostEstimate(
            flops=2 * rows * (features * columns + hidden * width),
            bytes_accessed=30000000,
            transcendentals=0,
        ),
        name="expert",
    )(received, w_up, partial, ninth, w_down)


def combine_kernel(x_ref, ninth_ref, w_ref, wlast_ref, resid_ref, out_ref, last):
    tokens, width = resid_ref.shape
    index = pl.program_id(0)

    @pl.when(index == 0)
    def _():
        last[...] = unfold(ninth_ref[...])

    own = last[:, pl.ds(pl.multiple_of(index * width, width), width)]
    both = f32dot(w_ref[...], x_ref[...]) + f32dot(wlast_ref[...], own)
    out_ref[...] = (resid_ref[...] + both[:tokens] + both[tokens:]).astype(jnp.bfloat16)


def combine(returned, weights, last_weights, resid):
    rows = returned.shape[0]
    tokens, features = resid.shape
    count = last_weights.shape[1]
    blocks = 2
    width = features // blocks
    return pl.pallas_call(
        combine_kernel,
        grid=(blocks,),
        in_specs=[
            pl.BlockSpec((rows, width), lambda i: (0, i)),
            pl.BlockSpec(
                (rows, features // GROUP), lambda i: (0, GROUP), pipeline_mode=pl.Buffered(1)
            ),
            whole_block((2 * tokens, rows)),
            whole_block((2 * tokens, count)),
            pl.BlockSpec((tokens, width), lambda i: (0, i)),
        ],
        out_specs=pl.BlockSpec((tokens, width), lambda i: (0, i)),
        out_shape=jax.ShapeDtypeStruct((tokens, features), jnp.bfloat16),
        scratch_shapes=[pltpu.VMEM((count, features), jnp.bfloat16)],
        compiler_params=params(),
        name="combine",
    )(returned, returned, weights, last_weights, resid)


def on_device(
    tokens,
    block_order,
    attn_gain,
    query_gain,
    key_gain,
    w_qkv,
    w_out,
    moe_gain,
    router,
    routes,
    w_gate_up,
    w_down,
):
    rows, model_width = tokens.shape
    size = query_gain.shape[0]
    ctx_size, exp_size = lax.axis_size("ctx"), lax.axis_size("exp")
    ctx_at, exp_at = lax.axis_index("ctx"), lax.axis_index("exp")
    ring = 4
    inner = exp_size // ring
    x_at, z_lo = ctx_at % ring, ctx_at // ring
    y_at, z_hi, core = exp_at // inner, exp_at // 2 % 2, exp_at % 2

    def device(z_lo, x, y, z_hi, core):
        return (z_lo * ring + x) * exp_size + y * inner + z_hi * 2 + core

    def bring(value, z_lo=0, x=0, y=0, z_hi=0, core=0):
        pairs = []
        for at in range(ctx_size * exp_size):
            c, e = at // exp_size, at % exp_size
            source = device(
                c // ring ^ z_lo,
                (c - x) % ring,
                (e // inner - y) % ring,
                e // 2 % 2 ^ z_hi,
                e % 2 ^ core,
            )
            pairs.append((source, at))
        return lax.ppermute(value, ("ctx", "exp"), pairs)

    def along_y(value):
        return jnp.concatenate([value] + [bring(value, y=k) for k in range(1, ring)])

    def along_x(values, step):
        return [values[0]] + [bring(values[k], x=step * k) for k in range(1, ring)]

    relative = jnp.arange(exp_size, dtype=jnp.int32)
    piece_of = (
        (core + relative) % 2 * (2 * ring)
        + (y_at - relative // inner) % ring * 2
        + (z_hi + relative // 2) % 2
    )
    relative = jnp.arange(2 * exp_size, dtype=jnp.int32)
    key_devices = device(
        (z_lo + relative) % 2,
        x_at,
        (y_at - relative // 4) % ring,
        (z_hi + relative // 2) % 2,
        (core + relative // (4 * ring)) % 2,
    )
    steps = jnp.arange(ring, dtype=jnp.int32)
    query_devices = device(z_lo, (x_at - steps) % ring, y_at, z_hi, core)

    def block_numbers(devices):
        every = jnp.arange(block_order.shape[0], dtype=jnp.int32)
        return jnp.sum(
            jnp.where(devices[:, None] == every[None, :], block_order[None, :], 0), axis=1
        )

    k_blocks = block_numbers(key_devices)
    q_blocks = block_numbers(query_devices)
    own_pos = q_blocks[0] * rows + jnp.arange(rows, dtype=jnp.int32)
    hide = jnp.repeat(
        jnp.where(k_blocks[None, :] > q_blocks[:, None], HIDDEN, 0.0), rows, axis=1
    )
    hide = jnp.pad(hide, ((0, size - ring), (0, 0))).astype(jnp.bfloat16)

    depth = model_width // ring
    widened = tokens.astype(jnp.float32)
    row_scale = lax.rsqrt(jnp.mean(widened * widened, axis=1, keepdims=True) + 1e-06)
    gained = (widened * attn_gain.astype(jnp.float32)).astype(jnp.bfloat16)
    w_share = lax.dynamic_slice_in_dim(w_qkv.T, x_at * depth, depth, 1)
    other, gained = lax.optimization_barrier((bring(w_share, z_hi=1), gained))
    near = along_y(jnp.stack([w_share, other]))
    shares = along_x(
        [
            lax.dynamic_slice_in_dim(gained, (x_at + k) % ring * depth, depth, 1)
            for k in range(ring)
        ],
        1,
    )
    near, shares = lax.optimization_barrier((near, shares))
    far = bring(near, core=1)
    w_out_all = lax.all_gather(w_out, "exp", axis=0, tiled=True)
    shares = project(shares, near, far, piece_of)
    shares, routes = lax.optimization_barrier((shares, routes))
    count = router.shape[1]
    pick, pick_last, named = slots(routes.T, count)
    half = size // 2
    freqs = jnp.exp(
        -math.log(rope_base) * jnp.arange(half, dtype=jnp.float32) * 2.0 / size
    )
    angles = own_pos.astype(jnp.float32)[:, None] * freqs[None, :]
    cos, sin = jnp.cos(angles), jnp.sin(angles)
    cos = jnp.concatenate([cos, cos], axis=1)
    sin = jnp.concatenate([-sin, sin], axis=1)
    parts = along_x(shares, -1)
    parts, pick, pick_last, named, hide, cos, sin = lax.optimization_barrier(
        (parts, pick, pick_last, named, hide, cos, sin)
    )
    heads = parts[0].shape[1] // size - 2
    queries, key_values = shape(parts, row_scale, query_gain, key_gain, cos, sin)
    others = [
        bring(key_values, z_lo=1),
        bring(key_values, z_hi=1),
        bring(key_values, z_lo=1, z_hi=1),
    ]
    others, left, right = lax.optimization_barrier(
        (others, bring(queries, x=1), bring(queries, x=ring - 1))
    )
    near = along_y(jnp.stack([key_values, *others])).reshape(-1, 2 * size)
    near, across = lax.optimization_barrier((near, bring(queries, x=2)))
    queries = [queries, left, across, right]
    far = bring(near, core=1)
    totals = attend(queries, near, hide, None, heads, size)
    parts = along_x(attend(queries, far, hide, totals, heads, size), -1)
    main = model_width // 4 * 3
    rest = model_width - main
    resid, moe_in, outgoing = finish(
        parts, w_out_all, tokens, moe_gain, pick, pick_last, heads, size, main
    )

    def exchange(x):
        wide = x.shape[1]
        x = lax.all_to_all(
            x.reshape(count, GROUP, wide), ("ctx", "exp"), split_axis=0, concat_axis=0, tiled=True
        )
        return x.reshape(count * GROUP, wide)

    first = exchange(outgoing)
    second = exchange(dispatch(moe_in, pick, main // rest, rest))
    first, moe_in = lax.optimization_barrier((first, moe_in))
    weights, last_weights = weigh(moe_in, router, named, pick, pick_last)
    partial, ninth = up_first(first, w_gate_up, w_down, main)
    returned = exchange(expert(second, w_gate_up, partial, ninth, w_down, main // rest))
    return combine(returned, weights, last_weights, resid)


def solution(mesh):
    return jax.shard_map(
        on_device,
        mesh=mesh,
        in_specs=(
            P(("ctx", "exp"), None),
            P(),
            P(),
            P(),
            P(),
            P(None, "exp"),
            P("exp", None),
            P(),
            P(),
            P(("ctx", "exp"), None),
            P(("ctx", "exp"), None, None),
            P(("ctx", "exp"), None, None),
        ),
        out_specs=P(("ctx", "exp"), None),
        check_vma=False,
    )
```

```python
import functools
import math

import jax
import jax.numpy as jnp
from jax import lax
from jax.experimental import pallas as pl
from jax.experimental.pallas import tpu as pltpu
from jax.sharding import PartitionSpec as P

rope_base = 1000000.0
GROUP = 8
VMEM_MB = 60
HIDDEN = -30000.0


def rms_scale(values, gain):
    widened = values.astype(jnp.float32)
    return (
        widened
        * lax.rsqrt(jnp.mean(widened * widened, axis=-1, keepdims=True) + 1e-06)
        * gain.astype(jnp.float32)
    )


def params(megabytes=VMEM_MB):
    return pltpu.CompilerParams(
        vmem_limit_bytes=megabytes * 1024 * 1024, dimension_semantics=("arbitrary",)
    )


def f32dot(a, b):
    return jnp.dot(a, b, preferred_element_type=jnp.float32)


def whole_block(shape):
    zeros = (0,) * len(shape)
    return pl.BlockSpec(shape, lambda *_: zeros, pipeline_mode=pl.Buffered(1))


def project_kernel(order_ref, *refs):
    ring = (len(refs) - 3) // 2
    x_refs, (near_ref, far_ref), out_refs, whole = (
        refs[:ring],
        refs[ring : ring + 2],
        refs[ring + 2 : -1],
        refs[-1],
    )
    half, columns = near_ref.shape[:2]
    rows = x_refs[0].shape[0]
    for e in range(2 * half):
        at = order_ref[e]
        near = near_ref[lax.rem(at, half)].astype(jnp.float32)
        far = far_ref[lax.rem(at, half)].astype(jnp.float32)
        whole[e * columns : (e + 1) * columns, :] = jnp.where(at < half, near, far).astype(
            jnp.bfloat16
        )
    x = jnp.concatenate([ref[...] for ref in x_refs], axis=0)
    out = lax.dot_general(
        x, whole[...], (((1,), (1,)), ((), ())), preferred_element_type=jnp.float32
    ).astype(jnp.bfloat16)
    for at, ref in enumerate(out_refs):
        ref[...] = out[at * rows : (at + 1) * rows]


def project(shares, near, far, order):
    rows, depth = shares[0].shape
    half, columns = near.shape[:2]
    out = jax.ShapeDtypeStruct((rows, 2 * half * columns), jnp.bfloat16)
    return pl.pallas_call(
        project_kernel,
        grid_spec=pltpu.PrefetchScalarGridSpec(
            num_scalar_prefetch=1,
            grid=(1,),
            in_specs=[whole_block(x.shape) for x in (*shares, near, far)],
            out_specs=[whole_block(out.shape)] * len(shares),
            scratch_shapes=[pltpu.VMEM((2 * half * columns, depth), jnp.bfloat16)],
        ),
        out_shape=[out] * len(shares),
        compiler_params=params(16),
        name="project",
    )(order, *shares, near, far)


def shape_kernel(heads, size, *refs):
    parts, (scale_ref, qgain_ref, kgain_ref, cos_ref, sin_ref, q_ref, kv_ref) = refs[:-7], refs[-7:]
    mixed = parts[0][...].astype(jnp.float32)
    for ref in parts[1:]:
        mixed = mixed + ref[...].astype(jnp.float32)
    mixed = mixed * scale_ref[...]
    half = size // 2

    def rope(values, gain):
        scale = lax.rsqrt(jnp.mean(values * values, axis=1, keepdims=True) + 1e-06)
        values = values * scale * gain.astype(jnp.float32)
        turned = jnp.concatenate([values[:, half:], values[:, :half]], axis=1)
        return values * cos_ref[...] + turned * sin_ref[...]

    for h in range(heads):
        part = slice(h * size, (h + 1) * size)
        q = rope(mixed[:, part], qgain_ref[...]) * (math.log2(math.e) / math.sqrt(size))
        q_ref[:, part] = q.astype(jnp.bfloat16)
    at = heads * size
    kv_ref[:, :size] = rope(mixed[:, at : at + size], kgain_ref[...]).astype(jnp.bfloat16)
    kv_ref[:, size:] = mixed[:, at + size :].astype(jnp.bfloat16)


def shape(parts, scale, query_gain, key_gain, cos, sin):
    rows, columns = parts[0].shape
    size = query_gain.shape[0]
    heads = columns // size - 2
    return pl.pallas_call(
        functools.partial(shape_kernel, heads, size),
        out_shape=[
            jax.ShapeDtypeStruct((rows, heads * size), jnp.bfloat16),
            jax.ShapeDtypeStruct((rows, 2 * size), jnp.bfloat16),
        ],
        compiler_params=pltpu.CompilerParams(vmem_limit_bytes=8 * 1024 * 1024),
        name="shape",
    )(*parts, scale, query_gain.reshape(1, -1), key_gain.reshape(1, -1), cos, sin)


def attend_kernel(heads, size, width, ring, last, *refs):
    q_refs, (kv_ref, hide_ref), refs = refs[:ring], refs[ring : ring + 2], refs[ring + 2 :]
    index = pl.program_id(0)
    rows = q_refs[0].shape[0]
    length = kv_ref.shape[0]
    before_ref, (held, keys, values) = refs[0] if last else None, refs[-3:]
    out_refs = refs[1:-3] if last else refs[:-3]

    @pl.when(index == 0)
    def _():
        for at, ref in enumerate(q_refs):
            held[at] = ref[...]
        keys[:size, :] = kv_ref[:, :size].T
        keys[size:, :] = hide_ref[...]
        values[:, :size] = kv_ref[:, size:]
        values[:, size:] = jnp.ones((length, size), jnp.bfloat16)

    mark = lax.broadcasted_iota(jnp.int32, (rows, size), 1) == index
    mark = jnp.where(mark, 1.0, 0.0).astype(jnp.bfloat16)
    row = lax.broadcasted_iota(jnp.int32, (rows, width), 0)
    key = lax.broadcasted_iota(jnp.int32, (rows, width), 1)
    later = (key > row) & (key < rows) & (index == 0)
    totals = []
    for h in range(heads):
        q = jnp.concatenate([held[index, :, h * size : (h + 1) * size], mark], axis=1)
        if last:
            total = before_ref[0, h]
        else:
            total = jnp.zeros((rows, 2 * size), jnp.float32)
        for start in range(0, length, width):
            part = pl.ds(start, width)
            scores = f32dot(q, keys[:, part])
            if start == 0 and not last:
                scores = jnp.where(later, HIDDEN, scores)
            total = total + f32dot(jnp.exp2(scores).astype(jnp.bfloat16), values[part, :])
        totals.append(total)
    if not last:
        for h in range(heads):
            out_refs[0][0, h] = totals[h]
        return
    lane = lax.broadcasted_iota(jnp.int32, (rows, size), 1)
    sums = jnp.zeros((rows, size), jnp.float32)
    results = []
    for h, total in enumerate(totals):
        results.append(total[:, :size].astype(jnp.bfloat16))
        high = total[:, size:].astype(jnp.bfloat16).astype(jnp.float32)
        sums = jnp.where(lane == 2 * h, high, sums)
        sums = jnp.where(lane == 2 * h + 1, total[:, size:] - high, sums)
    packed = jnp.concatenate([*results, sums.astype(jnp.bfloat16)], axis=1)
    for at, ref in enumerate(out_refs):

        @pl.when(index == at)
        def _(ref=ref):
            ref[...] = packed


def attend(queries, key_values, hide, before, heads, size):
    rows, columns = queries[0].shape
    ring = len(queries)
    length = key_values.shape[0]
    last = before is not None
    totals = (heads, rows, 2 * size)
    totals_spec = pl.BlockSpec((1, *totals), lambda i: (i, 0, 0, 0))
    in_specs = [whole_block(x.shape) for x in (*queries, key_values)]
    in_specs.append(
        pl.BlockSpec((size, length), lambda i: (0, int(last)), pipeline_mode=pl.Buffered(1))
    )
    operands = [*queries, key_values, hide]
    if last:
        in_specs.append(totals_spec)
        operands.append(before)
        out = jax.ShapeDtypeStruct((rows, columns + size), jnp.bfloat16)
        out_specs, out_shape = [whole_block(out.shape)] * ring, [out] * ring
    else:
        out_specs = totals_spec
        out_shape = jax.ShapeDtypeStruct((ring, *totals), jnp.float32)
    return pl.pallas_call(
        functools.partial(attend_kernel, heads, size, 512, ring, last),
        grid=(ring,),
        in_specs=in_specs,
        out_specs=out_specs,
        scratch_shapes=[
            pltpu.VMEM((ring, rows, columns), jnp.bfloat16),
            pltpu.VMEM((2 * size, length), jnp.bfloat16),
            pltpu.VMEM((length, 2 * size), jnp.bfloat16),
        ],
        out_shape=out_shape,
        compiler_params=params(20),
        cost_estimate=pl.CostEstimate(
            flops=16 * heads * rows * ring * length * size,
            bytes_accessed=8000000,
            transcendentals=heads * rows * ring * length,
        ),
        name="attend",
    )(*operands)


def repeat_rows(values):
    rows = values.shape[0]
    row = lax.broadcasted_iota(jnp.int32, (rows * GROUP, rows), 0)
    column = lax.broadcasted_iota(jnp.int32, (rows * GROUP, rows), 1)
    copies = (lax.div(row, GROUP) == column).astype(jnp.bfloat16)
    return f32dot(copies, values)


def slots_kernel(routes_ref, pick_ref, last_ref, named_ref):
    fanout, tokens = routes_ref.shape
    count = named_ref.shape[0]
    expert = lax.broadcasted_iota(jnp.int32, (count, tokens), 0)
    named = jnp.zeros((count, tokens), jnp.float32)
    for j in range(fanout):
        named = named + jnp.where(routes_ref[j : j + 1, :] == expert, 1.0, 0.0)
    earlier = lax.broadcasted_iota(jnp.int32, (tokens, tokens), 0)
    later = lax.broadcasted_iota(jnp.int32, (tokens, tokens), 1)
    before = (earlier < later).astype(jnp.bfloat16)
    rank = f32dot(named.astype(jnp.bfloat16), before)
    code = named * (rank + 1.0)
    named_ref[...] = named
    last_ref[...] = (code == GROUP + 1.0).astype(jnp.bfloat16)
    spread = repeat_rows(code.astype(jnp.bfloat16))
    slot = lax.rem(lax.broadcasted_iota(jnp.int32, spread.shape, 0), GROUP) + 1
    pick_ref[...] = (spread == slot.astype(jnp.float32)).astype(jnp.bfloat16)


def slots(routes_t, count):
    fanout, tokens = routes_t.shape
    return pl.pallas_call(
        slots_kernel,
        out_shape=[
            jax.ShapeDtypeStruct((count * GROUP, tokens), jnp.bfloat16),
            jax.ShapeDtypeStruct((count, tokens), jnp.bfloat16),
            jax.ShapeDtypeStruct((count, tokens), jnp.float32),
        ],
        compiler_params=pltpu.CompilerParams(vmem_limit_bytes=VMEM_MB * 1024 * 1024),
        name="slots",
    )(routes_t)


def weigh_kernel(x_ref, router_ref, named_ref, pick_ref, last_ref, out_ref, out_last_ref):
    logits = lax.dot_general(
        router_ref[...], x_ref[...], (((0,), (1,)), ((), ())), preferred_element_type=jnp.float32
    )
    named = named_ref[...] > 0.5
    largest = jnp.max(jnp.where(named, logits, -jnp.inf), axis=0, keepdims=True)
    shares = jnp.where(named, jnp.exp(jnp.minimum(logits - largest, 0.0)), 0.0)
    shares = shares / jnp.sum(shares, axis=0, keepdims=True)
    shares = shares.astype(jnp.bfloat16)
    out_ref[...] = (repeat_rows(shares).astype(jnp.bfloat16) * pick_ref[...]).T
    out_last_ref[...] = (shares * last_ref[...]).T


def weigh(moe_in, router, named, pick, last):
    tokens = moe_in.shape[0]
    return pl.pallas_call(
        weigh_kernel,
        out_shape=[
            jax.ShapeDtypeStruct((tokens, pick.shape[0]), jnp.bfloat16),
            jax.ShapeDtypeStruct((tokens, last.shape[0]), jnp.bfloat16),
        ],
        compiler_params=pltpu.CompilerParams(vmem_limit_bytes=VMEM_MB * 1024 * 1024),
        name="weigh",
    )(moe_in, router, named, pick, last)


def fold(rows):
    count, features = rows.shape
    return rows.reshape(count, GROUP, features // GROUP).reshape(count * GROUP, features // GROUP)


def unfold(rows):
    count, piece = rows.shape
    return rows.reshape(count // GROUP, GROUP, piece).reshape(count // GROUP, GROUP * piece)


def finish_kernel(
    heads,
    size,
    features,
    *refs,
):
    parts_refs, refs = refs[:-12], refs[-12:]
    w_ref, x_ref, gain_ref, pick_ref, last_ref, resid_hbm, norm_hbm, out_ref = refs[:8]
    resid_ref, norm_ref, resid_sent, norm_sent = refs[8:]
    copies = (
        pltpu.make_async_copy(resid_ref, resid_hbm, resid_sent),
        pltpu.make_async_copy(norm_ref, norm_hbm, norm_sent),
    )

    @pl.when(pl.program_id(0) == 0)
    def _():
        summed = parts_refs[0][...].astype(jnp.float32)
        for ref in parts_refs[1:]:
            summed = summed + ref[...].astype(jnp.float32)
        base = heads * size
        attended = []
        for h in range(heads):
            at = base + 2 * h
            total = summed[:, at : at + 1] + summed[:, at + 1 : at + 2]
            attended.append((summed[:, h * size : (h + 1) * size] / total).astype(jnp.bfloat16))
        projected = f32dot(jnp.concatenate(attended, axis=1), w_ref[...])
        resid = x_ref[...].astype(jnp.float32) + projected
        resid_ref[...] = resid
        scale = lax.rsqrt(jnp.mean(resid * resid, axis=1, keepdims=True) + 1e-06)
        norm_ref[...] = (resid * scale * gain_ref[...].astype(jnp.float32)).astype(jnp.bfloat16)
        for copy in copies:
            copy.start()

    out_ref[:, :features] = f32dot(pick_ref[...], norm_ref[:, :features]).astype(jnp.bfloat16)
    out_ref[:, features:] = fold(f32dot(last_ref[...], norm_ref[...]).astype(jnp.bfloat16))

    @pl.when(pl.program_id(0) == pl.num_programs(0) - 1)
    def _():
        for copy in copies:
            copy.wait()


def finish(parts, w_out, tokens, gain, pick, last, heads, size, features):
    rows, count = pick.shape[0], last.shape[0]
    wide = features + tokens.shape[1] // GROUP
    blocks = 4
    return pl.pallas_call(
        functools.partial(finish_kernel, heads, size, features),
        grid=(blocks,),
        in_specs=[
            *(whole_block(x.shape) for x in parts),
            whole_block(w_out.shape),
            whole_block(tokens.shape),
            whole_block((1, gain.shape[0])),
            pl.BlockSpec((rows // blocks, pick.shape[1]), lambda i: (i, 0)),
            pl.BlockSpec((count // blocks, pick.shape[1]), lambda i: (i, 0)),
        ],
        out_specs=[
            pl.BlockSpec(memory_space=pl.ANY),
            pl.BlockSpec(memory_space=pl.ANY),
            pl.BlockSpec((rows // blocks, wide), lambda i: (i, 0)),
        ],
        scratch_shapes=[
            pltpu.VMEM(tokens.shape, jnp.float32),
            pltpu.VMEM(tokens.shape, jnp.bfloat16),
            pltpu.SemaphoreType.DMA(()),
            pltpu.SemaphoreType.DMA(()),
        ],
        out_shape=[
            jax.ShapeDtypeStruct(tokens.shape, jnp.float32),
            jax.ShapeDtypeStruct(tokens.shape, jnp.bfloat16),
            jax.ShapeDtypeStruct((rows, wide), jnp.bfloat16),
        ],
        compiler_params=params(57),
        name="finish",
    )(*parts, w_out, tokens, gain.reshape(1, -1), pick, last)


def dispatch_kernel(x_ref, pick_ref, out_ref):
    out_ref[...] = f32dot(pick_ref[...], x_ref[...]).astype(jnp.bfloat16)


def dispatch(normed, pick, chunk, features):
    rows, tokens = pick.shape
    blocks = 4
    return pl.pallas_call(
        dispatch_kernel,
        grid=(blocks,),
        in_specs=[
            pl.BlockSpec((tokens, features), lambda i: (0, chunk)),
            pl.BlockSpec((rows // blocks, tokens), lambda i: (i, 0)),
        ],
        out_specs=pl.BlockSpec((rows // blocks, features), lambda i: (i, 0)),
        out_shape=jax.ShapeDtypeStruct((rows, features), jnp.bfloat16),
        compiler_params=params(),
        cost_estimate=pl.CostEstimate(
            flops=4 * rows * tokens * features, bytes_accessed=4 * rows * features, transcendentals=0
        ),
        name="dispatch",
    )(normed, pick)


def gated(gate_up):
    hidden = gate_up.shape[1] // 2
    gate = gate_up[:, :hidden]
    return (gate / (1.0 + jnp.exp(-gate)) * gate_up[:, hidden:]).astype(jnp.bfloat16)


def up_kernel(features, x_ref, wu_ref, wd_ref, out_ref, ninth_ref, last):
    index = pl.program_id(0)
    lasts = x_ref.shape[0] // GROUP
    out_ref[...] = f32dot(x_ref[:, :features], wu_ref[0, :features, :])
    last[pl.ds(pl.multiple_of(index * lasts, lasts), lasts), :] = unfold(x_ref[:, features:])

    @pl.when(index == pl.num_programs(0) - 1)
    def _():
        active = gated(f32dot(last[...], wu_ref[0]))
        ninth_ref[...] = fold(f32dot(active, wd_ref[0]).astype(jnp.bfloat16))


def up_first(received, w_up, w_down, features):
    rows, wide = received.shape
    columns = w_up.shape[2]
    width = w_down.shape[2]
    blocks = 4
    return pl.pallas_call(
        functools.partial(up_kernel, features),
        grid=(blocks,),
        in_specs=[
            pl.BlockSpec((rows // blocks, wide), lambda i: (i, 0)),
            whole_block(w_up.shape),
            whole_block(w_down.shape),
        ],
        out_specs=[
            pl.BlockSpec((rows // blocks, columns), lambda i: (i, 0)),
            pl.BlockSpec((rows, width // GROUP), lambda i: (0, 0)),
        ],
        out_shape=[
            jax.ShapeDtypeStruct((rows, columns), jnp.float32),
            jax.ShapeDtypeStruct((rows, width // GROUP), jnp.bfloat16),
        ],
        scratch_shapes=[pltpu.VMEM((rows // GROUP, width), jnp.bfloat16)],
        compiler_params=params(),
        cost_estimate=pl.CostEstimate(
            flops=2 * rows * features * columns, bytes_accessed=20000000, transcendentals=0
        ),
        name="up_first",
    )(received, w_up, w_down)


def expert_kernel(x_ref, wu_ref, partial_ref, ninth_ref, wd_hbm, out_ref, wd, arrived):
    index = pl.program_id(0)
    copy = pltpu.make_async_copy(wd_hbm.at[0], wd, arrived)

    @pl.when(index == 0)
    def _():
        copy.start()

    active = gated(partial_ref[...] + f32dot(x_ref[...], wu_ref[0]))

    @pl.when(index == 0)
    def _():
        copy.wait()

    width = wd.shape[1]
    out_ref[:, :width] = f32dot(active, wd[...]).astype(jnp.bfloat16)
    out_ref[:, width:] = ninth_ref[...]


def expert(received, w_up, partial, ninth, w_down, chunk):
    rows, features = received.shape
    columns = w_up.shape[2]
    hidden, width = w_down.shape[1:]
    blocks = 4
    out_wide = width + width // GROUP
    return pl.pallas_call(
        expert_kernel,
        grid=(blocks,),
        in_specs=[
            pl.BlockSpec((rows // blocks, features), lambda i: (i, 0)),
            pl.BlockSpec(
                (1, features, columns), lambda i: (0, chunk, 0), pipeline_mode=pl.Buffered(1)
            ),
            pl.BlockSpec((rows // blocks, columns), lambda i: (i, 0)),
            pl.BlockSpec((rows // blocks, width // GROUP), lambda i: (i, 0)),
            pl.BlockSpec(memory_space=pl.ANY),
        ],
        out_specs=pl.BlockSpec((rows // blocks, out_wide), lambda i: (i, 0)),
        out_shape=jax.ShapeDtypeStruct((rows, out_wide), jnp.bfloat16),
        scratch_shapes=[pltpu.VMEM((hidden, width), jnp.bfloat16), pltpu.SemaphoreType.DMA(())],
        compiler_params=params(55),
        cost_estimate=pl.CostEstimate(
            flops=2 * rows * (features * columns + hidden * width),
            bytes_accessed=30000000,
            transcendentals=0,
        ),
        name="expert",
    )(received, w_up, partial, ninth, w_down)


def combine_kernel(x_ref, ninth_ref, w_ref, wlast_ref, resid_ref, out_ref, last):
    width = resid_ref.shape[1]
    index = pl.program_id(0)

    @pl.when(index == 0)
    def _():
        last[...] = unfold(ninth_ref[...])

    own = last[:, pl.ds(pl.multiple_of(index * width, width), width)]
    added = f32dot(w_ref[...], x_ref[...]) + f32dot(wlast_ref[...], own)
    out_ref[...] = (resid_ref[...] + added).astype(jnp.bfloat16)


def combine(returned, weights, last_weights, resid):
    rows = returned.shape[0]
    tokens, features = resid.shape
    count = last_weights.shape[1]
    blocks = 2
    width = features // blocks
    return pl.pallas_call(
        combine_kernel,
        grid=(blocks,),
        in_specs=[
            pl.BlockSpec((rows, width), lambda i: (0, i)),
            pl.BlockSpec(
                (rows, features // GROUP), lambda i: (0, GROUP), pipeline_mode=pl.Buffered(1)
            ),
            whole_block((tokens, rows)),
            whole_block((tokens, count)),
            pl.BlockSpec((tokens, width), lambda i: (0, i)),
        ],
        out_specs=pl.BlockSpec((tokens, width), lambda i: (0, i)),
        out_shape=jax.ShapeDtypeStruct((tokens, features), jnp.bfloat16),
        scratch_shapes=[pltpu.VMEM((count, features), jnp.bfloat16)],
        compiler_params=params(),
        name="combine",
    )(returned, returned, weights, last_weights, resid)


def on_device(
    tokens,
    block_order,
    attn_gain,
    query_gain,
    key_gain,
    w_qkv,
    w_out,
    moe_gain,
    router,
    routes,
    w_gate_up,
    w_down,
):
    rows, model_width = tokens.shape
    size = query_gain.shape[0]
    ctx_size, exp_size = lax.axis_size("ctx"), lax.axis_size("exp")
    ctx_at, exp_at = lax.axis_index("ctx"), lax.axis_index("exp")
    ring = 4
    inner = exp_size // ring
    x_at, z_lo = ctx_at % ring, ctx_at // ring
    y_at, z_hi, core = exp_at // inner, exp_at // 2 % 2, exp_at % 2

    def device(z_lo, x, y, z_hi, core):
        return (z_lo * ring + x) * exp_size + y * inner + z_hi * 2 + core

    def bring(value, z_lo=0, x=0, y=0, z_hi=0, core=0):
        pairs = []
        for at in range(ctx_size * exp_size):
            c, e = at // exp_size, at % exp_size
            source = device(
                c // ring ^ z_lo,
                (c - x) % ring,
                (e // inner - y) % ring,
                e // 2 % 2 ^ z_hi,
                e % 2 ^ core,
            )
            pairs.append((source, at))
        return lax.ppermute(value, ("ctx", "exp"), pairs)

    def along_y(value):
        return jnp.concatenate([value] + [bring(value, y=k) for k in range(1, ring)])

    def along_x(values, step):
        return [values[0]] + [bring(values[k], x=step * k) for k in range(1, ring)]

    relative = jnp.arange(exp_size, dtype=jnp.int32)
    piece_of = (
        (core + relative) % 2 * (2 * ring)
        + (y_at - relative // inner) % ring * 2
        + (z_hi + relative // 2) % 2
    )
    relative = jnp.arange(2 * exp_size, dtype=jnp.int32)
    key_devices = device(
        (z_lo + relative) % 2,
        x_at,
        (y_at - relative // 4) % ring,
        (z_hi + relative // 2) % 2,
        (core + relative // (4 * ring)) % 2,
    )
    steps = jnp.arange(ring, dtype=jnp.int32)
    query_devices = device(z_lo, (x_at - steps) % ring, y_at, z_hi, core)

    def block_numbers(devices):
        every = jnp.arange(block_order.shape[0], dtype=jnp.int32)
        return jnp.sum(
            jnp.where(devices[:, None] == every[None, :], block_order[None, :], 0), axis=1
        )

    k_blocks = block_numbers(key_devices)
    q_blocks = block_numbers(query_devices)
    own_pos = q_blocks[0] * rows + jnp.arange(rows, dtype=jnp.int32)
    hide = jnp.repeat(
        jnp.where(k_blocks[None, :] > q_blocks[:, None], HIDDEN, 0.0), rows, axis=1
    )
    hide = jnp.pad(hide, ((0, size - ring), (0, 0))).astype(jnp.bfloat16)

    depth = model_width // ring
    widened = tokens.astype(jnp.float32)
    row_scale = lax.rsqrt(jnp.mean(widened * widened, axis=1, keepdims=True) + 1e-06)
    gained = (widened * attn_gain.astype(jnp.float32)).astype(jnp.bfloat16)
    w_share = lax.dynamic_slice_in_dim(w_qkv.T, x_at * depth, depth, 1)
    other, gained = lax.optimization_barrier((bring(w_share, z_hi=1), gained))
    near = along_y(jnp.stack([w_share, other]))
    shares = along_x(
        [
            lax.dynamic_slice_in_dim(gained, (x_at + k) % ring * depth, depth, 1)
            for k in range(ring)
        ],
        1,
    )
    near, shares = lax.optimization_barrier((near, shares))
    far = bring(near, core=1)
    w_out_all = lax.all_gather(w_out, "exp", axis=0, tiled=True)
    shares = project(shares, near, far, piece_of)
    shares, routes = lax.optimization_barrier((shares, routes))
    count = router.shape[1]
    pick, pick_last, named = slots(routes.T, count)
    half = size // 2
    freqs = jnp.exp(
        -math.log(rope_base) * jnp.arange(half, dtype=jnp.float32) * 2.0 / size
    )
    angles = own_pos.astype(jnp.float32)[:, None] * freqs[None, :]
    cos, sin = jnp.cos(angles), jnp.sin(angles)
    cos = jnp.concatenate([cos, cos], axis=1)
    sin = jnp.concatenate([-sin, sin], axis=1)
    parts = along_x(shares, -1)
    parts, pick, pick_last, named, hide, cos, sin = lax.optimization_barrier(
        (parts, pick, pick_last, named, hide, cos, sin)
    )
    heads = parts[0].shape[1] // size - 2
    queries, key_values = shape(parts, row_scale, query_gain, key_gain, cos, sin)
    others = [
        bring(key_values, z_lo=1),
        bring(key_values, z_hi=1),
        bring(key_values, z_lo=1, z_hi=1),
    ]
    others, left, right = lax.optimization_barrier(
        (others, bring(queries, x=1), bring(queries, x=ring - 1))
    )
    near = along_y(jnp.stack([key_values, *others])).reshape(-1, 2 * size)
    near, across = lax.optimization_barrier((near, bring(queries, x=2)))
    queries = [queries, left, across, right]
    far = bring(near, core=1)
    totals = attend(queries, near, hide, None, heads, size)
    parts = along_x(attend(queries, far, hide, totals, heads, size), -1)
    main = model_width // 4 * 3
    rest = model_width - main
    resid, moe_in, outgoing = finish(
        parts, w_out_all, tokens, moe_gain, pick, pick_last, heads, size, main
    )

    def exchange(x):
        wide = x.shape[1]
        x = lax.all_to_all(
            x.reshape(count, GROUP, wide), ("ctx", "exp"), split_axis=0, concat_axis=0, tiled=True
        )
        return x.reshape(count * GROUP, wide)

    first = exchange(outgoing)
    second = exchange(dispatch(moe_in, pick, main // rest, rest))
    first, moe_in = lax.optimization_barrier((first, moe_in))
    weights, last_weights = weigh(moe_in, router, named, pick, pick_last)
    partial, ninth = up_first(first, w_gate_up, w_down, main)
    returned = exchange(expert(second, w_gate_up, partial, ninth, w_down, main // rest))
    return combine(returned, weights, last_weights, resid)


def solution(mesh):
    return jax.shard_map(
        on_device,
        mesh=mesh,
        in_specs=(
            P(("ctx", "exp"), None),
            P(),
            P(),
            P(),
            P(),
            P(None, "exp"),
            P("exp", None),
            P(),
            P(),
            P(("ctx", "exp"), None),
            P(("ctx", "exp"), None, None),
            P(("ctx", "exp"), None, None),
        ),
        out_specs=P(("ctx", "exp"), None),
        check_vma=False,
    )
```

```python
import functools
import math

import jax
import jax.numpy as jnp
from jax import lax
from jax.experimental import pallas as pl
from jax.experimental.pallas import tpu as pltpu
from jax.sharding import PartitionSpec as P

rope_base = 1000000.0
GROUP = 8
VMEM_MB = 60
HIDDEN = -30000.0


def rms_scale(values, gain):
    widened = values.astype(jnp.float32)
    return (
        widened
        * lax.rsqrt(jnp.mean(widened * widened, axis=-1, keepdims=True) + 1e-06)
        * gain.astype(jnp.float32)
    )


def params(megabytes=VMEM_MB):
    return pltpu.CompilerParams(
        vmem_limit_bytes=megabytes * 1024 * 1024, dimension_semantics=("arbitrary",)
    )


def f32dot(a, b):
    return jnp.dot(a, b, preferred_element_type=jnp.float32)


def whole_block(shape):
    zeros = (0,) * len(shape)
    return pl.BlockSpec(shape, lambda *_: zeros, pipeline_mode=pl.Buffered(1))


def project_kernel(order_ref, *refs):
    ring = (len(refs) - 3) // 2
    x_refs, (near_ref, far_ref), out_refs, whole = (
        refs[:ring],
        refs[ring : ring + 2],
        refs[ring + 2 : -1],
        refs[-1],
    )
    half, columns = near_ref.shape[:2]
    rows = x_refs[0].shape[0]
    for e in range(2 * half):
        at = order_ref[e]
        near = near_ref[lax.rem(at, half)].astype(jnp.float32)
        far = far_ref[lax.rem(at, half)].astype(jnp.float32)
        whole[e * columns : (e + 1) * columns, :] = jnp.where(at < half, near, far).astype(
            jnp.bfloat16
        )
    x = jnp.concatenate([ref[...] for ref in x_refs], axis=0)
    out = lax.dot_general(
        x, whole[...], (((1,), (1,)), ((), ())), preferred_element_type=jnp.float32
    ).astype(jnp.bfloat16)
    for at, ref in enumerate(out_refs):
        ref[...] = out[at * rows : (at + 1) * rows]


def project(shares, near, far, order):
    rows, depth = shares[0].shape
    half, columns = near.shape[:2]
    out = jax.ShapeDtypeStruct((rows, 2 * half * columns), jnp.bfloat16)
    return pl.pallas_call(
        project_kernel,
        grid_spec=pltpu.PrefetchScalarGridSpec(
            num_scalar_prefetch=1,
            grid=(1,),
            in_specs=[whole_block(x.shape) for x in (*shares, near, far)],
            out_specs=[whole_block(out.shape)] * len(shares),
            scratch_shapes=[pltpu.VMEM((2 * half * columns, depth), jnp.bfloat16)],
        ),
        out_shape=[out] * len(shares),
        compiler_params=params(16),
        name="project",
    )(order, *shares, near, far)


def shape_kernel(heads, size, *refs):
    parts, (scale_ref, qgain_ref, kgain_ref, cos_ref, sin_ref, q_ref, kv_ref) = refs[:-7], refs[-7:]
    mixed = parts[0][...].astype(jnp.float32)
    for ref in parts[1:]:
        mixed = mixed + ref[...].astype(jnp.float32)
    mixed = mixed * scale_ref[...]
    half = size // 2

    def rope(values, gain):
        scale = lax.rsqrt(jnp.mean(values * values, axis=1, keepdims=True) + 1e-06)
        values = values * scale * gain.astype(jnp.float32)
        turned = jnp.concatenate([values[:, half:], values[:, :half]], axis=1)
        return values * cos_ref[...] + turned * sin_ref[...]

    for h in range(heads):
        part = slice(h * size, (h + 1) * size)
        q = rope(mixed[:, part], qgain_ref[...]) * (math.log2(math.e) / math.sqrt(size))
        q_ref[:, part] = q.astype(jnp.bfloat16)
    at = heads * size
    kv_ref[:, :size] = rope(mixed[:, at : at + size], kgain_ref[...]).astype(jnp.bfloat16)
    kv_ref[:, size:] = mixed[:, at + size :].astype(jnp.bfloat16)


def shape(parts, scale, query_gain, key_gain, cos, sin):
    rows, columns = parts[0].shape
    size = query_gain.shape[0]
    heads = columns // size - 2
    return pl.pallas_call(
        functools.partial(shape_kernel, heads, size),
        out_shape=[
            jax.ShapeDtypeStruct((rows, heads * size), jnp.bfloat16),
            jax.ShapeDtypeStruct((rows, 2 * size), jnp.bfloat16),
        ],
        compiler_params=pltpu.CompilerParams(vmem_limit_bytes=8 * 1024 * 1024),
        name="shape",
    )(*parts, scale, query_gain.reshape(1, -1), key_gain.reshape(1, -1), cos, sin)


def attend_kernel(heads, size, width, ring, last, first, *refs):
    q_refs, (kv_ref, hide_ref), refs = refs[:ring], refs[ring : ring + 2], refs[ring + 2 :]
    step = pl.program_id(0)
    index = step + first
    rows = q_refs[0].shape[0]
    length = kv_ref.shape[0]
    before_ref, (held, keys, values) = refs[0] if last else None, refs[-3:]
    out_refs = refs[1:-3] if last else refs[:-3]

    @pl.when(step == 0)
    def _():
        for at, ref in enumerate(q_refs):
            held[at] = ref[...]
        keys[:size, :] = kv_ref[:, :size].T
        keys[size:, :] = hide_ref[...]
        values[:, :size] = kv_ref[:, size:]
        values[:, size:] = jnp.ones((length, size), jnp.bfloat16)

    mark = lax.broadcasted_iota(jnp.int32, (rows, size), 1) == index
    mark = jnp.where(mark, 1.0, 0.0).astype(jnp.bfloat16)
    row = lax.broadcasted_iota(jnp.int32, (rows, width), 0)
    key = lax.broadcasted_iota(jnp.int32, (rows, width), 1)
    later = (key > row) & (key < rows) & (index == 0)
    totals = []
    for h in range(heads):
        q = jnp.concatenate([held[step, :, h * size : (h + 1) * size], mark], axis=1)
        if last:
            total = before_ref[0, h]
        else:
            total = jnp.zeros((rows, 2 * size), jnp.float32)
        for start in range(0, length, width):
            part = pl.ds(start, width)
            scores = f32dot(q, keys[:, part])
            if start == 0 and not last:
                scores = jnp.where(later, HIDDEN, scores)
            total = total + f32dot(jnp.exp2(scores).astype(jnp.bfloat16), values[part, :])
        totals.append(total)
    if not last:
        for h in range(heads):
            out_refs[0][0, h] = totals[h]
        return
    lane = lax.broadcasted_iota(jnp.int32, (rows, size), 1)
    sums = jnp.zeros((rows, size), jnp.float32)
    results = []
    for h, total in enumerate(totals):
        results.append(total[:, :size].astype(jnp.bfloat16))
        high = total[:, size:].astype(jnp.bfloat16).astype(jnp.float32)
        sums = jnp.where(lane == 2 * h, high, sums)
        sums = jnp.where(lane == 2 * h + 1, total[:, size:] - high, sums)
    packed = jnp.concatenate([*results, sums.astype(jnp.bfloat16)], axis=1)
    for at, ref in enumerate(out_refs):

        @pl.when(step == at)
        def _(ref=ref):
            ref[...] = packed


def attend(queries, key_values, hide, before, heads, size, first=0):
    rows, columns = queries[0].shape
    ring = len(queries)
    length = key_values.shape[0]
    last = before is not None
    totals = (heads, rows, 2 * size)
    totals_spec = pl.BlockSpec((1, *totals), lambda i: (i + first, 0, 0, 0))
    in_specs = [whole_block(x.shape) for x in (*queries, key_values)]
    in_specs.append(
        pl.BlockSpec((size, length), lambda i: (0, int(last)), pipeline_mode=pl.Buffered(1))
    )
    operands = [*queries, key_values, hide]
    if last:
        in_specs.append(totals_spec)
        operands.append(before)
        out = jax.ShapeDtypeStruct((rows, columns + size), jnp.bfloat16)
        out_specs, out_shape = [whole_block(out.shape)] * ring, [out] * ring
    else:
        out_specs = totals_spec
        out_shape = jax.ShapeDtypeStruct((ring, *totals), jnp.float32)
    return pl.pallas_call(
        functools.partial(attend_kernel, heads, size, 512, ring, last, first),
        grid=(ring,),
        in_specs=in_specs,
        out_specs=out_specs,
        scratch_shapes=[
            pltpu.VMEM((ring, rows, columns), jnp.bfloat16),
            pltpu.VMEM((2 * size, length), jnp.bfloat16),
            pltpu.VMEM((length, 2 * size), jnp.bfloat16),
        ],
        out_shape=out_shape,
        compiler_params=params(20),
        cost_estimate=pl.CostEstimate(
            flops=16 * heads * rows * ring * length * size,
            bytes_accessed=8000000,
            transcendentals=heads * rows * ring * length,
        ),
        name="attend",
    )(*operands)


def repeat_rows(values):
    rows = values.shape[0]
    row = lax.broadcasted_iota(jnp.int32, (rows * GROUP, rows), 0)
    column = lax.broadcasted_iota(jnp.int32, (rows * GROUP, rows), 1)
    copies = (lax.div(row, GROUP) == column).astype(jnp.bfloat16)
    return f32dot(copies, values)


def slots_kernel(routes_ref, pick_ref, last_ref, named_ref):
    fanout, tokens = routes_ref.shape
    count = named_ref.shape[0]
    expert = lax.broadcasted_iota(jnp.int32, (count, tokens), 0)
    named = jnp.zeros((count, tokens), jnp.float32)
    for j in range(fanout):
        named = named + jnp.where(routes_ref[j : j + 1, :] == expert, 1.0, 0.0)
    earlier = lax.broadcasted_iota(jnp.int32, (tokens, tokens), 0)
    later = lax.broadcasted_iota(jnp.int32, (tokens, tokens), 1)
    before = (earlier < later).astype(jnp.bfloat16)
    rank = f32dot(named.astype(jnp.bfloat16), before)
    code = named * (rank + 1.0)
    named_ref[...] = named
    last_ref[...] = (code == GROUP + 1.0).astype(jnp.bfloat16)
    spread = repeat_rows(code.astype(jnp.bfloat16))
    slot = lax.rem(lax.broadcasted_iota(jnp.int32, spread.shape, 0), GROUP) + 1
    pick_ref[...] = (spread == slot.astype(jnp.float32)).astype(jnp.bfloat16)


def slots(routes_t, count):
    fanout, tokens = routes_t.shape
    return pl.pallas_call(
        slots_kernel,
        out_shape=[
            jax.ShapeDtypeStruct((count * GROUP, tokens), jnp.bfloat16),
            jax.ShapeDtypeStruct((count, tokens), jnp.bfloat16),
            jax.ShapeDtypeStruct((count, tokens), jnp.float32),
        ],
        compiler_params=pltpu.CompilerParams(vmem_limit_bytes=VMEM_MB * 1024 * 1024),
        name="slots",
    )(routes_t)


def weigh_kernel(x_ref, router_ref, named_ref, pick_ref, last_ref, out_ref, out_last_ref):
    logits = lax.dot_general(
        router_ref[...], x_ref[...], (((0,), (1,)), ((), ())), preferred_element_type=jnp.float32
    )
    named = named_ref[...] > 0.5
    largest = jnp.max(jnp.where(named, logits, -jnp.inf), axis=0, keepdims=True)
    shares = jnp.where(named, jnp.exp(jnp.minimum(logits - largest, 0.0)), 0.0)
    shares = shares / jnp.sum(shares, axis=0, keepdims=True)
    shares = shares.astype(jnp.bfloat16)
    out_ref[...] = (repeat_rows(shares).astype(jnp.bfloat16) * pick_ref[...]).T
    out_last_ref[...] = (shares * last_ref[...]).T


def weigh(moe_in, router, named, pick, last):
    tokens = moe_in.shape[0]
    return pl.pallas_call(
        weigh_kernel,
        out_shape=[
            jax.ShapeDtypeStruct((tokens, pick.shape[0]), jnp.bfloat16),
            jax.ShapeDtypeStruct((tokens, last.shape[0]), jnp.bfloat16),
        ],
        compiler_params=pltpu.CompilerParams(vmem_limit_bytes=VMEM_MB * 1024 * 1024),
        name="weigh",
    )(moe_in, router, named, pick, last)


def fold(rows):
    count, features = rows.shape
    return rows.reshape(count, GROUP, features // GROUP).reshape(count * GROUP, features // GROUP)


def unfold(rows):
    count, piece = rows.shape
    return rows.reshape(count // GROUP, GROUP, piece).reshape(count // GROUP, GROUP * piece)


def finish_kernel(
    heads,
    size,
    features,
    *refs,
):
    parts_refs, refs = refs[:-12], refs[-12:]
    w_ref, x_ref, gain_ref, pick_ref, last_ref, resid_hbm, norm_hbm, out_ref = refs[:8]
    resid_ref, norm_ref, resid_sent, norm_sent = refs[8:]
    copies = (
        pltpu.make_async_copy(resid_ref, resid_hbm, resid_sent),
        pltpu.make_async_copy(norm_ref, norm_hbm, norm_sent),
    )

    @pl.when(pl.program_id(0) == 0)
    def _():
        summed = parts_refs[0][...].astype(jnp.float32)
        for ref in parts_refs[1:]:
            summed = summed + ref[...].astype(jnp.float32)
        base = heads * size
        attended = []
        for h in range(heads):
            at = base + 2 * h
            total = summed[:, at : at + 1] + summed[:, at + 1 : at + 2]
            attended.append((summed[:, h * size : (h + 1) * size] / total).astype(jnp.bfloat16))
        projected = f32dot(jnp.concatenate(attended, axis=1), w_ref[...])
        resid = x_ref[...].astype(jnp.float32) + projected
        resid_ref[...] = resid
        scale = lax.rsqrt(jnp.mean(resid * resid, axis=1, keepdims=True) + 1e-06)
        norm_ref[...] = (resid * scale * gain_ref[...].astype(jnp.float32)).astype(jnp.bfloat16)
        for copy in copies:
            copy.start()

    out_ref[:, :features] = f32dot(pick_ref[...], norm_ref[:, :features]).astype(jnp.bfloat16)
    out_ref[:, features:] = fold(f32dot(last_ref[...], norm_ref[...]).astype(jnp.bfloat16))

    @pl.when(pl.program_id(0) == pl.num_programs(0) - 1)
    def _():
        for copy in copies:
            copy.wait()


def finish(parts, w_out, tokens, gain, pick, last, heads, size, features):
    rows, count = pick.shape[0], last.shape[0]
    wide = features + tokens.shape[1] // GROUP
    blocks = 4
    return pl.pallas_call(
        functools.partial(finish_kernel, heads, size, features),
        grid=(blocks,),
        in_specs=[
            *(whole_block(x.shape) for x in parts),
            whole_block(w_out.shape),
            whole_block(tokens.shape),
            whole_block((1, gain.shape[0])),
            pl.BlockSpec((rows // blocks, pick.shape[1]), lambda i: (i, 0)),
            pl.BlockSpec((count // blocks, pick.shape[1]), lambda i: (i, 0)),
        ],
        out_specs=[
            pl.BlockSpec(memory_space=pl.ANY),
            pl.BlockSpec(memory_space=pl.ANY),
            pl.BlockSpec((rows // blocks, wide), lambda i: (i, 0)),
        ],
        scratch_shapes=[
            pltpu.VMEM(tokens.shape, jnp.float32),
            pltpu.VMEM(tokens.shape, jnp.bfloat16),
            pltpu.SemaphoreType.DMA(()),
            pltpu.SemaphoreType.DMA(()),
        ],
        out_shape=[
            jax.ShapeDtypeStruct(tokens.shape, jnp.float32),
            jax.ShapeDtypeStruct(tokens.shape, jnp.bfloat16),
            jax.ShapeDtypeStruct((rows, wide), jnp.bfloat16),
        ],
        compiler_params=params(57),
        name="finish",
    )(*parts, w_out, tokens, gain.reshape(1, -1), pick, last)


def dispatch_kernel(x_ref, pick_ref, out_ref):
    out_ref[...] = f32dot(pick_ref[...], x_ref[...]).astype(jnp.bfloat16)


def dispatch(normed, pick, chunk, features):
    rows, tokens = pick.shape
    blocks = 4
    return pl.pallas_call(
        dispatch_kernel,
        grid=(blocks,),
        in_specs=[
            pl.BlockSpec((tokens, features), lambda i: (0, chunk)),
            pl.BlockSpec((rows // blocks, tokens), lambda i: (i, 0)),
        ],
        out_specs=pl.BlockSpec((rows // blocks, features), lambda i: (i, 0)),
        out_shape=jax.ShapeDtypeStruct((rows, features), jnp.bfloat16),
        compiler_params=params(),
        cost_estimate=pl.CostEstimate(
            flops=4 * rows * tokens * features, bytes_accessed=4 * rows * features, transcendentals=0
        ),
        name="dispatch",
    )(normed, pick)


def gated(gate_up):
    hidden = gate_up.shape[1] // 2
    gate = gate_up[:, :hidden]
    return (gate / (1.0 + jnp.exp(-gate)) * gate_up[:, hidden:]).astype(jnp.bfloat16)


def up_kernel(features, x_ref, wu_ref, wd_ref, out_ref, ninth_ref, last):
    index = pl.program_id(0)
    lasts = x_ref.shape[0] // GROUP
    out_ref[...] = f32dot(x_ref[:, :features], wu_ref[0, :features, :])
    last[pl.ds(pl.multiple_of(index * lasts, lasts), lasts), :] = unfold(x_ref[:, features:])

    @pl.when(index == pl.num_programs(0) - 1)
    def _():
        active = gated(f32dot(last[...], wu_ref[0]))
        ninth_ref[...] = fold(f32dot(active, wd_ref[0]).astype(jnp.bfloat16))


def up_first(received, w_up, w_down, features):
    rows, wide = received.shape
    columns = w_up.shape[2]
    width = w_down.shape[2]
    blocks = 4
    return pl.pallas_call(
        functools.partial(up_kernel, features),
        grid=(blocks,),
        in_specs=[
            pl.BlockSpec((rows // blocks, wide), lambda i: (i, 0)),
            whole_block(w_up.shape),
            whole_block(w_down.shape),
        ],
        out_specs=[
            pl.BlockSpec((rows // blocks, columns), lambda i: (i, 0)),
            pl.BlockSpec((rows, width // GROUP), lambda i: (0, 0)),
        ],
        out_shape=[
            jax.ShapeDtypeStruct((rows, columns), jnp.float32),
            jax.ShapeDtypeStruct((rows, width // GROUP), jnp.bfloat16),
        ],
        scratch_shapes=[pltpu.VMEM((rows // GROUP, width), jnp.bfloat16)],
        compiler_params=params(),
        cost_estimate=pl.CostEstimate(
            flops=2 * rows * features * columns, bytes_accessed=20000000, transcendentals=0
        ),
        name="up_first",
    )(received, w_up, w_down)


def expert_kernel(x_ref, wu_ref, partial_ref, ninth_ref, wd_hbm, out_ref, wd, arrived):
    index = pl.program_id(0)
    copy = pltpu.make_async_copy(wd_hbm.at[0], wd, arrived)

    @pl.when(index == 0)
    def _():
        copy.start()

    active = gated(partial_ref[...] + f32dot(x_ref[...], wu_ref[0]))

    @pl.when(index == 0)
    def _():
        copy.wait()

    width = wd.shape[1]
    out_ref[:, :width] = f32dot(active, wd[...]).astype(jnp.bfloat16)
    out_ref[:, width:] = ninth_ref[...]


def expert(received, w_up, partial, ninth, w_down, chunk):
    rows, features = received.shape
    columns = w_up.shape[2]
    hidden, width = w_down.shape[1:]
    blocks = 4
    out_wide = width + width // GROUP
    return pl.pallas_call(
        expert_kernel,
        grid=(blocks,),
        in_specs=[
            pl.BlockSpec((rows // blocks, features), lambda i: (i, 0)),
            pl.BlockSpec(
                (1, features, columns), lambda i: (0, chunk, 0), pipeline_mode=pl.Buffered(1)
            ),
            pl.BlockSpec((rows // blocks, columns), lambda i: (i, 0)),
            pl.BlockSpec((rows // blocks, width // GROUP), lambda i: (i, 0)),
            pl.BlockSpec(memory_space=pl.ANY),
        ],
        out_specs=pl.BlockSpec((rows // blocks, out_wide), lambda i: (i, 0)),
        out_shape=jax.ShapeDtypeStruct((rows, out_wide), jnp.bfloat16),
        scratch_shapes=[pltpu.VMEM((hidden, width), jnp.bfloat16), pltpu.SemaphoreType.DMA(())],
        compiler_params=params(55),
        cost_estimate=pl.CostEstimate(
            flops=2 * rows * (features * columns + hidden * width),
            bytes_accessed=30000000,
            transcendentals=0,
        ),
        name="expert",
    )(received, w_up, partial, ninth, w_down)


def combine_kernel(x_ref, ninth_ref, w_ref, wlast_ref, resid_ref, out_ref, last):
    width = resid_ref.shape[1]
    index = pl.program_id(0)

    @pl.when(index == 0)
    def _():
        last[...] = unfold(ninth_ref[...])

    own = last[:, pl.ds(pl.multiple_of(index * width, width), width)]
    added = f32dot(w_ref[...], x_ref[...]) + f32dot(wlast_ref[...], own)
    out_ref[...] = (resid_ref[...] + added).astype(jnp.bfloat16)


def combine(returned, weights, last_weights, resid):
    rows = returned.shape[0]
    tokens, features = resid.shape
    count = last_weights.shape[1]
    blocks = 2
    width = features // blocks
    return pl.pallas_call(
        combine_kernel,
        grid=(blocks,),
        in_specs=[
            pl.BlockSpec((rows, width), lambda i: (0, i)),
            pl.BlockSpec(
                (rows, features // GROUP), lambda i: (0, GROUP), pipeline_mode=pl.Buffered(1)
            ),
            whole_block((tokens, rows)),
            whole_block((tokens, count)),
            pl.BlockSpec((tokens, width), lambda i: (0, i)),
        ],
        out_specs=pl.BlockSpec((tokens, width), lambda i: (0, i)),
        out_shape=jax.ShapeDtypeStruct((tokens, features), jnp.bfloat16),
        scratch_shapes=[pltpu.VMEM((count, features), jnp.bfloat16)],
        compiler_params=params(),
        name="combine",
    )(returned, returned, weights, last_weights, resid)


def on_device(
    tokens,
    block_order,
    attn_gain,
    query_gain,
    key_gain,
    w_qkv,
    w_out,
    moe_gain,
    router,
    routes,
    w_gate_up,
    w_down,
):
    rows, model_width = tokens.shape
    size = query_gain.shape[0]
    ctx_size, exp_size = lax.axis_size("ctx"), lax.axis_size("exp")
    ctx_at, exp_at = lax.axis_index("ctx"), lax.axis_index("exp")
    ring = 4
    inner = exp_size // ring
    x_at, z_lo = ctx_at % ring, ctx_at // ring
    y_at, z_hi, core = exp_at // inner, exp_at // 2 % 2, exp_at % 2

    def device(z_lo, x, y, z_hi, core):
        return (z_lo * ring + x) * exp_size + y * inner + z_hi * 2 + core

    def bring(value, z_lo=0, x=0, y=0, z_hi=0, core=0):
        pairs = []
        for at in range(ctx_size * exp_size):
            c, e = at // exp_size, at % exp_size
            source = device(
                c // ring ^ z_lo,
                (c - x) % ring,
                (e // inner - y) % ring,
                e // 2 % 2 ^ z_hi,
                e % 2 ^ core,
            )
            pairs.append((source, at))
        return lax.ppermute(value, ("ctx", "exp"), pairs)

    def along_y(value):
        return jnp.concatenate([value] + [bring(value, y=k) for k in range(1, ring)])

    def along_x(values, step):
        return [values[0]] + [bring(values[k], x=step * k) for k in range(1, ring)]

    relative = jnp.arange(exp_size, dtype=jnp.int32)
    piece_of = (
        (core + relative) % 2 * (2 * ring)
        + (y_at - relative // inner) % ring * 2
        + (z_hi + relative // 2) % 2
    )
    relative = jnp.arange(2 * exp_size, dtype=jnp.int32)
    key_devices = device(
        (z_lo + relative) % 2,
        x_at,
        (y_at - relative // 4) % ring,
        (z_hi + relative // 2) % 2,
        (core + relative // (4 * ring)) % 2,
    )
    steps = jnp.arange(ring, dtype=jnp.int32)
    query_devices = device(z_lo, (x_at - steps) % ring, y_at, z_hi, core)

    def block_numbers(devices):
        every = jnp.arange(block_order.shape[0], dtype=jnp.int32)
        return jnp.sum(
            jnp.where(devices[:, None] == every[None, :], block_order[None, :], 0), axis=1
        )

    k_blocks = block_numbers(key_devices)
    q_blocks = block_numbers(query_devices)
    own_pos = q_blocks[0] * rows + jnp.arange(rows, dtype=jnp.int32)
    hide = jnp.repeat(
        jnp.where(k_blocks[None, :] > q_blocks[:, None], HIDDEN, 0.0), rows, axis=1
    )
    hide = jnp.pad(hide, ((0, size - ring), (0, 0))).astype(jnp.bfloat16)

    depth = model_width // ring
    widened = tokens.astype(jnp.float32)
    row_scale = lax.rsqrt(jnp.mean(widened * widened, axis=1, keepdims=True) + 1e-06)
    gained = (widened * attn_gain.astype(jnp.float32)).astype(jnp.bfloat16)
    w_share = lax.dynamic_slice_in_dim(w_qkv.T, x_at * depth, depth, 1)
    other, gained = lax.optimization_barrier((bring(w_share, z_hi=1), gained))
    near = along_y(jnp.stack([w_share, other]))
    shares = along_x(
        [
            lax.dynamic_slice_in_dim(gained, (x_at + k) % ring * depth, depth, 1)
            for k in range(ring)
        ],
        1,
    )
    near, shares = lax.optimization_barrier((near, shares))
    far = bring(near, core=1)
    w_out_all = lax.all_gather(w_out, "exp", axis=0, tiled=True)
    shares = project(shares, near, far, piece_of)
    shares, routes = lax.optimization_barrier((shares, routes))
    count = router.shape[1]
    pick, pick_last, named = slots(routes.T, count)
    half = size // 2
    freqs = jnp.exp(
        -math.log(rope_base) * jnp.arange(half, dtype=jnp.float32) * 2.0 / size
    )
    angles = own_pos.astype(jnp.float32)[:, None] * freqs[None, :]
    cos, sin = jnp.cos(angles), jnp.sin(angles)
    cos = jnp.concatenate([cos, cos], axis=1)
    sin = jnp.concatenate([-sin, sin], axis=1)
    parts = along_x(shares, -1)
    parts, pick, pick_last, named, hide, cos, sin = lax.optimization_barrier(
        (parts, pick, pick_last, named, hide, cos, sin)
    )
    heads = parts[0].shape[1] // size - 2
    queries, key_values = shape(parts, row_scale, query_gain, key_gain, cos, sin)
    others = [
        bring(key_values, z_lo=1),
        bring(key_values, z_hi=1),
        bring(key_values, z_lo=1, z_hi=1),
    ]
    others, left, right = lax.optimization_barrier(
        (others, bring(queries, x=1), bring(queries, x=ring - 1))
    )
    near = along_y(jnp.stack([key_values, *others])).reshape(-1, 2 * size)
    near, across = lax.optimization_barrier((near, bring(queries, x=2)))
    queries = [queries, left, across, right]
    far = bring(near, core=1)
    totals = attend(queries, near, hide, None, heads, size)
    others = attend(queries[1:], far, hide, totals, heads, size, 1)
    own = attend(queries[:1], far, hide, totals, heads, size)
    parts = along_x([*own, *others], -1)
    main = model_width // 4 * 3
    rest = model_width - main
    resid, moe_in, outgoing = finish(
        parts, w_out_all, tokens, moe_gain, pick, pick_last, heads, size, main
    )

    def exchange(x):
        wide = x.shape[1]
        x = lax.all_to_all(
            x.reshape(count, GROUP, wide), ("ctx", "exp"), split_axis=0, concat_axis=0, tiled=True
        )
        return x.reshape(count * GROUP, wide)

    first = exchange(outgoing)
    second = exchange(dispatch(moe_in, pick, main // rest, rest))
    first, moe_in = lax.optimization_barrier((first, moe_in))
    weights, last_weights = weigh(moe_in, router, named, pick, pick_last)
    partial, ninth = up_first(first, w_gate_up, w_down, main)
    returned = exchange(expert(second, w_gate_up, partial, ninth, w_down, main // rest))
    return combine(returned, weights, last_weights, resid)


def solution(mesh):
    return jax.shard_map(
        on_device,
        mesh=mesh,
        in_specs=(
            P(("ctx", "exp"), None),
            P(),
            P(),
            P(),
            P(),
            P(None, "exp"),
            P("exp", None),
            P(),
            P(),
            P(("ctx", "exp"), None),
            P(("ctx", "exp"), None, None),
            P(("ctx", "exp"), None, None),
        ),
        out_specs=P(("ctx", "exp"), None),
        check_vma=False,
    )
```

```python
import functools
import math

import jax
import jax.numpy as jnp
from jax import lax
from jax.experimental import pallas as pl
from jax.experimental.pallas import tpu as pltpu
from jax.sharding import PartitionSpec as P

rope_base = 1000000.0
GROUP = 8
VMEM_MB = 60
HIDDEN = -30000.0


def rms_scale(values, gain):
    widened = values.astype(jnp.float32)
    return (
        widened
        * lax.rsqrt(jnp.mean(widened * widened, axis=-1, keepdims=True) + 1e-06)
        * gain.astype(jnp.float32)
    )


def params(megabytes=VMEM_MB):
    return pltpu.CompilerParams(
        vmem_limit_bytes=megabytes * 1024 * 1024, dimension_semantics=("arbitrary",)
    )


def f32dot(a, b):
    return jnp.dot(a, b, preferred_element_type=jnp.float32)


def whole_block(shape):
    zeros = (0,) * len(shape)
    return pl.BlockSpec(shape, lambda *_: zeros, pipeline_mode=pl.Buffered(1))


def project_kernel(order_ref, *refs):
    ring = (len(refs) - 3) // 2
    x_refs, (near_ref, far_ref), out_refs, whole = (
        refs[:ring],
        refs[ring : ring + 2],
        refs[ring + 2 : -1],
        refs[-1],
    )
    half, columns = near_ref.shape[:2]
    rows = x_refs[0].shape[0]
    for e in range(2 * half):
        at = order_ref[e]
        near = near_ref[lax.rem(at, half)].astype(jnp.float32)
        far = far_ref[lax.rem(at, half)].astype(jnp.float32)
        whole[e * columns : (e + 1) * columns, :] = jnp.where(at < half, near, far).astype(
            jnp.bfloat16
        )
    x = jnp.concatenate([ref[...] for ref in x_refs], axis=0)
    out = lax.dot_general(
        x, whole[...], (((1,), (1,)), ((), ())), preferred_element_type=jnp.float32
    ).astype(jnp.bfloat16)
    for at, ref in enumerate(out_refs):
        ref[...] = out[at * rows : (at + 1) * rows]


def project(shares, near, far, order):
    rows, depth = shares[0].shape
    half, columns = near.shape[:2]
    out = jax.ShapeDtypeStruct((rows, 2 * half * columns), jnp.bfloat16)
    return pl.pallas_call(
        project_kernel,
        grid_spec=pltpu.PrefetchScalarGridSpec(
            num_scalar_prefetch=1,
            grid=(1,),
            in_specs=[whole_block(x.shape) for x in (*shares, near, far)],
            out_specs=[whole_block(out.shape)] * len(shares),
            scratch_shapes=[pltpu.VMEM((2 * half * columns, depth), jnp.bfloat16)],
        ),
        out_shape=[out] * len(shares),
        compiler_params=params(16),
        name="project",
    )(order, *shares, near, far)


def shape_kernel(heads, size, *refs):
    parts, (scale_ref, qgain_ref, kgain_ref, cos_ref, sin_ref, q_ref, kv_ref) = refs[:-7], refs[-7:]
    mixed = parts[0][...].astype(jnp.float32)
    for ref in parts[1:]:
        mixed = mixed + ref[...].astype(jnp.float32)
    mixed = mixed * scale_ref[...]
    half = size // 2

    def rope(values, gain):
        scale = lax.rsqrt(jnp.mean(values * values, axis=1, keepdims=True) + 1e-06)
        values = values * scale * gain.astype(jnp.float32)
        turned = jnp.concatenate([values[:, half:], values[:, :half]], axis=1)
        return values * cos_ref[...] + turned * sin_ref[...]

    for h in range(heads):
        part = slice(h * size, (h + 1) * size)
        q = rope(mixed[:, part], qgain_ref[...]) * (math.log2(math.e) / math.sqrt(size))
        q_ref[:, part] = q.astype(jnp.bfloat16)
    at = heads * size
    kv_ref[:, :size] = rope(mixed[:, at : at + size], kgain_ref[...]).astype(jnp.bfloat16)
    kv_ref[:, size:] = mixed[:, at + size :].astype(jnp.bfloat16)


def shape(parts, scale, query_gain, key_gain, cos, sin):
    rows, columns = parts[0].shape
    size = query_gain.shape[0]
    heads = columns // size - 2
    return pl.pallas_call(
        functools.partial(shape_kernel, heads, size),
        out_shape=[
            jax.ShapeDtypeStruct((rows, heads * size), jnp.bfloat16),
            jax.ShapeDtypeStruct((rows, 2 * size), jnp.bfloat16),
        ],
        compiler_params=pltpu.CompilerParams(vmem_limit_bytes=8 * 1024 * 1024),
        name="shape",
    )(*parts, scale, query_gain.reshape(1, -1), key_gain.reshape(1, -1), cos, sin)


def attend_kernel(heads, size, width, ring, last, first, *refs):
    q_refs, (kv_ref, hide_ref), refs = refs[:ring], refs[ring : ring + 2], refs[ring + 2 :]
    step = pl.program_id(0)
    index = step + first
    rows = q_refs[0].shape[0]
    length = kv_ref.shape[0]
    before_ref, (held, keys, values) = refs[0] if last else None, refs[-3:]
    out_refs = refs[1:-3] if last else refs[:-3]

    @pl.when(step == 0)
    def _():
        for at, ref in enumerate(q_refs):
            held[at] = ref[...]
        keys[:size, :] = kv_ref[:, :size].T
        keys[size:, :] = hide_ref[...]
        values[:, :size] = kv_ref[:, size:]
        values[:, size:] = jnp.ones((length, size), jnp.bfloat16)

    mark = lax.broadcasted_iota(jnp.int32, (rows, size), 1) == index
    mark = jnp.where(mark, 1.0, 0.0).astype(jnp.bfloat16)
    row = lax.broadcasted_iota(jnp.int32, (rows, width), 0)
    key = lax.broadcasted_iota(jnp.int32, (rows, width), 1)
    later = (key > row) & (key < rows) & (index == 0)
    totals = []
    for h in range(heads):
        q = jnp.concatenate([held[step, :, h * size : (h + 1) * size], mark], axis=1)
        if last:
            total = before_ref[0, h]
        else:
            total = jnp.zeros((rows, 2 * size), jnp.float32)
        for start in range(0, length, width):
            part = pl.ds(start, width)
            scores = f32dot(q, keys[:, part])
            if start == 0 and not last:
                scores = jnp.where(later, HIDDEN, scores)
            total = total + f32dot(jnp.exp2(scores).astype(jnp.bfloat16), values[part, :])
        totals.append(total)
    if not last:
        for h in range(heads):
            out_refs[0][0, h] = totals[h]
        return
    lane = lax.broadcasted_iota(jnp.int32, (rows, size), 1)
    sums = jnp.zeros((rows, size), jnp.float32)
    results = []
    for h, total in enumerate(totals):
        results.append(total[:, :size].astype(jnp.bfloat16))
        high = total[:, size:].astype(jnp.bfloat16).astype(jnp.float32)
        sums = jnp.where(lane == 2 * h, high, sums)
        sums = jnp.where(lane == 2 * h + 1, total[:, size:] - high, sums)
    packed = jnp.concatenate([*results, sums.astype(jnp.bfloat16)], axis=1)
    for at, ref in enumerate(out_refs):

        @pl.when(step == at)
        def _(ref=ref):
            ref[...] = packed


def attend(queries, key_values, hide, before, heads, size, first=0):
    rows, columns = queries[0].shape
    ring = len(queries)
    length = key_values.shape[0]
    last = before is not None
    totals = (heads, rows, 2 * size)
    totals_spec = pl.BlockSpec((1, *totals), lambda i: (i + first, 0, 0, 0))
    in_specs = [whole_block(x.shape) for x in (*queries, key_values)]
    in_specs.append(
        pl.BlockSpec((size, length), lambda i: (0, int(last)), pipeline_mode=pl.Buffered(1))
    )
    operands = [*queries, key_values, hide]
    if last:
        in_specs.append(totals_spec)
        operands.append(before)
        out = jax.ShapeDtypeStruct((rows, columns + size), jnp.bfloat16)
        out_specs, out_shape = [whole_block(out.shape)] * ring, [out] * ring
    else:
        out_specs = totals_spec
        out_shape = jax.ShapeDtypeStruct((ring, *totals), jnp.float32)
    return pl.pallas_call(
        functools.partial(attend_kernel, heads, size, 512, ring, last, first),
        grid=(ring,),
        in_specs=in_specs,
        out_specs=out_specs,
        scratch_shapes=[
            pltpu.VMEM((ring, rows, columns), jnp.bfloat16),
            pltpu.VMEM((2 * size, length), jnp.bfloat16),
            pltpu.VMEM((length, 2 * size), jnp.bfloat16),
        ],
        out_shape=out_shape,
        compiler_params=params(20),
        cost_estimate=pl.CostEstimate(
            flops=16 * heads * rows * ring * length * size,
            bytes_accessed=8000000,
            transcendentals=heads * rows * ring * length,
        ),
        name="attend",
    )(*operands)


def repeat_rows(values):
    rows = values.shape[0]
    row = lax.broadcasted_iota(jnp.int32, (rows * GROUP, rows), 0)
    column = lax.broadcasted_iota(jnp.int32, (rows * GROUP, rows), 1)
    copies = (lax.div(row, GROUP) == column).astype(jnp.bfloat16)
    return f32dot(copies, values)


def slots_kernel(routes_ref, pick_ref, last_ref, named_ref):
    fanout, tokens = routes_ref.shape
    count = named_ref.shape[0]
    expert = lax.broadcasted_iota(jnp.int32, (count, tokens), 0)
    named = jnp.zeros((count, tokens), jnp.float32)
    for j in range(fanout):
        named = named + jnp.where(routes_ref[j : j + 1, :] == expert, 1.0, 0.0)
    earlier = lax.broadcasted_iota(jnp.int32, (tokens, tokens), 0)
    later = lax.broadcasted_iota(jnp.int32, (tokens, tokens), 1)
    before = (earlier < later).astype(jnp.bfloat16)
    rank = f32dot(named.astype(jnp.bfloat16), before)
    code = named * (rank + 1.0)
    named_ref[...] = named
    last_ref[...] = (code == GROUP + 1.0).astype(jnp.bfloat16)
    spread = repeat_rows(code.astype(jnp.bfloat16))
    slot = lax.rem(lax.broadcasted_iota(jnp.int32, spread.shape, 0), GROUP) + 1
    pick_ref[...] = (spread == slot.astype(jnp.float32)).astype(jnp.bfloat16)


def slots(routes_t, count):
    fanout, tokens = routes_t.shape
    return pl.pallas_call(
        slots_kernel,
        out_shape=[
            jax.ShapeDtypeStruct((count * GROUP, tokens), jnp.bfloat16),
            jax.ShapeDtypeStruct((count, tokens), jnp.bfloat16),
            jax.ShapeDtypeStruct((count, tokens), jnp.float32),
        ],
        compiler_params=pltpu.CompilerParams(vmem_limit_bytes=VMEM_MB * 1024 * 1024),
        name="slots",
    )(routes_t)


def weigh_kernel(x_ref, router_ref, named_ref, pick_ref, last_ref, out_ref, out_last_ref):
    logits = lax.dot_general(
        router_ref[...], x_ref[...], (((0,), (1,)), ((), ())), preferred_element_type=jnp.float32
    )
    named = named_ref[...] > 0.5
    largest = jnp.max(jnp.where(named, logits, -jnp.inf), axis=0, keepdims=True)
    shares = jnp.where(named, jnp.exp(jnp.minimum(logits - largest, 0.0)), 0.0)
    shares = shares / jnp.sum(shares, axis=0, keepdims=True)
    shares = shares.astype(jnp.bfloat16)
    out_ref[...] = (repeat_rows(shares).astype(jnp.bfloat16) * pick_ref[...]).T
    out_last_ref[...] = (shares * last_ref[...]).T


def weigh(moe_in, router, named, pick, last):
    tokens = moe_in.shape[0]
    return pl.pallas_call(
        weigh_kernel,
        out_shape=[
            jax.ShapeDtypeStruct((tokens, pick.shape[0]), jnp.bfloat16),
            jax.ShapeDtypeStruct((tokens, last.shape[0]), jnp.bfloat16),
        ],
        compiler_params=pltpu.CompilerParams(vmem_limit_bytes=VMEM_MB * 1024 * 1024),
        name="weigh",
    )(moe_in, router, named, pick, last)


def fold(rows):
    count, features = rows.shape
    return rows.reshape(count, GROUP, features // GROUP).reshape(count * GROUP, features // GROUP)


def unfold(rows):
    count, piece = rows.shape
    return rows.reshape(count // GROUP, GROUP, piece).reshape(count // GROUP, GROUP * piece)


def finish_kernel(
    heads,
    size,
    features,
    *refs,
):
    parts_refs, refs = refs[:-12], refs[-12:]
    w_ref, x_ref, gain_ref, pick_ref, last_ref, resid_hbm, norm_hbm, out_ref = refs[:8]
    resid_ref, norm_ref, resid_sent, norm_sent = refs[8:]
    copies = (
        pltpu.make_async_copy(resid_ref, resid_hbm, resid_sent),
        pltpu.make_async_copy(norm_ref, norm_hbm, norm_sent),
    )

    @pl.when(pl.program_id(0) == 0)
    def _():
        summed = parts_refs[0][...].astype(jnp.float32)
        for ref in parts_refs[1:]:
            summed = summed + ref[...].astype(jnp.float32)
        base = heads * size
        attended = []
        for h in range(heads):
            at = base + 2 * h
            total = summed[:, at : at + 1] + summed[:, at + 1 : at + 2]
            attended.append((summed[:, h * size : (h + 1) * size] / total).astype(jnp.bfloat16))
        projected = f32dot(jnp.concatenate(attended, axis=1), w_ref[...])
        resid = x_ref[...].astype(jnp.float32) + projected
        resid_ref[...] = resid
        scale = lax.rsqrt(jnp.mean(resid * resid, axis=1, keepdims=True) + 1e-06)
        norm_ref[...] = (resid * scale * gain_ref[...].astype(jnp.float32)).astype(jnp.bfloat16)
        for copy in copies:
            copy.start()

    out_ref[:, :features] = f32dot(pick_ref[...], norm_ref[:, :features]).astype(jnp.bfloat16)
    out_ref[:, features:] = fold(f32dot(last_ref[...], norm_ref[...]).astype(jnp.bfloat16))

    @pl.when(pl.program_id(0) == pl.num_programs(0) - 1)
    def _():
        for copy in copies:
            copy.wait()


def finish(parts, w_out, tokens, gain, pick, last, heads, size, features):
    rows, count = pick.shape[0], last.shape[0]
    wide = features + tokens.shape[1] // GROUP
    blocks = 2
    return pl.pallas_call(
        functools.partial(finish_kernel, heads, size, features),
        grid=(blocks,),
        in_specs=[
            *(whole_block(x.shape) for x in parts),
            whole_block(w_out.shape),
            whole_block(tokens.shape),
            whole_block((1, gain.shape[0])),
            pl.BlockSpec((rows // blocks, pick.shape[1]), lambda i: (i, 0)),
            pl.BlockSpec((count // blocks, pick.shape[1]), lambda i: (i, 0)),
        ],
        out_specs=[
            pl.BlockSpec(memory_space=pl.ANY),
            pl.BlockSpec(memory_space=pl.ANY),
            pl.BlockSpec((rows // blocks, wide), lambda i: (i, 0)),
        ],
        scratch_shapes=[
            pltpu.VMEM(tokens.shape, jnp.float32),
            pltpu.VMEM(tokens.shape, jnp.bfloat16),
            pltpu.SemaphoreType.DMA(()),
            pltpu.SemaphoreType.DMA(()),
        ],
        out_shape=[
            jax.ShapeDtypeStruct(tokens.shape, jnp.float32),
            jax.ShapeDtypeStruct(tokens.shape, jnp.bfloat16),
            jax.ShapeDtypeStruct((rows, wide), jnp.bfloat16),
        ],
        compiler_params=params(57),
        name="finish",
    )(*parts, w_out, tokens, gain.reshape(1, -1), pick, last)


def dispatch_kernel(x_ref, pick_ref, out_ref):
    out_ref[...] = f32dot(pick_ref[...], x_ref[...]).astype(jnp.bfloat16)


def dispatch(normed, pick, chunk, features):
    rows, tokens = pick.shape
    blocks = 4
    return pl.pallas_call(
        dispatch_kernel,
        grid=(blocks,),
        in_specs=[
            pl.BlockSpec((tokens, features), lambda i: (0, chunk)),
            pl.BlockSpec((rows // blocks, tokens), lambda i: (i, 0)),
        ],
        out_specs=pl.BlockSpec((rows // blocks, features), lambda i: (i, 0)),
        out_shape=jax.ShapeDtypeStruct((rows, features), jnp.bfloat16),
        compiler_params=params(),
        cost_estimate=pl.CostEstimate(
            flops=4 * rows * tokens * features, bytes_accessed=4 * rows * features, transcendentals=0
        ),
        name="dispatch",
    )(normed, pick)


def gated(gate_up):
    hidden = gate_up.shape[1] // 2
    gate = gate_up[:, :hidden]
    return (gate / (1.0 + jnp.exp(-gate)) * gate_up[:, hidden:]).astype(jnp.bfloat16)


def up_kernel(features, x_ref, wu_ref, wd_ref, out_ref, ninth_ref, last):
    index = pl.program_id(0)
    lasts = x_ref.shape[0] // GROUP
    out_ref[...] = f32dot(x_ref[:, :features], wu_ref[0, :features, :])
    last[pl.ds(pl.multiple_of(index * lasts, lasts), lasts), :] = unfold(x_ref[:, features:])

    @pl.when(index == pl.num_programs(0) - 1)
    def _():
        active = gated(f32dot(last[...], wu_ref[0]))
        ninth_ref[...] = fold(f32dot(active, wd_ref[0]).astype(jnp.bfloat16))


def up_first(received, w_up, w_down, features):
    rows, wide = received.shape
    columns = w_up.shape[2]
    width = w_down.shape[2]
    blocks = 4
    return pl.pallas_call(
        functools.partial(up_kernel, features),
        grid=(blocks,),
        in_specs=[
            pl.BlockSpec((rows // blocks, wide), lambda i: (i, 0)),
            whole_block(w_up.shape),
            whole_block(w_down.shape),
        ],
        out_specs=[
            pl.BlockSpec((rows // blocks, columns), lambda i: (i, 0)),
            pl.BlockSpec((rows, width // GROUP), lambda i: (0, 0)),
        ],
        out_shape=[
            jax.ShapeDtypeStruct((rows, columns), jnp.float32),
            jax.ShapeDtypeStruct((rows, width // GROUP), jnp.bfloat16),
        ],
        scratch_shapes=[pltpu.VMEM((rows // GROUP, width), jnp.bfloat16)],
        compiler_params=params(),
        cost_estimate=pl.CostEstimate(
            flops=2 * rows * features * columns, bytes_accessed=20000000, transcendentals=0
        ),
        name="up_first",
    )(received, w_up, w_down)


def expert_kernel(x_ref, wu_ref, partial_ref, ninth_ref, wd_hbm, out_ref, wd, arrived):
    index = pl.program_id(0)
    copy = pltpu.make_async_copy(wd_hbm.at[0], wd, arrived)

    @pl.when(index == 0)
    def _():
        copy.start()

    active = gated(partial_ref[...] + f32dot(x_ref[...], wu_ref[0]))

    @pl.when(index == 0)
    def _():
        copy.wait()

    width = wd.shape[1]
    out_ref[:, :width] = f32dot(active, wd[...]).astype(jnp.bfloat16)
    out_ref[:, width:] = ninth_ref[...]


def expert(received, w_up, partial, ninth, w_down, chunk):
    rows, features = received.shape
    columns = w_up.shape[2]
    hidden, width = w_down.shape[1:]
    blocks = 4
    out_wide = width + width // GROUP
    return pl.pallas_call(
        expert_kernel,
        grid=(blocks,),
        in_specs=[
            pl.BlockSpec((rows // blocks, features), lambda i: (i, 0)),
            pl.BlockSpec(
                (1, features, columns), lambda i: (0, chunk, 0), pipeline_mode=pl.Buffered(1)
            ),
            pl.BlockSpec((rows // blocks, columns), lambda i: (i, 0)),
            pl.BlockSpec((rows // blocks, width // GROUP), lambda i: (i, 0)),
            pl.BlockSpec(memory_space=pl.ANY),
        ],
        out_specs=pl.BlockSpec((rows // blocks, out_wide), lambda i: (i, 0)),
        out_shape=jax.ShapeDtypeStruct((rows, out_wide), jnp.bfloat16),
        scratch_shapes=[pltpu.VMEM((hidden, width), jnp.bfloat16), pltpu.SemaphoreType.DMA(())],
        compiler_params=params(55),
        cost_estimate=pl.CostEstimate(
            flops=2 * rows * (features * columns + hidden * width),
            bytes_accessed=30000000,
            transcendentals=0,
        ),
        name="expert",
    )(received, w_up, partial, ninth, w_down)


def combine_kernel(x_ref, ninth_ref, w_ref, wlast_ref, resid_ref, out_ref, last):
    width = resid_ref.shape[1]
    index = pl.program_id(0)

    @pl.when(index == 0)
    def _():
        last[...] = unfold(ninth_ref[...])

    own = last[:, pl.ds(pl.multiple_of(index * width, width), width)]
    added = f32dot(w_ref[...], x_ref[...]) + f32dot(wlast_ref[...], own)
    out_ref[...] = (resid_ref[...] + added).astype(jnp.bfloat16)


def combine(returned, weights, last_weights, resid):
    rows = returned.shape[0]
    tokens, features = resid.shape
    count = last_weights.shape[1]
    blocks = 2
    width = features // blocks
    return pl.pallas_call(
        combine_kernel,
        grid=(blocks,),
        in_specs=[
            pl.BlockSpec((rows, width), lambda i: (0, i)),
            pl.BlockSpec(
                (rows, features // GROUP), lambda i: (0, GROUP), pipeline_mode=pl.Buffered(1)
            ),
            whole_block((tokens, rows)),
            whole_block((tokens, count)),
            pl.BlockSpec((tokens, width), lambda i: (0, i)),
        ],
        out_specs=pl.BlockSpec((tokens, width), lambda i: (0, i)),
        out_shape=jax.ShapeDtypeStruct((tokens, features), jnp.bfloat16),
        scratch_shapes=[pltpu.VMEM((count, features), jnp.bfloat16)],
        compiler_params=params(),
        name="combine",
    )(returned, returned, weights, last_weights, resid)


def on_device(
    tokens,
    block_order,
    attn_gain,
    query_gain,
    key_gain,
    w_qkv,
    w_out,
    moe_gain,
    router,
    routes,
    w_gate_up,
    w_down,
):
    rows, model_width = tokens.shape
    size = query_gain.shape[0]
    ctx_size, exp_size = lax.axis_size("ctx"), lax.axis_size("exp")
    ctx_at, exp_at = lax.axis_index("ctx"), lax.axis_index("exp")
    ring = 4
    inner = exp_size // ring
    x_at, z_lo = ctx_at % ring, ctx_at // ring
    y_at, z_hi, core = exp_at // inner, exp_at // 2 % 2, exp_at % 2

    def device(z_lo, x, y, z_hi, core):
        return (z_lo * ring + x) * exp_size + y * inner + z_hi * 2 + core

    def bring(value, z_lo=0, x=0, y=0, z_hi=0, core=0):
        pairs = []
        for at in range(ctx_size * exp_size):
            c, e = at // exp_size, at % exp_size
            source = device(
                c // ring ^ z_lo,
                (c - x) % ring,
                (e // inner - y) % ring,
                e // 2 % 2 ^ z_hi,
                e % 2 ^ core,
            )
            pairs.append((source, at))
        return lax.ppermute(value, ("ctx", "exp"), pairs)

    def along_y(value):
        return jnp.concatenate([value] + [bring(value, y=k) for k in range(1, ring)])

    def along_x(values, step):
        return [values[0]] + [bring(values[k], x=step * k) for k in range(1, ring)]

    relative = jnp.arange(exp_size, dtype=jnp.int32)
    piece_of = (
        (core + relative) % 2 * (2 * ring)
        + (y_at - relative // inner) % ring * 2
        + (z_hi + relative // 2) % 2
    )
    relative = jnp.arange(2 * exp_size, dtype=jnp.int32)
    key_devices = device(
        (z_lo + relative) % 2,
        x_at,
        (y_at - relative // 4) % ring,
        (z_hi + relative // 2) % 2,
        (core + relative // (4 * ring)) % 2,
    )
    steps = jnp.arange(ring, dtype=jnp.int32)
    query_devices = device(z_lo, (x_at - steps) % ring, y_at, z_hi, core)

    def block_numbers(devices):
        every = jnp.arange(block_order.shape[0], dtype=jnp.int32)
        return jnp.sum(
            jnp.where(devices[:, None] == every[None, :], block_order[None, :], 0), axis=1
        )

    k_blocks = block_numbers(key_devices)
    q_blocks = block_numbers(query_devices)
    own_pos = q_blocks[0] * rows + jnp.arange(rows, dtype=jnp.int32)
    hide = jnp.repeat(
        jnp.where(k_blocks[None, :] > q_blocks[:, None], HIDDEN, 0.0), rows, axis=1
    )
    hide = jnp.pad(hide, ((0, size - ring), (0, 0))).astype(jnp.bfloat16)

    depth = model_width // ring
    widened = tokens.astype(jnp.float32)
    row_scale = lax.rsqrt(jnp.mean(widened * widened, axis=1, keepdims=True) + 1e-06)
    gained = (widened * attn_gain.astype(jnp.float32)).astype(jnp.bfloat16)
    w_share = lax.dynamic_slice_in_dim(w_qkv.T, x_at * depth, depth, 1)
    other, gained = lax.optimization_barrier((bring(w_share, z_hi=1), gained))
    near = along_y(jnp.stack([w_share, other]))
    shares = along_x(
        [
            lax.dynamic_slice_in_dim(gained, (x_at + k) % ring * depth, depth, 1)
            for k in range(ring)
        ],
        1,
    )
    near, shares = lax.optimization_barrier((near, shares))
    far = bring(near, core=1)
    w_out_all = lax.all_gather(w_out, "exp", axis=0, tiled=True)
    shares = project(shares, near, far, piece_of)
    shares, routes = lax.optimization_barrier((shares, routes))
    count = router.shape[1]
    pick, pick_last, named = slots(routes.T, count)
    half = size // 2
    freqs = jnp.exp(
        -math.log(rope_base) * jnp.arange(half, dtype=jnp.float32) * 2.0 / size
    )
    angles = own_pos.astype(jnp.float32)[:, None] * freqs[None, :]
    cos, sin = jnp.cos(angles), jnp.sin(angles)
    cos = jnp.concatenate([cos, cos], axis=1)
    sin = jnp.concatenate([-sin, sin], axis=1)
    parts = along_x(shares, -1)
    parts, pick, pick_last, named, hide, cos, sin = lax.optimization_barrier(
        (parts, pick, pick_last, named, hide, cos, sin)
    )
    heads = parts[0].shape[1] // size - 2
    queries, key_values = shape(parts, row_scale, query_gain, key_gain, cos, sin)
    others = [
        bring(key_values, z_lo=1),
        bring(key_values, z_hi=1),
        bring(key_values, z_lo=1, z_hi=1),
    ]
    others, left, right = lax.optimization_barrier(
        (others, bring(queries, x=1), bring(queries, x=ring - 1))
    )
    near = along_y(jnp.stack([key_values, *others])).reshape(-1, 2 * size)
    near, across = lax.optimization_barrier((near, bring(queries, x=2)))
    queries = [queries, left, across, right]
    far = bring(near, core=1)
    totals = attend(queries, near, hide, None, heads, size)
    others = attend(queries[1:], far, hide, totals, heads, size, 1)
    own = attend(queries[:1], far, hide, totals, heads, size)
    parts = along_x([*own, *others], -1)
    main = model_width // 4 * 3
    rest = model_width - main
    resid, moe_in, outgoing = finish(
        parts, w_out_all, tokens, moe_gain, pick, pick_last, heads, size, main
    )

    def exchange(x):
        wide = x.shape[1]
        x = lax.all_to_all(
            x.reshape(count, GROUP, wide), ("ctx", "exp"), split_axis=0, concat_axis=0, tiled=True
        )
        return x.reshape(count * GROUP, wide)

    first = exchange(outgoing)
    second = exchange(dispatch(moe_in, pick, main // rest, rest))
    first, moe_in = lax.optimization_barrier((first, moe_in))
    weights, last_weights = weigh(moe_in, router, named, pick, pick_last)
    partial, ninth = up_first(first, w_gate_up, w_down, main)
    returned = exchange(expert(second, w_gate_up, partial, ninth, w_down, main // rest))
    return combine(returned, weights, last_weights, resid)


def solution(mesh):
    return jax.shard_map(
        on_device,
        mesh=mesh,
        in_specs=(
            P(("ctx", "exp"), None),
            P(),
            P(),
            P(),
            P(),
            P(None, "exp"),
            P("exp", None),
            P(),
            P(),
            P(("ctx", "exp"), None),
            P(("ctx", "exp"), None, None),
            P(("ctx", "exp"), None, None),
        ),
        out_specs=P(("ctx", "exp"), None),
        check_vma=False,
    )
```
